32 devices in a mesh: ctx: 16 (over z, y, x), wshard: 2 (over core).
Axes of the slice: x: 2, y: 2, z: 4, core: 2. Of those that a mesh axis runs over, the one named last changes fastest.
Arguments:
- tokens: bfloat16 [2, 2048, 1536], P('wshard', 'ctx'), may hold values from -6 to 6
- cotangent: bfloat16 [2, 2048, 1536], P('wshard', 'ctx'), may hold values from -6 to 6
- doc_lengths: int32 [2, 4], P('wshard'), may hold values from 1 to 1024, 2048 in all within a row
- norm_attn: bfloat16 [1536], P(('ctx', 'wshard')), may hold values from 0.5 to 1.5
- w_qkv: bfloat16 [1536, 2048], P(('ctx', 'wshard')), may hold values from -0.15625 to 0.15625
- b_qkv: bfloat16 [2048], P(('ctx', 'wshard')), may hold values from -1.1953125 to 1.1953125
- w_out: bfloat16 [1536, 1536], P(None, ('ctx', 'wshard')), may hold values from -0.625 to 0.625
- norm_mlp: bfloat16 [1536], P(('ctx', 'wshard')), may hold values from 0.5 to 1.5
- w_gate: bfloat16 [1536, 8960], P(('ctx', 'wshard')), may hold values from -0.15625 to 0.15625
- w_up: bfloat16 [1536, 8960], P(('ctx', 'wshard')), may hold values from -0.15625 to 0.15625
- w_down: bfloat16 [8960, 1536], P(('ctx', 'wshard')), may hold values from -0.0625 to 0.0625
Outputs:
- output: bfloat16 [2, 2048, 1536], P('wshard', 'ctx')
- grad_tokens: float32 [2, 2048, 1536], P('wshard', 'ctx')
- grad_norm_attn: float32 [1536], P(('ctx', 'wshard'))
- grad_w_qkv: float32 [1536, 2048], P(('ctx', 'wshard'))
- grad_b_qk: float32 [1792], P(('ctx', 'wshard'))
- grad_b_v: float32 [256], P(('ctx', 'wshard'))
- grad_w_out: float32 [1536, 1536], P(None, ('ctx', 'wshard'))
- grad_norm_mlp: float32 [1536], P(('ctx', 'wshard'))
- grad_w_gate: float32 [1536, 8960], P(('ctx', 'wshard'))
- grad_w_up: float32 [1536, 8960], P(('ctx', 'wshard'))
- grad_w_down: float32 [8960, 1536], P(('ctx', 'wshard'))
The draws below stay inside these ranges and needn't reach their ends.
Inputs may be any that keep to these rules, and one draw needn't show every extreme that they name: Each row of doc_lengths lists the lengths of its stream's 4 documents in stream order; a row sums to 2048 and its largest entry is 1024.
All inputs are finite; a program needn't handle non-finite values.
Results may differ from the reference program's by a relative error of at most 0.022.
Values may be sent and summed in bfloat16 or wider, within the bound.
No kernel may reach another device: no remote copies, remote signals or barrier semaphores. Data moves between devices by JAX's collectives and lax.ppermute only.
A program may use at most 640 MiB of HBM per device.

```python
import math
import jax
import jax.numpy as jnp
import numpy as np
from jax import lax

D = 1536
H = 12
KVH = 2
HD = 128
FF = 8960
TOK_DEV = 128
KEY_BLOCK = 512
STREAMS = 2
STREAM = 2048
LONGEST = 1024
NDOCS = 4
QKV = 2048
N_CTX = 16


def block_scale(stream_key, shape, pieces, low, high):
    loudness, own = 1.0, jax.random.fold_in(stream_key, 6)
    for axis_at, shards_of in pieces:
        draws = jnp.exp(jax.random.uniform(jax.random.fold_in(own, axis_at), (shards_of,), jnp.float32, low / len(pieces), high / len(pieces)))
        loudness = loudness * jnp.repeat(draws, shape[axis_at] // shards_of).reshape([-1 if axis == axis_at else 1 for axis in range(len(shape))])
    return loudness


def profile(number_of, total, limit, lean):
    weights = [(1 << 20) // math.isqrt(rank ** lean) + 1 for rank in range(2, number_of + 1)]
    surplus, counts = total - limit - (number_of - 1), [1] * (number_of - 1)
    while surplus > 0:
        free = [i for i in range(number_of - 1) if counts[i] < limit]
        mass, remaining = sum([weights[i] for i in free]), surplus
        for i in free:
            addition = min(limit - counts[i], max(1, remaining * weights[i] // mass), surplus)
            counts[i] = counts[i] + addition
            surplus = surplus - addition
    return np.array([limit] + counts)


def uneven(rng, count, total, most, lean):
    if count == 2:
        one = jax.random.randint(rng, (), max(1, total - most), min(most, total - 1) + 1)
        return jnp.stack([one, total - one])
    sizes = jnp.asarray(profile(count, total, most, lean), jnp.int32)
    twos = (count - 1) // 2
    giver, taker = sizes[1:1 + 2 * twos:2], sizes[2:2 + 2 * twos:2]
    slack = jnp.minimum(giver - 1, most - taker)
    moved = jax.random.randint(jax.random.fold_in(rng, 1), (twos,), 0, 1 << 20) % (slack + 1)
    sizes = sizes.at[1:1 + 2 * twos:2].set(giver - moved).at[2:2 + 2 * twos:2].set(taker + moved)
    return sizes[jax.random.permutation(jax.random.fold_in(rng, 2), count)]


def bell_draw(rng, shape, deviation, limit, cuts=(), kind=jnp.bfloat16):
    values = jax.random.normal(rng, shape, jnp.float32) * deviation
    if len(cuts) > 0:
        values = block_scale(rng, shape, cuts, -0.22, 0.18) * values
    return jnp.clip(values, min=-limit, max=limit).astype(kind)


def setup_inputs(seed: int = 0) -> dict:
    key_list = jax.random.split(jax.random.key(seed), 12)
    return {
        "tokens": bell_draw(key_list[0], (STREAMS, STREAM, D), 1.0, 6.0, ((0, 2), (1, 16))),
        "cotangent": bell_draw(key_list[1], (STREAMS, STREAM, D), 1.0, 6.0, ((0, 2), (1, 16))),
        "doc_lengths": jax.vmap(lambda own: uneven(own, NDOCS, STREAM, LONGEST, 1))(jax.random.split(key_list[2], STREAMS)).reshape((STREAMS, NDOCS)).astype(jnp.int32),
        "norm_attn": jnp.clip(1.0 + 0.1 * jax.random.normal(key_list[3], (D,), jnp.float32), 0.5, 1.5).astype(jnp.bfloat16),
        "w_qkv": bell_draw(key_list[4], (D, QKV), D ** -0.5, 0.15625, ((0, 32),)),
        "b_qkv": bell_draw(key_list[5], (QKV,), 0.2, 1.1953125, ((0, 32),)),
        "w_out": bell_draw(key_list[6], (H * HD, D), (H * HD // 16) ** -0.5, 0.625, ((1, 32),)),
        "norm_mlp": jnp.clip(1.0 + 0.1 * jax.random.normal(key_list[7], (D,), jnp.float32), 0.5, 1.5).astype(jnp.bfloat16),
        "w_gate": bell_draw(key_list[8], (D, FF), D ** -0.5, 0.15625, ((0, 32),)),
        "w_up": bell_draw(key_list[9], (D, FF), D ** -0.5, 0.15625, ((0, 32),)),
        "w_down": bell_draw(key_list[10], (FF, D), FF ** -0.5, 0.0625, ((0, 32),)),
    }


@jax.custom_vjp
def low(v):
    return lax.optimization_barrier(v.astype(jnp.bfloat16)).astype(jnp.float32)

@jax.custom_vjp
def low_back(v):
    return v

def low_keep(v):
    return (low(v), None)

def low_pass(kept, grad):
    return (grad,)

def back_keep(v):
    return (v, None)

def back_low(kept, grad):
    return (low(grad),)
low.defvjp(low_keep, low_pass)
low_back.defvjp(back_keep, back_low)
EPSILON = 1e-06
ROPE_BASE = 1000000.0

def matmul(left_side, right_side):
    return jnp.dot(left_side, right_side, precision=lax.Precision.HIGHEST)

def stream_places():
    row_ids = jnp.arange(STREAM, dtype=jnp.int32)
    half_rows = TOK_DEV // 2
    device = row_ids // TOK_DEV
    inner_row = row_ids % TOK_DEV
    blocks = jnp.where(inner_row < half_rows, device, 2 * N_CTX - 1 - device)
    return (blocks * half_rows + inner_row % half_rows).astype(jnp.int32)

def documents_positions(lengths, places):
    ends_at = jnp.cumsum(lengths).astype(jnp.int32)
    passed = ends_at[None, :] <= places[:, None]
    documents = lax.optimization_barrier(jnp.sum(passed.astype(jnp.int32), axis=1)).astype(jnp.int32)
    starts = lax.optimization_barrier(jnp.sum(jnp.where(passed, lengths[None, :], 0), axis=1)).astype(jnp.int32)
    return (documents, (places - starts).astype(jnp.int32))

def rope_tables(positions):
    half_width = HD // 2
    frequency = ROPE_BASE ** (-jnp.arange(half_width, dtype=jnp.float32) * 2.0 / HD)
    angles = positions.astype(jnp.float32)[:, None] * frequency[None, :]
    cos_table = jnp.concatenate([jnp.cos(angles), jnp.cos(angles)], axis=-1)[:, None, :]
    sin_table = jnp.concatenate([jnp.sin(angles), jnp.sin(angles)], axis=-1)[:, None, :]
    return (cos_table, sin_table)

def rotate(values, cos_table, sin_table):
    half_width = values.shape[-1] // 2
    turned = jnp.concatenate([-values[..., half_width:], values[..., :half_width]], axis=-1)
    return values * cos_table + turned * sin_table

def stream_forward(inputs, lengths, weights):
    gain_attn, full_qkv, full_bias, full_out, gain_mlp, full_gate, full_up, full_down = weights
    documents, positions = documents_positions(lengths, stream_places())
    cos_table, sin_table = rope_tables(positions)
    q_width = H * HD
    kv_width = KVH * HD
    groups = H // KVH
    block_count = STREAM // KEY_BLOCK
    score_scale = 1.0 / math.sqrt(HD)
    scale_one = lax.rsqrt(lax.optimization_barrier(jnp.mean(inputs * inputs, axis=-1, keepdims=True)) + EPSILON)
    normed_one = low(inputs * scale_one * gain_attn)
    project = low_back(matmul(normed_one, full_qkv) + full_bias)
    queries = low(rotate(project[:, :q_width].reshape(STREAM, H, HD), cos_table, sin_table))
    queries = queries.reshape(STREAM, KVH, groups, HD)
    keys_all = low(rotate(project[:, q_width:q_width + kv_width].reshape(STREAM, KVH, HD), cos_table, sin_table))
    values_all = low(project[:, q_width + kv_width:].reshape(STREAM, KVH, HD))

    def attend_block(block_in):
        query_block, doc_block, pos_block = block_in
        scores = low_back(jnp.einsum('tkgd,skd->tkgs', query_block, keys_all, precision=lax.Precision.HIGHEST) * score_scale)
        allowed = (doc_block[:, None] == documents[None, :]) & (positions[None, :] <= pos_block[:, None])
        masked = jnp.where(allowed[:, None, None, :], scores, -1e+30)
        shifted = jnp.exp(masked - lax.optimization_barrier(jnp.max(masked, axis=-1, keepdims=True)))
        probability = shifted / lax.optimization_barrier(jnp.sum(shifted, axis=-1, keepdims=True))
        return jnp.einsum('tkgs,skd->tkgd', low(probability), values_all, precision=lax.Precision.HIGHEST)
    attended = lax.map(jax.checkpoint(attend_block), (queries.reshape(block_count, KEY_BLOCK, KVH, groups, HD), documents.reshape(block_count, KEY_BLOCK), positions.reshape(block_count, KEY_BLOCK)))
    attended = low(low_back(attended.reshape(STREAM, q_width)))
    hidden_res = inputs + low_back(matmul(attended, full_out))
    scale_two = lax.rsqrt(lax.optimization_barrier(jnp.mean(hidden_res * hidden_res, axis=-1, keepdims=True)) + EPSILON)
    normed_two = low(hidden_res * scale_two * gain_mlp)
    gate_pre = low_back(matmul(normed_two, full_gate))
    up_pre = low_back(matmul(normed_two, full_up))
    activated = low(jax.nn.silu(gate_pre) * up_pre)
    return hidden_res + low_back(matmul(activated, full_down))

def reference(tokens, cotangent, doc_lengths, norm_attn, w_qkv, b_qkv, w_out, norm_mlp, w_gate, w_up, w_down):
    weights = tuple((argument.astype(jnp.float32) for argument in (norm_attn, w_qkv, b_qkv, w_out, norm_mlp, w_gate, w_up, w_down)))
    inputs = tokens.astype(jnp.float32)

    def whole_layer(inputs_all, weights_all):

        def one_stream(stream_in):
            return stream_forward(stream_in[0], stream_in[1], weights_all)
        return lax.map(jax.checkpoint(one_stream), (inputs_all, doc_lengths))
    output, pullback = jax.vjp(whole_layer, inputs, weights)
    input_grad, weight_grads = pullback(cotangent.astype(jnp.float32))
    qk_width = (H + KVH) * HD
    bias_grad = weight_grads[2]
    return (output.astype(jnp.bfloat16), input_grad, weight_grads[0], weight_grads[1], bias_grad[:qk_width], bias_grad[qk_width:], weight_grads[3], weight_grads[4], weight_grads[5], weight_grads[6], weight_grads[7])
```

```python
import math

import jax
import jax.numpy as jnp
from jax import lax
from jax.sharding import PartitionSpec as P

H = 12
KVH = 2
HD = 128
EPSILON = 1e-06
ROPE_BASE = 1000000.0
CUBE = (0, 1, 2)
ORDERS = ((0, 1, 2), (1, 2, 0), (2, 0, 1))
bf16 = jnp.bfloat16
f32 = jnp.float32


def core_swap(x):
    return lax.ppermute(x, "wshard", [(0, 1), (1, 0)])


def chip_swap(x, flip):
    count = lax.axis_size("ctx")
    return lax.ppermute(x, "ctx", [(i, i ^ flip) for i in range(count)])


def high_bits():
    return tuple(range(3, lax.axis_size("ctx").bit_length() - 1))


def my_bit(bit):
    return (lax.axis_index("ctx") >> bit) & 1


def gather_relative(x, bits):
    for bit in bits:
        x = jnp.concatenate([x, chip_swap(x, 1 << bit)], axis=0)
    return x


def relative_flips(bits):
    flips = [0]
    for bit in bits:
        flips = flips + [f ^ (1 << bit) for f in flips]
    return flips


def scatter_relative(x, bits):
    total = x
    for at, bit in enumerate(reversed(bits)):
        half = total.shape[0] // 2
        keep, send = total[:half], total[half:]
        total = keep.astype(f32) + chip_swap(send.astype(bf16), 1 << bit).astype(f32)
        if at < len(bits) - 1:
            total = total.astype(bf16)
    return total


def gather_ordered(x, bits):
    names = []
    for bit in bits:
        other = chip_swap(x, 1 << bit)
        upper = my_bit(bit) == 1
        x = jnp.stack([jnp.where(upper, other, x), jnp.where(upper, x, other)])
        names = [bit] + names
    want = sorted(names, reverse=True)
    rest = tuple(range(len(names), x.ndim))
    x = x.transpose(tuple(names.index(b) for b in want) + rest)
    return x.reshape((2 ** len(names),) + x.shape[len(names) :])


def scatter_ordered(x, bits):
    count = len(bits)
    names = sorted(bits, reverse=True)
    x = x.reshape((2,) * count + x.shape[1:])
    for at, bit in enumerate(bits):
        axis = names.index(bit)
        mine = my_bit(bit)
        keep = lax.dynamic_index_in_dim(x, mine, axis, keepdims=False)
        send = lax.dynamic_index_in_dim(x, 1 - mine, axis, keepdims=False)
        x = keep.astype(f32) + chip_swap(send.astype(bf16), 1 << bit).astype(f32)
        if at < count - 1:
            x = x.astype(bf16)
        names.pop(axis)
    return x


def row_parts(rows):
    third = rows * 3 // 8
    return ((0, third), (third, 2 * third), (2 * third, rows))


def documents_positions(lengths, places):
    ends_at = jnp.cumsum(lengths)
    passed = ends_at[None, :] <= places[:, None]
    documents = jnp.sum(passed.astype(jnp.int32), axis=1)
    starts = jnp.sum(jnp.where(passed, lengths[None, :], 0), axis=1)
    return (documents, places - starts)


def places_of(device, inner_row, tok_dev):
    ctx_size = lax.axis_size("ctx")
    half_rows = tok_dev // 2
    blocks = jnp.where(inner_row < half_rows, device, 2 * ctx_size - 1 - device)
    return blocks * half_rows + inner_row % half_rows


def rope_tables(positions):
    half_width = HD // 2
    frequency = ROPE_BASE ** (-jnp.arange(half_width, dtype=f32) * 2.0 / HD)
    angles = positions.astype(f32)[:, None] * frequency[None, :]
    cos_table = jnp.concatenate([jnp.cos(angles), jnp.cos(angles)], axis=-1)[:, None, :]
    sin_table = jnp.concatenate([jnp.sin(angles), jnp.sin(angles)], axis=-1)[:, None, :]
    return (cos_table, sin_table)


def rotate(values, cos_table, sin_table):
    half_width = values.shape[-1] // 2
    turned = jnp.concatenate([-values[..., half_width:], values[..., :half_width]], axis=-1)
    return values * cos_table + turned * sin_table


def unrotate(gradient, cos_table, sin_table):
    half_width = gradient.shape[-1] // 2
    scaled = gradient * sin_table
    turned = jnp.concatenate([scaled[..., half_width:], -scaled[..., :half_width]], axis=-1)
    return gradient * cos_table + turned


def dot(left, right, left_axis, right_axis):
    return lax.dot_general(
        left, right, (((left_axis,), (right_axis,)), ((), ())), preferred_element_type=f32
    )


def rms_back(grad_in, values, scale_rows, gain_row):
    weighted = grad_in * gain_row
    return scale_rows * weighted - values * scale_rows**3 * jnp.mean(
        weighted * values, axis=-1, keepdims=True
    )


def half_of(x, which, axis):
    size = x.shape[axis] // 2
    return lax.dynamic_slice_in_dim(x, which * size, size, axis)


def head_columns(x, core):
    q_width, kv_width = H * HD, KVH * HD
    return jnp.concatenate(
        [
            half_of(x[:, :q_width], core, 1),
            half_of(x[:, q_width : q_width + kv_width], core, 1),
            half_of(x[:, q_width + kv_width :], core, 1),
        ],
        axis=1,
    )


def by_core(mine, other, core):
    return jnp.stack([jnp.where(core == 0, mine, other), jnp.where(core == 0, other, mine)])


def gather_rows(x, bits):
    high = tuple(b for b in bits if b > 2)
    rows = x.shape[0]
    parts = []
    cuts = (0, rows // 48 * 16, rows // 48 * 32, rows) if rows >= 48 else (0, rows)
    for (start, stop), order in zip(zip(cuts[:-1], cuts[1:]), ORDERS):
        parts.append(gather_ordered(x[start:stop], high + order))
    whole = jnp.concatenate(parts, axis=1)
    return whole.reshape((-1,) + x.shape[1:])


def scatter_rows(x, bits):
    high = tuple(b for b in bits if b > 2)
    chips = 2 ** len(bits)
    rows = x.shape[0] // chips
    x = x.reshape(chips, rows, x.shape[1])
    cuts = (0, rows // 48 * 16, rows // 48 * 32, rows) if rows >= 48 else (0, rows)
    parts = [
        scatter_ordered(x[:, start:stop], order + high)
        for (start, stop), order in zip(zip(cuts[:-1], cuts[1:]), ORDERS)
    ]
    return jnp.concatenate(parts, axis=0)


def on_device(
    tokens, cotangent, doc_lengths, norm_attn, w_qkv, b_qkv, w_out, norm_mlp, w_gate, w_up, w_down
):
    ctx_size = lax.axis_size("ctx")
    chip = lax.axis_index("ctx")
    core = lax.axis_index("wshard")
    high = high_bits()
    bits = tuple(range(3)) + high
    groups = ctx_size // 8
    member, group = chip % 8, chip // 8
    tok_dev, width = tokens.shape[1], tokens.shape[2]
    ff = w_gate.shape[1]
    ff_chip = ff // ctx_size
    ff_own = ff // 8
    heads = H // KVH
    hq = heads * HD
    score_scale = 1.0 / math.sqrt(HD)

    mine = head_columns(w_qkv, core)
    other = core_swap(head_columns(w_qkv, 1 - core))
    qkv_w = gather_rows(by_core(mine, other, core).reshape(-1, mine.shape[1]), bits)
    small = jnp.concatenate([norm_attn, b_qkv, norm_mlp])
    small_all = gather_ordered(by_core(small, core_swap(small), core), bits).reshape(
        2 * ctx_size, -1
    )
    n_gain, n_bias = norm_attn.shape[0], b_qkv.shape[0]
    gain_one = small_all[:, :n_gain].reshape(-1).astype(f32)
    bias = small_all[:, n_gain : n_gain + n_bias].reshape(1, -1).astype(f32)
    gain_two = small_all[:, n_gain + n_bias :].reshape(-1).astype(f32)
    bias = head_columns(bias, core)
    out_t = w_out.T
    out_mine = half_of(out_t, core, 1)
    out_other = core_swap(half_of(out_t, 1 - core, 1))
    out_w = gather_rows(by_core(out_mine, out_other, core).reshape(-1, hq), bits)

    rows_dev = w_gate.shape[0]

    def by_member(w):
        return w.reshape(rows_dev, groups, 8, ff_chip).transpose(2, 0, 1, 3).reshape(8, rows_dev, ff_own)

    both = jnp.concatenate([by_member(w_gate), by_member(w_up)], axis=2)
    arrived = [lax.dynamic_index_in_dim(both, member, 0, keepdims=False)]
    for k in range(1, 8):
        send = lax.dynamic_index_in_dim(both, member ^ k, 0, keepdims=False)
        arrived.append(chip_swap(send, k))
    arrived = jnp.stack(arrived)
    cube_rows = jnp.stack(
        [lax.dynamic_index_in_dim(arrived, member ^ k, 0, keepdims=False) for k in range(8)]
    )
    all_rows = gather_ordered(cube_rows, high)
    all_rows = by_core(all_rows, core_swap(all_rows), core)
    gate_up = all_rows.transpose(1, 2, 0, 3, 4).reshape(width, 2 * ff_own)
    down = by_core(w_down, core_swap(w_down), core).reshape(ff_chip, width)
    down = gather_ordered(down, high).reshape(ff_own, width)

    def streams(x):
        return jnp.stack([x, core_swap(x)])

    token_pair = streams(tokens[0])
    length_pair = streams(doc_lengths[0])
    inner = jnp.arange(tok_dev, dtype=jnp.int32)
    parts = row_parts(tok_dev)
    key_places = jnp.concatenate(
        [
            places_of(
                (chip ^ jnp.array(relative_flips(high + order), jnp.int32))[:, None],
                inner[None, start:stop],
                tok_dev,
            ).reshape(-1)
            for (start, stop), order in zip(parts, ORDERS)
        ]
    )
    own_places = places_of(chip, inner, tok_dev)
    own_docs, own_pos = jax.vmap(lambda l: documents_positions(l, own_places))(length_pair)
    key_docs, key_pos = jax.vmap(lambda l: documents_positions(l, key_places))(length_pair)
    cos_table, sin_table = rope_tables(own_pos.reshape(-1))

    inputs_pair = token_pair.reshape(2 * tok_dev, width).astype(f32)
    scale_one = lax.rsqrt(jnp.mean(inputs_pair * inputs_pair, axis=-1, keepdims=True) + EPSILON)
    normed_one = (inputs_pair * scale_one * gain_one).astype(bf16)
    project = dot(normed_one, qkv_w, 1, 0) + bias
    queries = rotate(project[:, :hq].reshape(-1, heads, HD), cos_table, sin_table).astype(bf16)
    keys_own = rotate(project[:, hq : hq + HD].reshape(-1, 1, HD), cos_table, sin_table)
    keys_own = keys_own.reshape(2, tok_dev, HD).astype(bf16)
    values_own = project[:, hq + HD :].reshape(2, tok_dev, HD).astype(bf16)
    kv_own = jnp.concatenate([keys_own, values_own], axis=2)
    kv_parts = [
        gather_relative(kv_own[None, :, start:stop], high + order)
        .transpose(1, 0, 2, 3)
        .reshape(2, -1, 2 * HD)
        for (start, stop), order in zip(parts, ORDERS)
    ]
    kv_all = jnp.concatenate(kv_parts, axis=1)
    keys, values = kv_all[..., :HD], kv_all[..., HD:]

    queries = queries.reshape(2, tok_dev, heads, HD)
    allowed = (own_docs[:, :, None] == key_docs[:, None, :]) & (
        key_pos[:, None, :] <= own_pos[:, :, None]
    )
    allowed = allowed[:, None]
    scores = (
        jnp.einsum("sthd,skd->shtk", queries, keys, preferred_element_type=f32) * score_scale
    )
    masked = jnp.where(allowed, scores, -1e30)
    top = jnp.max(masked, axis=-1, keepdims=True)
    shifted = jnp.exp(masked - top)
    probability = shifted / jnp.sum(shifted, axis=-1, keepdims=True)
    probability_b = probability.astype(bf16)
    attended = jnp.einsum("shtk,skd->sthd", probability_b, values, preferred_element_type=f32)
    attended_b = attended.reshape(2 * tok_dev, hq).astype(bf16)
    branch = dot(attended_b, out_w, 1, 1)
    inputs = inputs_pair[:tok_dev]
    hidden_res = inputs + branch[:tok_dev] + core_swap(branch[tok_dev:])
    scale_two = lax.rsqrt(jnp.mean(hidden_res * hidden_res, axis=-1, keepdims=True) + EPSILON)
    normed_two = (hidden_res * scale_two * gain_two).astype(bf16)

    def cube_gather(x):
        return jnp.concatenate(
            [
                gather_relative(x[start:stop], order)
                for (start, stop), order in zip(parts, ORDERS)
            ]
        )

    def cube_scatter(x):
        sums = []
        for (start, stop), order in zip(parts, ORDERS):
            sums.append(scatter_relative(x[8 * start : 8 * stop], order))
        return jnp.concatenate(sums)

    out_grad_b = cotangent[0]
    out_grad = out_grad_b.astype(f32)
    out_grad_all = cube_gather(out_grad_b)
    act_grad = dot(out_grad_all, down, 1, 1)
    normed_all = cube_gather(normed_two)
    pre = dot(normed_all, gate_up, 1, 0)
    gate_pre, up_pre = pre[:, :ff_own], pre[:, ff_own:]
    gate_sig = jax.nn.sigmoid(gate_pre)
    gate_act = gate_pre * gate_sig
    activated = (gate_act * up_pre).astype(bf16)
    gate_grad = (act_grad * up_pre * gate_sig * (1.0 + gate_pre * (1.0 - gate_sig))).astype(bf16)
    up_grad = (act_grad * gate_act).astype(bf16)
    pre_grad = jnp.concatenate([gate_grad, up_grad], axis=1)
    normed_two_grad = cube_scatter(dot(pre_grad, gate_up, 1, 1).astype(bf16))
    branch_mlp = cube_scatter(dot(activated, down, 1, 0).astype(bf16))
    output = (hidden_res + branch_mlp).astype(bf16)

    down_part = dot(activated, out_grad_all, 0, 0).astype(bf16).reshape(groups, 2, -1, width)
    keep = lax.dynamic_index_in_dim(down_part, core, 1, keepdims=False)
    send = lax.dynamic_index_in_dim(down_part, 1 - core, 1, keepdims=False)
    down_sum = (keep.astype(f32) + core_swap(send).astype(f32)).astype(bf16)
    grad_down = scatter_ordered(down_sum, tuple(reversed(high)))

    gu_part = dot(normed_all, pre_grad, 0, 0).astype(bf16)
    gu_part = gu_part.reshape(groups, 8, 2, rows_dev, 2 * ff_own)
    keep = lax.dynamic_index_in_dim(gu_part, core, 2, keepdims=False)
    send = lax.dynamic_index_in_dim(gu_part, 1 - core, 2, keepdims=False)
    gu_sum = (keep.astype(f32) + core_swap(send).astype(f32)).astype(bf16)
    gu_sum = scatter_ordered(gu_sum, tuple(reversed(high))).astype(bf16)
    arrived = [lax.dynamic_index_in_dim(gu_sum, member, 0, keepdims=False)]
    for k in range(1, 8):
        send = lax.dynamic_index_in_dim(gu_sum, member ^ k, 0, keepdims=False)
        arrived.append(chip_swap(send, k))
    arrived = jnp.stack(arrived)
    from_members = jnp.stack(
        [lax.dynamic_index_in_dim(arrived, member ^ k, 0, keepdims=False) for k in range(8)]
    )

    def to_columns(x):
        x = x.reshape(8, rows_dev, groups, ff_chip).transpose(1, 2, 0, 3)
        return x.reshape(rows_dev, ff).astype(f32)

    grad_gate = to_columns(from_members[:, :, :ff_own])
    grad_up = to_columns(from_members[:, :, ff_own:])

    gain_two_grad = jnp.sum(normed_two_grad * hidden_res * scale_two, axis=0)
    hidden_grad = out_grad + rms_back(normed_two_grad, hidden_res, scale_two, gain_two)

    branch_grad = streams(hidden_grad.astype(bf16)).reshape(2 * tok_dev, width)
    attended_grad = dot(branch_grad, out_w, 1, 0).astype(bf16)
    grad_out_t = scatter_rows(dot(branch_grad, attended_b, 0, 0).astype(bf16), bits)
    grad_heads = attended_grad.reshape(2, tok_dev, heads, HD)
    delta = jnp.sum(grad_heads.astype(f32) * attended, axis=-1).transpose(0, 2, 1)[..., None]
    prob_grad = jnp.einsum("sthd,skd->shtk", grad_heads, values, preferred_element_type=f32)
    score_grad = (probability * (prob_grad - delta)).astype(bf16)
    query_grad = (
        jnp.einsum("shtk,skd->sthd", score_grad, keys, preferred_element_type=f32) * score_scale
    )
    key_grad = (
        jnp.einsum("shtk,sthd->skd", score_grad, queries, preferred_element_type=f32) * score_scale
    )
    value_grad = jnp.einsum("shtk,sthd->skd", probability_b, grad_heads, preferred_element_type=f32)
    kv_grad = jnp.concatenate([key_grad, value_grad], axis=2).astype(bf16)
    kv_sums = []
    for (start, stop), order in zip(parts, ORDERS):
        own = kv_grad[:, ctx_size * start : ctx_size * stop]
        own = own.reshape(2, ctx_size, stop - start, 2 * HD).transpose(1, 0, 2, 3)
        kv_sums.append(scatter_relative(own, high + order)[0])
    kv_sum = jnp.concatenate(kv_sums, axis=1).reshape(2 * tok_dev, 2 * HD)
    query_pre = unrotate(query_grad.reshape(-1, heads, HD), cos_table, sin_table)
    key_pre = unrotate(kv_sum[:, None, :HD], cos_table, sin_table)
    project_grad_q = query_pre.reshape(-1, hq).astype(bf16)
    project_grad_kv = jnp.concatenate([key_pre[:, 0], kv_sum[:, HD:]], axis=1).astype(bf16)
    grad_q = scatter_rows(dot(normed_one, project_grad_q, 0, 0).astype(bf16), bits)
    grad_kv = scatter_rows(dot(normed_one, project_grad_kv, 0, 0).astype(bf16), bits)
    project_grad = jnp.concatenate([project_grad_q, project_grad_kv], axis=1)
    normed_one_grad = dot(project_grad, qkv_w, 1, 1)
    normed_one_grad = normed_one_grad[:tok_dev] + core_swap(normed_one_grad[tok_dev:])
    gain_one_grad = jnp.sum(normed_one_grad * inputs * scale_one[:tok_dev], axis=0)
    input_grad = hidden_grad + rms_back(normed_one_grad, inputs, scale_one[:tok_dev], gain_one)

    mine = half_of(jnp.concatenate([grad_q, grad_kv], axis=1), core, 0)
    other = half_of(jnp.concatenate([grad_q, grad_kv], axis=1), 1 - core, 0)
    pair = by_core(mine, core_swap(other), core)

    def whole_columns(x):
        return jnp.concatenate(
            [
                x[0, :, :hq],
                x[1, :, :hq],
                x[0, :, hq : hq + HD],
                x[1, :, hq : hq + HD],
                x[0, :, hq + HD :],
                x[1, :, hq + HD :],
            ],
            axis=1,
        )

    grad_qkv = whole_columns(pair)
    out_mine = half_of(grad_out_t, core, 0)
    out_other = half_of(grad_out_t, 1 - core, 0)
    out_pair = by_core(out_mine, core_swap(out_other), core)
    grad_out = out_pair.transpose(1, 0, 2).reshape(-1, 2 * hq).T

    bias_grad = jnp.sum(project_grad.astype(f32), axis=0, keepdims=True)
    zeros = jnp.zeros_like(bias_grad)
    bias_full = jnp.stack(
        [jnp.where(core == 0, bias_grad, zeros), jnp.where(core == 0, zeros, bias_grad)]
    )
    sums = jnp.concatenate([gain_one_grad, gain_two_grad, whole_columns(bias_full)[0]])
    sums = sums.reshape(-1, 128)
    sums = sums + core_swap(sums)
    for bit in bits:
        sums = sums + chip_swap(sums, 1 << bit)
    sums = sums.reshape(-1)
    at = 2 * chip + core

    def owned(x):
        size = x.shape[0] // (2 * ctx_size)
        return lax.dynamic_slice_in_dim(x, at * size, size, 0)

    qk_width = (H + KVH) * HD
    bias_sum = sums[2 * width :]
    return (
        output[None],
        input_grad[None],
        owned(sums[:width]),
        grad_qkv,
        owned(bias_sum[:qk_width]),
        owned(bias_sum[qk_width:]),
        grad_out,
        owned(sums[width : 2 * width]),
        grad_gate,
        grad_up,
        grad_down,
    )


def solution(mesh):
    whole = ("ctx", "wshard")
    rows, columns, flat = P(whole, None), P(None, whole), P(whole)
    tokens = P("wshard", "ctx", None)
    return jax.shard_map(
        on_device,
        mesh=mesh,
        in_specs=(tokens, tokens, P("wshard", None), flat, rows, flat, columns, flat, rows, rows, rows),
        out_specs=(tokens, tokens, flat, rows, flat, flat, columns, flat, rows, rows, rows),
        check_vma=False,
    )
```

```python
import functools
import math

import jax
import jax.numpy as jnp
from jax import lax
from jax.experimental import pallas as pl
from jax.experimental.pallas import tpu as pltpu
from jax.sharding import PartitionSpec as P

H = 12
KVH = 2
HD = 128
EPSILON = 1e-06
ROPE_BASE = 1000000.0
ORDERS = ((0, 1, 2), (1, 2, 0), (2, 0, 1))
CHUNK = 256
NEVER = -1e30
SCALE = 1.0 / math.sqrt(HD)
bf16 = jnp.bfloat16
f32 = jnp.float32
VMEM = pl.BlockSpec(memory_space=pltpu.VMEM)
SMEM = pl.BlockSpec(memory_space=pltpu.SMEM)
BIG = pltpu.CompilerParams(vmem_limit_bytes=56 * 1024 * 1024)


def after(x, *others):
    return lax.optimization_barrier((x,) + others)[0]


def together(*groups):
    flat, tree = jax.tree.flatten(groups)
    return jax.tree.unflatten(tree, lax.optimization_barrier(flat))


def core_swap(x):
    return lax.ppermute(x, "wshard", [(0, 1), (1, 0)])


def chip_swap(x, flip):
    count = lax.axis_size("ctx")
    return lax.ppermute(x, "ctx", [(i, i ^ flip) for i in range(count)])


def cubes():
    count = lax.axis_size("ctx")
    return [list(range(i, i + 8)) for i in range(0, count, 8)]


def cube_exchange(x):
    return lax.all_to_all(
        x, "ctx", split_axis=0, concat_axis=0, tiled=True, axis_index_groups=cubes()
    )


def group_bits():
    return tuple(range(lax.axis_size("ctx").bit_length() - 4))


def member_bits():
    first = len(group_bits())
    return (first, first + 1, first + 2)


def group_lists():
    groups = lax.axis_size("ctx") // 8
    return [[g + groups * m for m in range(8)] for g in range(groups)]


def group_exchange(x):
    return lax.all_to_all(
        x, "ctx", split_axis=0, concat_axis=0, tiled=True, axis_index_groups=group_lists()
    )


def high_bits():
    return tuple(range(3, lax.axis_size("ctx").bit_length() - 1))


def my_bit(bit):
    return (lax.axis_index("ctx") >> bit) & 1


def gather_relative(x, bits):
    for bit in bits:
        x = jnp.concatenate([x, chip_swap(x, 1 << bit)], axis=0)
    return x


def gather_list(x, bits):
    found = [x]
    for bit in bits:
        found = found + [chip_swap(y, 1 << bit) for y in found]
    return found


def relative_flips(bits):
    flips = [0]
    for bit in bits:
        flips = flips + [f ^ (1 << bit) for f in flips]
    return flips


def sum_over(x, axis, bits):
    for at, bit in enumerate(bits):
        shape = x.shape
        x = x.reshape(shape[:axis] + (2, shape[axis] // 2) + shape[axis + 1 :])
        keep = lax.dynamic_index_in_dim(x, my_bit(bit), axis, keepdims=False)
        send = lax.dynamic_index_in_dim(x, 1 - my_bit(bit), axis, keepdims=False)
        x = keep.astype(f32) + chip_swap(send.astype(bf16), 1 << bit).astype(f32)
        if at < len(bits) - 1:
            x = x.astype(bf16)
    return jnp.squeeze(x, axis).astype(f32)


def sum_over_high(x, high):
    return sum_over(x, 0, tuple(reversed(high)))


def row_parts(rows):
    third = rows * 3 // 8
    return ((0, third), (third, 2 * third), (2 * third, rows))


def doubled(parts, bits):
    return [jnp.concatenate([x, chip_swap(x, 1 << bit)]) for x, bit in zip(parts, bits)]


def with_arrived(parts, bits):
    found = []
    for x, bit in zip(parts, bits):
        found.extend([x, chip_swap(x, 1 << bit)])
    return found


def both_halves(x, layout, bit):
    axis = layout.index(bit)
    keep = lax.dynamic_index_in_dim(x, my_bit(bit), axis, keepdims=False)
    send = lax.dynamic_index_in_dim(x, 1 - my_bit(bit), axis, keepdims=False)
    return keep, send


class Scatter:
    def __init__(self, parts, layout):
        self.parts = list(parts)
        self.layouts = [list(layout) for _ in self.parts]

    def split(self, bits):
        pairs = [both_halves(x, l, b) for x, l, b in zip(self.parts, self.layouts, bits)]
        for layout, bit in zip(self.layouts, bits):
            layout.remove(bit)
        return [k for k, _ in pairs], [s.astype(bf16) for _, s in pairs]

    def step(self, bits, kept=None, sent=None):
        if kept is None:
            kept, sent = self.split(bits)
        self.add(kept, [chip_swap(x, 1 << bit) for x, bit in zip(sent, bits)])

    def add(self, kept, arrived):
        self.parts = [k.astype(f32) + a.astype(f32) for k, a in zip(kept, arrived)]
        if self.layouts[0]:
            self.parts = [x.astype(bf16) for x in self.parts]


def dot(left, right, left_axis, right_axis):
    return lax.dot_general(
        left, right, (((left_axis,), (right_axis,)), ((), ())), preferred_element_type=f32
    )


def rms_back(grad_in, values, scale_rows, gain_row):
    weighted = grad_in * gain_row
    return scale_rows * weighted - values * scale_rows**3 * jnp.mean(
        weighted * values, axis=-1, keepdims=True
    )


def half_of(x, which, axis):
    size = x.shape[axis] // 2
    return lax.dynamic_slice_in_dim(x, which * size, size, axis)


def head_columns(x, core):
    q_width, kv_width = H * HD, KVH * HD
    return jnp.concatenate(
        [
            half_of(x[:, :q_width], core, 1),
            half_of(x[:, q_width : q_width + kv_width], core, 1),
            half_of(x[:, q_width + kv_width :], core, 1),
        ],
        axis=1,
    )


def by_core(mine, other, core):
    return jnp.stack([jnp.where(core == 0, mine, other), jnp.where(core == 0, other, mine)])


def order_weights_kernel(flips, extra_rows, where_ref, *refs):
    parts, out = refs[: 2 * len(flips)], refs[2 * len(flips)]
    chip, core = where_ref[0], where_ref[1]
    count, rows = parts[0].shape[0], out.shape[2]
    at = 0
    for p, part_flips in enumerate(flips):
        columns = parts[2 * p].shape[3]
        for k, flip in enumerate(part_flips):
            part = parts[2 * p + k // count]
            for h in range(2):
                out[chip ^ flip, core ^ h, :, at : at + columns] = part[k % count, h, :rows]
                if extra_rows and p == len(flips) - 1:
                    extra = part[k % count, h, rows:].astype(f32)[:1]
                    refs[-1][chip ^ flip, core ^ h] = extra
        at += columns


def order_weights(parts, flips, where):
    count, _, rows, _ = parts[0].shape
    columns = sum(p.shape[3] for p in parts[::2])
    extra = parts[-1].shape[2] > rows
    shapes = [jax.ShapeDtypeStruct((2 * count, 2, rows, columns), bf16)]
    if extra:
        shapes.append(jax.ShapeDtypeStruct((2 * count, 2, 1, parts[-1].shape[3]), f32))
    return pl.pallas_call(
        functools.partial(order_weights_kernel, flips, extra),
        out_shape=shapes,
        in_specs=[SMEM] + [VMEM] * len(parts),
        out_specs=[VMEM] * len(shapes),
        compiler_params=BIG,
        name="order_weights",
    )(where, *parts)


def order_rows_kernel(flips, where_ref, *refs):
    out = refs[-1]
    chip, core = where_ref[0], where_ref[1]
    group = chip % len(flips)
    for k, flip in enumerate(flips):
        out[:, group ^ flip, core] = refs[k][...]
        out[:, group ^ flip, 1 - core] = refs[len(flips) + k][...]


def order_rows(own, other, flips, where):
    members, rows, columns = own[0].shape
    groups = len(own)
    tile = columns // 2 if columns % 256 == 0 else columns
    source = pl.BlockSpec((1, rows, tile), lambda m, n: (m, 0, n))
    return pl.pallas_call(
        functools.partial(order_rows_kernel, flips),
        grid=(members, columns // tile),
        out_shape=jax.ShapeDtypeStruct((members, groups, 2, rows, columns), bf16),
        in_specs=[SMEM] + [source] * (2 * groups),
        out_specs=pl.BlockSpec((1, groups, 2, rows, tile), lambda m, n: (m, 0, 0, 0, n)),
        compiler_params=BIG,
        name="order_rows",
    )(where, *own, *other)


def order_tokens_kernel(flips, cuts, groups, where_ref, *refs):
    out = refs[-1]
    member = where_ref[0] // groups
    for p, (start, stop) in enumerate(cuts):
        for k, flip in enumerate(flips[p]):
            half = refs[2 * p + k // 4]
            out[member ^ (flip // groups), start:stop, :] = half[k % 4]


def order_tokens(halves, flips, cuts, groups, where):
    rows, width = cuts[-1][1], halves[0].shape[2]
    return pl.pallas_call(
        functools.partial(order_tokens_kernel, flips, cuts, groups),
        out_shape=jax.ShapeDtypeStruct((8, rows, width), bf16),
        in_specs=[SMEM] + [VMEM] * len(halves),
        out_specs=VMEM,
        compiler_params=BIG,
        name="order_tokens",
    )(where, *halves)


def padded(ff_own):
    return -(-ff_own // 128) * 128


def pack_members_kernel(gate, up, out):
    own, wide = gate.shape[1] // 8, out.shape[2] // 2
    for m in range(8):
        for at, source in ((0, gate), (wide, up)):
            out[m, :, at : at + own] = source[:, m * own : (m + 1) * own]
            out[m, :, at + own : at + wide] = jnp.zeros((out.shape[1], wide - own), bf16)


def pack_members(gate, up):
    rows, ff = gate.shape
    return pl.pallas_call(
        pack_members_kernel,
        out_shape=jax.ShapeDtypeStruct((8, rows, 2 * padded(ff // 8)), bf16),
        in_specs=[VMEM] * 2,
        out_specs=VMEM,
        compiler_params=BIG,
        name="pack_members",
    )(gate, up)


def unpack_members_kernel(packed_gate, packed_up, gate, up):
    own = gate.shape[1] // 8
    for m in range(8):
        for packed, target in ((packed_gate, gate), (packed_up, up)):
            target[:, m * own : (m + 1) * own] = packed[m, :, :own].astype(f32)


def unpack_members(packed_gate, packed_up, ff):
    rows = packed_gate.shape[1]
    return pl.pallas_call(
        unpack_members_kernel,
        out_shape=[jax.ShapeDtypeStruct((rows, ff), f32)] * 2,
        in_specs=[VMEM] * 2,
        out_specs=[VMEM] * 2,
        compiler_params=BIG,
        name="unpack_members",
    )(packed_gate, packed_up)


def mlp_kernel(loads, groups, where_ref, normed, out_grad, down, *refs):
    sources = refs[: len(loads)]
    pre_grad, activated, normed_grad, gate_up, arrived = refs[len(loads) :]
    chip, core = where_ref[0], where_ref[1]

    @pl.when(pl.program_id(0) == 0)
    def _():
        copies = []
        for source, (flip, other, first) in zip(sources, loads):
            if flip is None:
                copies.append(pltpu.make_async_copy(source, gate_up, arrived.at[len(copies)]))
                continue
            rows = source.shape[1]
            for i in range(source.shape[0]):
                device = 2 * ((first + i) * groups + (chip % groups ^ flip)) + (core ^ other)
                target = gate_up.at[pl.ds(pl.multiple_of(device * rows, 16), rows), :]
                copies.append(pltpu.make_async_copy(source.at[i], target, arrived.at[len(copies)]))
        for copy in copies:
            copy.start()
        for copy in copies:
            copy.wait()

    ff_own = down.shape[0]
    wide = gate_up.shape[1] // 2
    gates, ups = slice(0, ff_own), slice(wide, wide + ff_own)
    n = normed[...]
    gate = dot(n, gate_up[:, gates], 1, 0)
    up = dot(n, gate_up[:, ups], 1, 0)
    act_grad = dot(out_grad[...], down[...], 1, 1)
    sig = jax.nn.sigmoid(gate)
    act = gate * sig
    activated[...] = (act * up).astype(bf16)
    if wide > ff_own:
        gap = jnp.zeros((n.shape[0], wide - ff_own), bf16)
        pre_grad[:, ff_own:wide] = gap
        pre_grad[:, wide + ff_own :] = gap
    pre_grad[:, gates] = (act_grad * up * sig * (1.0 + gate * (1.0 - sig))).astype(bf16)
    pre_grad[:, ups] = (act_grad * act).astype(bf16)
    normed_grad[...] = dot(pre_grad[...], gate_up[...], 1, 1).astype(bf16)


def mlp(where, groups, normed, out_grad, down, sources, loads, tile=256):
    rows, width = normed.shape
    ff_own, wide = down.shape[0], sources[0].shape[-1]
    count = sum(1 if flip is None else x.shape[0] for x, (flip, _, _) in zip(sources, loads))

    def by_rows(columns):
        return pl.BlockSpec((tile, columns), lambda i: (i, 0))

    return pl.pallas_call(
        functools.partial(mlp_kernel, loads, groups),
        grid=(rows // tile,),
        out_shape=[
            jax.ShapeDtypeStruct((rows, wide), bf16),
            jax.ShapeDtypeStruct((rows, ff_own), bf16),
            jax.ShapeDtypeStruct((rows, width), bf16),
        ],
        in_specs=[
            SMEM,
            by_rows(width),
            by_rows(width),
            pl.BlockSpec(down.shape, lambda i: (0, 0), pipeline_mode=pl.Buffered(1)),
        ]
        + [pl.BlockSpec(memory_space=pl.ANY)] * len(sources),
        out_specs=[by_rows(wide), by_rows(ff_own), by_rows(width)],
        scratch_shapes=[pltpu.VMEM((width, wide), bf16), pltpu.SemaphoreType.DMA((count,))],
        compiler_params=BIG,
        name="mlp",
    )(where, normed, out_grad, down, *sources)


def gate_up_grads_kernel(rows_dev, where_ref, normed, pre_grad, keep, send):
    grads = dot(normed[...], pre_grad[...], 0, 0)
    core = where_ref[1]
    for i in range(keep.shape[0]):
        low = grads[2 * i * rows_dev : (2 * i + 1) * rows_dev].astype(bf16)
        upper = grads[(2 * i + 1) * rows_dev : (2 * i + 2) * rows_dev].astype(bf16)
        keep[i] = jnp.where(core == 0, low, upper)
        send[i] = jnp.where(core == 0, upper, low)


def gate_up_grads(normed, pre_grad, rows_dev, where, tile=384):
    rows, width = normed.shape
    wide = pre_grad.shape[1]
    chips, step = width // (2 * rows_dev), tile // (2 * rows_dev)
    result = pl.BlockSpec((step, rows_dev, wide), lambda i: (i, 0, 0))
    return pl.pallas_call(
        functools.partial(gate_up_grads_kernel, rows_dev),
        grid=(width // tile,),
        out_shape=[jax.ShapeDtypeStruct((chips, rows_dev, wide), bf16)] * 2,
        in_specs=[
            SMEM,
            pl.BlockSpec((rows, tile), lambda i: (0, i)),
            pl.BlockSpec((rows, wide), lambda i: (0, 0), pipeline_mode=pl.Buffered(1)),
        ],
        out_specs=[result] * 2,
        compiler_params=BIG,
        name="gate_up_grads",
    )(where, normed, pre_grad)


def down_grads_kernel(where_ref, activated, out_grad, keep, send):
    grads = dot(activated[...], out_grad[...], 0, 0)
    core = where_ref[1]
    rows_dev = keep.shape[1]
    for i in range(keep.shape[0]):
        low = grads[2 * i * rows_dev : (2 * i + 1) * rows_dev].astype(bf16)
        upper = grads[(2 * i + 1) * rows_dev : (2 * i + 2) * rows_dev].astype(bf16)
        keep[i] = jnp.where(core == 0, low, upper)
        send[i] = jnp.where(core == 0, upper, low)


def down_grads(activated, out_grad, groups, where, tile=512):
    rows, ff_own = activated.shape
    width = out_grad.shape[1]
    rows_dev = ff_own // (2 * groups)
    result = pl.BlockSpec((groups, rows_dev, tile), lambda i: (0, 0, i))
    return pl.pallas_call(
        down_grads_kernel,
        grid=(width // tile,),
        out_shape=[jax.ShapeDtypeStruct((groups, rows_dev, width), bf16)] * 2,
        in_specs=[
            SMEM,
            pl.BlockSpec((rows, ff_own), lambda i: (0, 0), pipeline_mode=pl.Buffered(1)),
            pl.BlockSpec((rows, tile), lambda i: (0, i)),
        ],
        out_specs=[result] * 2,
        compiler_params=BIG,
        name="down_grads",
    )(where, activated, out_grad)


def project_kernel(heads, own, other, gain, weight, bias, cos, sin, normed, queries, kv):
    hq = heads * HD
    for s, tokens in enumerate((own, other)):
        x = tokens[...].astype(f32)
        scale = lax.rsqrt(jnp.mean(x * x, axis=-1, keepdims=True) + EPSILON)
        n = (x * scale * gain[...]).astype(bf16)
        normed[s] = n
        cos_s, sin_s = cos[s], sin[s]
        project = dot(n, weight[...], 1, 0) + bias[...]

        def turn(z):
            return z * cos_s + pltpu.roll(z, HD // 2, 1) * sin_s

        for h in range(heads):
            queries[s, h] = turn(project[:, h * HD : (h + 1) * HD]).astype(bf16)
        kv[s, :, :HD] = turn(project[:, hq : hq + HD]).astype(bf16)
        kv[s, :, HD:] = project[:, hq + HD :].astype(bf16)


def project(own, other, gain, weight, bias, cos, sin):
    rows, width = own.shape
    heads = H // KVH
    return pl.pallas_call(
        functools.partial(project_kernel, heads),
        out_shape=[
            jax.ShapeDtypeStruct((2, rows, width), bf16),
            jax.ShapeDtypeStruct((2, heads, rows, HD), bf16),
            jax.ShapeDtypeStruct((2, rows, 2 * HD), bf16),
        ],
        in_specs=[VMEM] * 7,
        out_specs=[VMEM] * 3,
        compiler_params=BIG,
        name="project",
    )(own, other, gain, weight, bias, cos, sin)


def pieces(cuts, half):
    found = []
    for p, (start, stop) in enumerate(cuts):
        for b in range(2):
            low, high = max(start, b * half), min(stop, (b + 1) * half)
            if low < high:
                found.append((p, low - start, low - b * half, high - low, b))
    return found


def attend_kernel(
    flips, cuts, heads, where_ref, range_ref, queries, starts, places, weight, *refs
):
    parts, (kv, attended, attended_b, logs, branch) = refs[: 2 * len(cuts)], refs[2 * len(cuts) :]
    chip = where_ref[0]
    rows = queries.shape[2]
    half = rows // 2
    count = parts[0].shape[0]
    chips = 2 * count
    for p, first, at, size, b in pieces(cuts, half):
        for k, flip in enumerate(flips[p]):
            part = parts[2 * p + k // count]
            source = chip ^ flip
            block = source if b == 0 else 2 * chips - 1 - source
            place = pl.multiple_of(block * half + at, 16)
            for s in range(2):
                kv[s, pl.ds(place, size), :] = part[k % count, s, first : first + size, :]

    for s in range(2):
        for b in range(2):
            mine = slice(b * half, (b + 1) * half)
            q = queries[s, :, mine, :].reshape(heads * half, HD)
            start = jnp.concatenate([starts[s, mine, :]] * heads, axis=0)
            place = jnp.concatenate([places[s, mine, :]] * heads, axis=0)

            def step(i, state):
                top, total, out = state
                first = pl.multiple_of(i * CHUNK, CHUNK)
                keys = kv[s, pl.ds(first, CHUNK), :HD]
                values = kv[s, pl.ds(first, CHUNK), HD:]
                scores = dot(q, keys, 1, 1) * SCALE
                key_place = first + lax.broadcasted_iota(jnp.int32, scores.shape, 1)
                seen = (key_place >= start) & (key_place <= place)
                scores = jnp.where(seen, scores, NEVER)
                new_top = jnp.maximum(top, jnp.max(scores, axis=1, keepdims=True))
                fade = jnp.exp(top - new_top)
                weights = jnp.exp(scores - new_top)
                total = total * fade + jnp.sum(weights, axis=1, keepdims=True)
                out = out * fade + dot(weights.astype(bf16), values, 1, 0)
                return new_top, total, out

            at = 4 * s + 2 * b
            top, total, out = lax.fori_loop(
                range_ref[at],
                range_ref[at + 1],
                step,
                (
                    jnp.full((heads * half, 1), NEVER, f32),
                    jnp.zeros((heads * half, 1), f32),
                    jnp.zeros((heads * half, HD), f32),
                ),
            )
            out = out / total
            logs[s, b] = top + jnp.log(total)
            attended[s, b] = out
            for h in range(heads):
                attended_b[s, mine, h * HD : (h + 1) * HD] = out[h * half : (h + 1) * half].astype(
                    bf16
                )
        branch[s] = dot(attended_b[s], weight[...], 1, 1)


def attend(where, ranges, queries, starts, places, weight, parts, flips, cuts):
    _, heads, rows, _ = queries.shape
    keys = 2 * parts[0].shape[0] * rows
    half = rows // 2
    return pl.pallas_call(
        functools.partial(attend_kernel, flips, cuts, heads),
        out_shape=[
            jax.ShapeDtypeStruct((2, keys, 2 * HD), bf16),
            jax.ShapeDtypeStruct((2, 2, heads * half, HD), f32),
            jax.ShapeDtypeStruct((2, rows, heads * HD), bf16),
            jax.ShapeDtypeStruct((2, 2, heads * half, 1), f32),
            jax.ShapeDtypeStruct((2, rows, weight.shape[0]), f32),
        ],
        in_specs=[SMEM] * 2 + [VMEM] * (4 + len(parts)),
        out_specs=[VMEM] * 5,
        compiler_params=BIG,
        name="attend",
    )(where, ranges, queries, starts, places, weight, *parts)


def attend_back_kernel(
    heads,
    range_ref,
    branch_own,
    branch_other,
    weight,
    queries,
    kv,
    attended,
    logs,
    starts,
    places,
    cos,
    sin,
    query_out,
    kv_out,
    grads,
    kv_sum,
):
    rows = queries.shape[2]
    half = rows // 2
    chips = kv.shape[1] // rows
    kv_sum[...] = jnp.zeros_like(kv_sum)
    for s, branch in enumerate((branch_own, branch_other)):
        grads[s] = dot(branch[...], weight[...], 1, 0).astype(bf16)
    for s in range(2):
        for b in range(2):
            mine = slice(b * half, (b + 1) * half)
            q = queries[s, :, mine, :].reshape(heads * half, HD)
            start = jnp.concatenate([starts[s, mine, :]] * heads, axis=0)
            place = jnp.concatenate([places[s, mine, :]] * heads, axis=0)
            grad = jnp.concatenate(
                [grads[s, mine, h * HD : (h + 1) * HD] for h in range(heads)], axis=0
            )
            delta = jnp.sum(grad.astype(f32) * attended[s, b], axis=1, keepdims=True)
            log_total = logs[s, b]

            def step(i, query_grad):
                first = pl.multiple_of(i * CHUNK, CHUNK)
                keys = kv[s, pl.ds(first, CHUNK), :HD]
                values = kv[s, pl.ds(first, CHUNK), HD:]
                scores = dot(q, keys, 1, 1) * SCALE
                key_place = first + lax.broadcasted_iota(jnp.int32, scores.shape, 1)
                seen = (key_place >= start) & (key_place <= place)
                weights = jnp.where(seen, jnp.exp(scores - log_total), 0.0)
                weight_grad = dot(grad, values, 1, 1)
                score_grad = (weights * (weight_grad - delta)).astype(bf16)
                kv_sum[s, pl.ds(first, CHUNK), :HD] += dot(score_grad, q, 0, 0)
                kv_sum[s, pl.ds(first, CHUNK), HD:] += dot(weights.astype(bf16), grad, 0, 0)
                return query_grad + dot(score_grad, keys, 1, 0)

            at = 4 * s + 2 * b
            query_grad = lax.fori_loop(
                range_ref[at], range_ref[at + 1], step, jnp.zeros((heads * half, HD), f32)
            )
            cos_b, sin_b = cos[s, mine, :] * SCALE, sin[s, mine, :] * SCALE
            for h in range(heads):
                z = query_grad[h * half : (h + 1) * half]
                z = z * cos_b - pltpu.roll(z, HD // 2, 1) * sin_b
                query_out[s, mine, h * HD : (h + 1) * HD] = z.astype(bf16)

    def give(chip, carry):
        for s in range(2):
            for b in range(2):
                block = chip if b == 0 else 2 * chips - 1 - chip
                place = pl.multiple_of(block * half, half)
                mine = slice(b * half, (b + 1) * half)
                source = kv_sum[s, pl.ds(place, half), :]
                kv_out[chip % 8, chip // 8, s, mine, :HD] = (source[:, :HD] * SCALE).astype(bf16)
                kv_out[chip % 8, chip // 8, s, mine, HD:] = source[:, HD:].astype(bf16)
        return carry

    lax.fori_loop(0, chips, give, 0)


def attend_back(
    ranges, branch_own, branch_other, weight, queries, kv, attended, logs, starts, places, cos, sin
):
    _, heads, rows, _ = queries.shape
    keys = kv.shape[1]
    chips = keys // rows
    return pl.pallas_call(
        functools.partial(attend_back_kernel, heads),
        out_shape=[
            jax.ShapeDtypeStruct((2, rows, heads * HD), bf16),
            jax.ShapeDtypeStruct((8, chips // 8, 2, rows, 2 * HD), bf16),
        ],
        in_specs=[SMEM] + [VMEM] * 11,
        out_specs=[VMEM] * 2,
        scratch_shapes=[
            pltpu.VMEM((2, rows, heads * HD), bf16),
            pltpu.VMEM((2, keys, 2 * HD), f32),
        ],
        compiler_params=BIG,
        name="attend_back",
    )(
        ranges,
        branch_own,
        branch_other,
        weight,
        queries,
        kv,
        attended,
        logs,
        starts,
        places,
        cos,
        sin,
    )


def on_device(
    tokens, cotangent, doc_lengths, norm_attn, w_qkv, b_qkv, w_out, norm_mlp, w_gate, w_up, w_down
):
    ctx_size = lax.axis_size("ctx")
    chip = lax.axis_index("ctx")
    core = lax.axis_index("wshard")
    where = jnp.stack([chip, core]).astype(jnp.int32)
    high = high_bits()
    groups = ctx_size // 8
    tok_dev, width = tokens.shape[1], tokens.shape[2]
    ff = w_gate.shape[1]
    ff_own = ff // 8
    heads = H // KVH
    hq = heads * HD
    rows_dev = w_qkv.shape[0]
    cuts = row_parts(tok_dev)
    half = tok_dev // 2
    flips = [relative_flips(high + order) for order in ORDERS]
    group_flips = relative_flips(group_bits())
    low, middle, upper = member_bits()

    n_gain, n_bias = norm_attn.shape[0], b_qkv.shape[0]
    small = jnp.concatenate([norm_attn, b_qkv, norm_mlp])[None]
    small = jnp.pad(small, ((0, 15), (hq, 2 * HD - small.shape[1])))
    qkv_send = jnp.concatenate([head_columns(w_qkv, 1 - core), small])
    qkv_own = jnp.concatenate([head_columns(w_qkv, core), small])
    token_own, out_grad_b = tokens[0], cotangent[0]
    out_t = w_out.T
    qkv_other = core_swap(qkv_send)
    token_other = core_swap(token_own)
    length_other = core_swap(doc_lengths[0])
    out_other = core_swap(half_of(out_t, 1 - core, 1))
    down_found = gather_list(w_down, group_bits())
    length_pair = jnp.stack([doc_lengths[0], length_other])
    qkv_pair = jnp.stack([qkv_own, qkv_other])[None]
    qkv_pair, w_gate, out_other = together(qkv_pair, w_gate, out_other)
    out_pair = by_core(half_of(out_t, core, 1), out_other, core)
    out_w = lax.all_gather(out_pair, "ctx", axis=0, tiled=False).reshape(width, hq)
    out_grad_all = lax.all_gather(
        after(out_grad_b, out_w), "ctx", axis=0, tiled=True, axis_index_groups=group_lists()
    )
    qkv_pair = gather_relative(qkv_pair, high)
    packed = pack_members(w_gate, w_up)
    qkv_pair, packed, down_found = together(qkv_pair, packed, down_found)
    column_cuts = ((0, hq // 2, rows_dev), (hq // 2, hq, rows_dev), (hq, hq + 2 * HD, rows_dev + 16))
    qkv_parts = [qkv_pair[:, :, :rows, start:stop] for start, stop, rows in column_cuts]
    qkv_parts = doubled(qkv_parts, [order[0] for order in ORDERS])
    packed = group_exchange(packed)
    down_other = [core_swap(x) for x in down_found]
    qkv_parts = doubled(qkv_parts, [order[1] for order in ORDERS])
    qkv_parts, packed = together(qkv_parts, packed)
    packed_other = core_swap(packed)
    qkv_parts = with_arrived(qkv_parts, [order[2] for order in ORDERS])
    shares = ((0, 3), (3, 8))
    qkv_parts, packed = together(qkv_parts, packed)
    packed_found = [gather_list(packed[:3], group_bits())]

    inner = jnp.arange(tok_dev, dtype=jnp.int32)
    blocks = jnp.where(inner < half, chip, 2 * ctx_size - 1 - chip)
    places = (blocks * half + inner % half).astype(jnp.int32)
    ends = jnp.cumsum(length_pair, axis=1)
    passed = ends[:, None, :] <= places[None, :, None]
    starts = jnp.sum(jnp.where(passed, length_pair[:, None, :], 0), axis=2)
    places = jnp.broadcast_to(places[None], starts.shape)
    frequency = ROPE_BASE ** (-jnp.arange(HD // 2, dtype=f32) * 2.0 / HD)
    angles = (places - starts).astype(f32)[..., None] * frequency
    cos_half, sin_half = jnp.cos(angles), jnp.sin(angles)
    cos = jnp.concatenate([cos_half, cos_half], axis=-1)
    sin = jnp.concatenate([-sin_half, sin_half], axis=-1)
    first = jnp.min(starts.reshape(2, 2, half), axis=2) // CHUNK
    last = jnp.max(places.reshape(2, 2, half), axis=2) // CHUNK + 1
    ranges = jnp.stack([first, last], axis=-1).reshape(-1).astype(jnp.int32)
    starts, places = starts[..., None], places[..., None]

    qkv_w, small_all = order_weights(qkv_parts, flips, where)
    qkv_w = qkv_w.reshape(width, hq + 2 * HD)
    small_all = small_all.reshape(2 * ctx_size, 2 * HD)
    gain_one = small_all[:, :n_gain].reshape(1, -1)
    bias = small_all[:, n_gain : n_gain + n_bias].reshape(1, -1)
    gain_two = small_all[:, n_gain + n_bias : 2 * n_gain + n_bias].reshape(1, -1)
    bias = head_columns(bias, core)
    normed_one, queries, kv_own = project(token_own, token_other, gain_one, qkv_w, bias, cos, sin)
    kv_own, packed_found, packed = together(kv_own, packed_found, packed)

    kv_own = gather_relative(kv_own[None], high)
    kv_own, packed = together(kv_own, packed)
    packed_found.append(gather_list(packed[3:], group_bits()))
    kv_parts = [kv_own[:, :, start:stop] for start, stop in cuts]
    for step in range(2):
        kv_parts = doubled(kv_parts, [order[step] for order in ORDERS])
    kv_parts, packed_found, packed = together(kv_parts, packed_found, packed)
    down = order_rows([x[None] for x in down_found], [x[None] for x in down_other], group_flips, where)
    down = down.reshape(ff_own, width)
    kv_parts = with_arrived(kv_parts, [order[2] for order in ORDERS])
    kv_parts, down, out_w = together(kv_parts, down, out_w)
    kv, attended, attended_b, logs, branch = attend(
        where, ranges, queries, starts, places, out_w, kv_parts, flips, cuts
    )
    branch_other = core_swap(branch[1])
    inputs = token_own.astype(f32)
    hidden_res = inputs + branch[0] + branch_other
    scale_two = lax.rsqrt(jnp.mean(hidden_res * hidden_res, axis=-1, keepdims=True) + EPSILON)
    normed_two = (hidden_res * scale_two * gain_two).astype(bf16)

    group_orders = ((upper, middle, low), (upper, low, middle))
    group_cuts = ((0, half), (half, tok_dev))
    token_parts = gather_relative(normed_two[None], (upper,))
    token_parts = [token_parts[:, start:stop] for start, stop in group_cuts]
    token_parts = doubled(token_parts, [order[1] for order in group_orders])
    token_parts = with_arrived(token_parts, [order[2] for order in group_orders])
    token_flips = [relative_flips(order) for order in group_orders]
    normed_all = order_tokens(token_parts, token_flips, group_cuts, groups, where)
    normed_all = normed_all.reshape(8 * tok_dev, width)

    sources, loads = [packed, packed_other], [(0, 0, 0), (0, 1, 0)]
    for found, (first, _) in zip(packed_found, shares):
        for piece, flip in list(zip(found, group_flips))[1:]:
            sources.extend([piece, core_swap(piece)])
            loads.extend([(flip, 0, first), (flip, 1, first)])
    if rows_dev % 16:
        own, other = [], []
        for flip in group_flips:
            for core_flip, side in enumerate((own, other)):
                found = [x for x, load in zip(sources, loads) if load[:2] == (flip, core_flip)]
                side.append(jnp.concatenate(found))
        sources, loads = [order_rows(own, other, group_flips, where).reshape(width, -1)], [(None, 0, 0)]
    out_grad = out_grad_b.astype(f32)
    pre_grad, activated, normed_grad_part = mlp(
        where, groups, normed_all, out_grad_all, down, sources, loads
    )

    normed_grad_part = normed_grad_part.reshape(2, 2, 2, tok_dev, width)
    scatter = Scatter(
        [normed_grad_part[:, :, :, start:stop] for start, stop in group_cuts], (upper, middle, low)
    )
    bits = [order[2] for order in group_orders]
    kept, sent = scatter.split(bits)
    gu_keep, gu_send = gate_up_grads(normed_all, after(pre_grad, *sent), rows_dev, where)
    scatter.step(bits, kept, sent)
    scatter.parts, gu_keep, gu_send = together(scatter.parts, gu_keep, gu_send)

    bits = [order[1] for order in group_orders]
    kept, sent = scatter.split(bits)
    gu_arrived = core_swap(gu_send)
    branch_part = dot(after(activated, *sent), down, 1, 0).astype(bf16)
    scatter.step(bits, kept, sent)
    scatter.parts, branch_part, gu_arrived = together(scatter.parts, branch_part, gu_arrived)

    kept, sent = scatter.split((upper, upper))
    gu_sum = (gu_keep.astype(f32) + gu_arrived.astype(f32)).astype(bf16)
    scatter.step((upper, upper), kept, sent)
    scatter.parts, gu_sum, branch_part = together(scatter.parts, gu_sum, branch_part)
    branch_mlp = lax.psum_scatter(
        branch_part, "ctx", scatter_dimension=0, tiled=True, axis_index_groups=group_lists()
    )
    normed_two_grad = jnp.concatenate(scatter.parts)
    gain_two_grad = jnp.sum(normed_two_grad * hidden_res * scale_two, axis=0)
    hidden_grad = out_grad + rms_back(normed_two_grad, hidden_res, scale_two, gain_two)

    wide = gu_sum.shape[2] // 2
    column = wide // 256 * 128
    gu_cuts = ((0, column), (column, wide), (wide, wide + column), (wide + column, 2 * wide))
    gu_pieces = [gu_sum.reshape(8, groups, rows_dev, -1)[..., a:b] for a, b in gu_cuts]
    falling = tuple(reversed(group_bits()))
    gu_done = []

    def weight_parts(x):
        return x.astype(bf16).reshape(ctx_size // 8, 8, 2, rows_dev, x.shape[1])

    branch_own = hidden_grad.astype(bf16)
    branch_other = core_swap(branch_own)
    gu_done.append(sum_over(gu_pieces[0], 1, falling).astype(bf16))
    branch_own, branch_other, gu_pieces, gu_done = together(
        branch_own, branch_other, gu_pieces, gu_done
    )
    gu_done.append(sum_over(gu_pieces[1], 1, falling).astype(bf16))
    project_grad_q, kv_grad = attend_back(
        ranges, branch_own, branch_other, out_w, queries, kv, attended, logs, starts, places, cos, sin
    )
    (kv_grad, project_grad_q), gu_done, gu_pieces, activated = together(
        (kv_grad, project_grad_q), gu_done, gu_pieces, activated
    )
    kv_sum = cube_exchange(kv_grad)
    gu_third = sum_over(gu_pieces[2], 1, falling).astype(bf16)
    down_keep, down_send = down_grads(activated, out_grad_all, groups, where)
    branch_grad = jnp.concatenate([branch_own, branch_other])
    normed_one = normed_one.reshape(-1, width)
    project_grad_q = project_grad_q.reshape(-1, hq)
    grad_out_part = weight_parts(dot(branch_grad, attended_b.reshape(-1, hq), 0, 0))
    grad_q_part = weight_parts(dot(normed_one, project_grad_q, 0, 0))
    wide_part = jnp.concatenate([grad_q_part, grad_out_part], axis=-1)
    names = tuple(reversed(high)) + (2, 1, 0)
    wide_part = wide_part.reshape((2,) * len(names) + wide_part.shape[2:])
    third = 2 * hq // 3
    scatter = Scatter([wide_part[..., i * third : (i + 1) * third] for i in range(3)], names)
    bits = [order[0] for order in ORDERS]
    kept, sent = scatter.split(bits)
    kv_sum, sent, down_send = together(kv_sum, sent, down_send)

    kv_sum = jnp.sum(kv_sum.astype(f32), axis=0).astype(bf16)
    kv_sum = sum_over_high(kv_sum, high)
    grad_gate = group_exchange(jnp.concatenate(gu_done, axis=2))
    arrived = [chip_swap(x, 1 << bit) for x, bit in zip(sent, bits)]
    key_pre = kv_sum[..., :HD]
    key_pre = key_pre * cos - jnp.roll(key_pre, HD // 2, axis=-1) * sin
    project_grad_kv = jnp.concatenate([key_pre, kv_sum[..., HD:]], axis=-1).astype(bf16)
    project_grad_kv = project_grad_kv.reshape(-1, 2 * HD)
    grad_kv = weight_parts(dot(normed_one, project_grad_kv, 0, 0)).swapaxes(0, 1)
    grad_kv, grad_gate, arrived, gu_third, gu_pieces = together(
        grad_kv, grad_gate, arrived, gu_third, gu_pieces
    )

    grad_kv = cube_exchange(grad_kv)
    gu_last = sum_over(gu_pieces[3], 1, falling).astype(bf16)
    scatter.add(kept, arrived)
    scatter.step([order[1] for order in ORDERS])
    down_arrived = core_swap(down_send)
    project_grad = jnp.concatenate([project_grad_q, project_grad_kv], axis=1)
    normed_one_grad = dot(project_grad, qkv_w, 1, 1)
    normed_one_grad = normed_one_grad[:tok_dev] + core_swap(normed_one_grad[tok_dev:])
    grad_kv, gu_last, scatter.parts, down_arrived = together(
        grad_kv, gu_last, scatter.parts, down_arrived
    )
    grad_up = group_exchange(jnp.concatenate([gu_third, gu_last], axis=2))
    grad_kv = jnp.sum(grad_kv.astype(f32), axis=0).astype(bf16)
    grad_kv = sum_over_high(grad_kv, high)
    down_sum = (down_keep.astype(f32) + down_arrived.astype(f32)).astype(bf16)
    grad_down = sum_over(down_sum, 0, falling)
    scatter.step([order[2] for order in ORDERS])
    scatter.parts = [jnp.concatenate(scatter.parts, axis=-1)]
    scale_one = lax.rsqrt(jnp.mean(inputs * inputs, axis=-1, keepdims=True) + EPSILON)
    gain_one_grad = jnp.sum(normed_one_grad * inputs * scale_one, axis=0)
    input_grad = hidden_grad + rms_back(normed_one_grad, inputs, scale_one, gain_one)
    grad_kv, grad_up, scatter.parts, gain_one_grad, grad_down, branch_mlp = together(
        grad_kv, grad_up, scatter.parts, gain_one_grad, grad_down, branch_mlp
    )
    output = (hidden_res + branch_mlp.astype(f32)).astype(bf16)
    for bit in reversed(high):
        scatter.step((bit,))
    scattered = scatter.parts[0]

    grad_gate, grad_up = unpack_members(grad_gate, grad_up, ff)
    chip_grad = jnp.concatenate([scattered[..., :hq], grad_kv, scattered[..., hq:]], axis=-1)

    def pick(x, which):
        return lax.dynamic_index_in_dim(x, which, 0, keepdims=False)

    def whole_columns(x):
        return jnp.concatenate(
            [
                x[0, :, :hq],
                x[1, :, :hq],
                x[0, :, hq : hq + HD],
                x[1, :, hq : hq + HD],
                x[0, :, hq + HD : hq + 2 * HD],
                x[1, :, hq + HD : hq + 2 * HD],
            ],
            axis=1,
        )

    pair = by_core(pick(chip_grad, core), core_swap(pick(chip_grad, 1 - core)), core)
    grad_qkv = whole_columns(pair)
    grad_out = pair[:, :, hq + 2 * HD :].transpose(1, 0, 2).reshape(-1, 2 * hq).T

    bias_grad = jnp.sum(project_grad.astype(f32), axis=0, keepdims=True)
    zeros = jnp.zeros_like(bias_grad)
    bias_full = whole_columns(
        jnp.stack([jnp.where(core == 0, bias_grad, zeros), jnp.where(core == 0, zeros, bias_grad)])
    )[0]
    qk_width = (H + KVH) * HD
    sums = jnp.concatenate(
        [
            x.reshape(ctx_size, 1, -1)
            for x in (gain_one_grad, gain_two_grad, bias_full[:qk_width], bias_full[qk_width:])
        ],
        axis=2,
    )
    sums = lax.all_to_all(sums, "ctx", split_axis=0, concat_axis=0, tiled=True)
    sums = jnp.sum(sums, axis=0)
    sums = (sums + core_swap(sums))[0]

    def owned(start, size):
        return lax.dynamic_slice_in_dim(sums, start + core * (size // 2), size // 2, 0)

    own_width, own_qk, own_v = width // ctx_size, qk_width // ctx_size, KVH * HD // ctx_size
    return (
        output[None],
        input_grad[None],
        owned(0, own_width),
        grad_qkv,
        owned(2 * own_width, own_qk),
        owned(2 * own_width + own_qk, own_v),
        grad_out,
        owned(own_width, own_width),
        grad_gate,
        grad_up,
        grad_down,
    )


def solution(mesh):
    whole = ("ctx", "wshard")
    rows, columns, flat = P(whole, None), P(None, whole), P(whole)
    tokens = P("wshard", "ctx", None)
    return jax.shard_map(
        on_device,
        mesh=mesh,
        in_specs=(tokens, tokens, P("wshard", None), flat, rows, flat, columns, flat, rows, rows, rows),
        out_specs=(tokens, tokens, flat, rows, flat, flat, columns, flat, rows, rows, rows),
        check_vma=False,
    )
```

```python
import functools
import math

import jax
import jax.numpy as jnp
from jax import lax
from jax.experimental import pallas as pl
from jax.experimental.pallas import tpu as pltpu
from jax.sharding import PartitionSpec as P

H = 12
KVH = 2
HD = 128
EPSILON = 1e-06
ROPE_BASE = 1000000.0
ORDERS = ((0, 1, 2), (1, 2, 0), (2, 0, 1))
CHUNK = 256
NEVER = -1e30
SCALE = 1.0 / math.sqrt(HD)
bf16 = jnp.bfloat16
f32 = jnp.float32
VMEM = pl.BlockSpec(memory_space=pltpu.VMEM)
SMEM = pl.BlockSpec(memory_space=pltpu.SMEM)
BIG = pltpu.CompilerParams(vmem_limit_bytes=56 * 1024 * 1024)


def after(x, *others):
    return together(x, *others)[0]


def together(*groups):
    flat, tree = jax.tree.flatten(groups)
    return jax.tree.unflatten(tree, lax.optimization_barrier(flat))


def core_swap(x):
    return lax.ppermute(x, "wshard", [(0, 1), (1, 0)])


def chip_swap(x, flip):
    count = lax.axis_size("ctx")
    return lax.ppermute(x, "ctx", [(i, i ^ flip) for i in range(count)])


def cubes():
    count = lax.axis_size("ctx")
    return [list(range(i, i + 8)) for i in range(0, count, 8)]


def cube_exchange(x):
    return lax.all_to_all(
        x, "ctx", split_axis=0, concat_axis=0, tiled=True, axis_index_groups=cubes()
    )


def group_bits():
    return tuple(range(lax.axis_size("ctx").bit_length() - 4))


def member_bits():
    first = len(group_bits())
    return (first, first + 1, first + 2)


def group_lists():
    groups = lax.axis_size("ctx") // 8
    return [[g + groups * m for m in range(8)] for g in range(groups)]


def group_exchange(x):
    return lax.all_to_all(
        x, "ctx", split_axis=0, concat_axis=0, tiled=True, axis_index_groups=group_lists()
    )


def high_bits():
    return tuple(range(3, lax.axis_size("ctx").bit_length() - 1))


def my_bit(bit):
    return (lax.axis_index("ctx") >> bit) & 1


def gather_relative(x, bits):
    for bit in bits:
        x = jnp.concatenate([x, chip_swap(x, 1 << bit)], axis=0)
    return x


def gather_list(x, bits):
    found = [x]
    for bit in bits:
        found = found + [chip_swap(y, 1 << bit) for y in found]
    return found


def relative_flips(bits):
    flips = [0]
    for bit in bits:
        flips = flips + [f ^ (1 << bit) for f in flips]
    return flips


def sum_over(x, axis, bits):
    for at, bit in enumerate(bits):
        shape = x.shape
        x = x.reshape(shape[:axis] + (2, shape[axis] // 2) + shape[axis + 1 :])
        keep = lax.dynamic_index_in_dim(x, my_bit(bit), axis, keepdims=False)
        send = lax.dynamic_index_in_dim(x, 1 - my_bit(bit), axis, keepdims=False)
        x = keep.astype(f32) + chip_swap(send.astype(bf16), 1 << bit).astype(f32)
        if at < len(bits) - 1:
            x = x.astype(bf16)
    return jnp.squeeze(x, axis).astype(f32)


def sum_over_high(x, high):
    return sum_over(x, 0, tuple(reversed(high)))


def row_parts(rows):
    third = rows * 3 // 8
    return ((0, third), (third, 2 * third), (2 * third, rows))


def doubled(parts, bits):
    return [jnp.concatenate([x, chip_swap(x, 1 << bit)]) for x, bit in zip(parts, bits)]


def with_arrived(parts, bits):
    found = []
    for x, bit in zip(parts, bits):
        found.extend([x, chip_swap(x, 1 << bit)])
    return found


def both_halves(x, layout, bit):
    axis = layout.index(bit)
    keep = lax.dynamic_index_in_dim(x, my_bit(bit), axis, keepdims=False)
    send = lax.dynamic_index_in_dim(x, 1 - my_bit(bit), axis, keepdims=False)
    return keep, send


class Scatter:
    def __init__(self, parts, layout):
        self.parts = list(parts)
        self.layouts = [list(layout) for _ in self.parts]

    def split(self, bits):
        pairs = [both_halves(x, l, b) for x, l, b in zip(self.parts, self.layouts, bits)]
        for layout, bit in zip(self.layouts, bits):
            layout.remove(bit)
        return [k for k, _ in pairs], [s.astype(bf16) for _, s in pairs]

    def step(self, bits, kept=None, sent=None):
        if kept is None:
            kept, sent = self.split(bits)
        self.add(kept, [chip_swap(x, 1 << bit) for x, bit in zip(sent, bits)])

    def add(self, kept, arrived):
        self.parts = [k.astype(f32) + a.astype(f32) for k, a in zip(kept, arrived)]
        if self.layouts[0]:
            self.parts = [x.astype(bf16) for x in self.parts]


def dot(left, right, left_axis, right_axis):
    return lax.dot_general(
        left, right, (((left_axis,), (right_axis,)), ((), ())), preferred_element_type=f32
    )


def rms_back(grad_in, values, scale_rows, gain_row):
    weighted = grad_in * gain_row
    return scale_rows * weighted - values * scale_rows**3 * jnp.mean(
        weighted * values, axis=-1, keepdims=True
    )


def half_of(x, which, axis):
    size = x.shape[axis] // 2
    return lax.dynamic_slice_in_dim(x, which * size, size, axis)


def head_columns(x, core):
    q_width, kv_width = H * HD, KVH * HD
    return jnp.concatenate(
        [
            half_of(x[:, :q_width], core, 1),
            half_of(x[:, q_width : q_width + kv_width], core, 1),
            half_of(x[:, q_width + kv_width :], core, 1),
        ],
        axis=1,
    )


def by_core(mine, other, core):
    return jnp.stack([jnp.where(core == 0, mine, other), jnp.where(core == 0, other, mine)])


def order_weights_kernel(flips, extra_rows, where_ref, *refs):
    parts, out = refs[: 2 * len(flips)], refs[2 * len(flips)]
    chip, core = where_ref[0], where_ref[1]
    count, rows = parts[0].shape[0], out.shape[2]
    at = 0
    for p, part_flips in enumerate(flips):
        columns = parts[2 * p].shape[3]
        for k, flip in enumerate(part_flips):
            part = parts[2 * p + k // count]
            for h in range(2):
                out[chip ^ flip, core ^ h, :, at : at + columns] = part[k % count, h, :rows]
                if extra_rows and p == len(flips) - 1:
                    extra = part[k % count, h, rows:].astype(f32)[:1]
                    refs[-1][chip ^ flip, core ^ h] = extra
        at += columns


def order_weights(parts, flips, where):
    count, _, rows, _ = parts[0].shape
    columns = sum(p.shape[3] for p in parts[::2])
    extra = parts[-1].shape[2] > rows
    shapes = [jax.ShapeDtypeStruct((2 * count, 2, rows, columns), bf16)]
    if extra:
        shapes.append(jax.ShapeDtypeStruct((2 * count, 2, 1, parts[-1].shape[3]), f32))
    return pl.pallas_call(
        functools.partial(order_weights_kernel, flips, extra),
        out_shape=shapes,
        in_specs=[SMEM] + [VMEM] * len(parts),
        out_specs=[VMEM] * len(shapes),
        compiler_params=BIG,
        name="order_weights",
    )(where, *parts)


def order_rows_kernel(flips, where_ref, *refs):
    out = refs[-1]
    chip, core = where_ref[0], where_ref[1]
    group = chip % len(flips)
    for k, flip in enumerate(flips):
        out[:, group ^ flip, core] = refs[k][...]
        out[:, group ^ flip, 1 - core] = refs[len(flips) + k][...]


def order_rows(own, other, flips, where):
    members, rows, columns = own[0].shape
    groups = len(own)
    tile = columns // 2 if columns % 256 == 0 else columns
    source = pl.BlockSpec((1, rows, tile), lambda m, n: (m, 0, n))
    return pl.pallas_call(
        functools.partial(order_rows_kernel, flips),
        grid=(members, columns // tile),
        out_shape=jax.ShapeDtypeStruct((members, groups, 2, rows, columns), bf16),
        in_specs=[SMEM] + [source] * (2 * groups),
        out_specs=pl.BlockSpec((1, groups, 2, rows, tile), lambda m, n: (m, 0, 0, 0, n)),
        compiler_params=BIG,
        name="order_rows",
    )(where, *own, *other)


def order_tokens_kernel(flips, cuts, groups, where_ref, *refs):
    out = refs[-1]
    member = where_ref[0] // groups
    for p, (start, stop) in enumerate(cuts):
        for k, flip in enumerate(flips[p]):
            half = refs[2 * p + k // 4]
            out[member ^ (flip // groups), start:stop, :] = half[k % 4]


def order_tokens(halves, flips, cuts, groups, where):
    rows, width = cuts[-1][1], halves[0].shape[2]
    return pl.pallas_call(
        functools.partial(order_tokens_kernel, flips, cuts, groups),
        out_shape=jax.ShapeDtypeStruct((8, rows, width), bf16),
        in_specs=[SMEM] + [VMEM] * len(halves),
        out_specs=VMEM,
        compiler_params=BIG,
        name="order_tokens",
    )(where, *halves)


def padded(ff_own):
    return -(-ff_own // 128) * 128


def pack_members_kernel(gate, up, out):
    own, wide = gate.shape[1] // 8, out.shape[2] // 2
    for m in range(8):
        for at, source in ((0, gate), (wide, up)):
            out[m, :, at : at + own] = source[:, m * own : (m + 1) * own]
            out[m, :, at + own : at + wide] = jnp.zeros((out.shape[1], wide - own), bf16)


def pack_members(gate, up):
    rows, ff = gate.shape
    return pl.pallas_call(
        pack_members_kernel,
        out_shape=jax.ShapeDtypeStruct((8, rows, 2 * padded(ff // 8)), bf16),
        in_specs=[VMEM] * 2,
        out_specs=VMEM,
        compiler_params=BIG,
        name="pack_members",
    )(gate, up)


def unpack_members_kernel(packed_gate, packed_up, gate, up):
    own = gate.shape[1] // 8
    for m in range(8):
        for packed, target in ((packed_gate, gate), (packed_up, up)):
            target[:, m * own : (m + 1) * own] = packed[m, :, :own].astype(f32)


def unpack_members(packed_gate, packed_up, ff):
    rows = packed_gate.shape[1]
    return pl.pallas_call(
        unpack_members_kernel,
        out_shape=[jax.ShapeDtypeStruct((rows, ff), f32)] * 2,
        in_specs=[VMEM] * 2,
        out_specs=[VMEM] * 2,
        compiler_params=BIG,
        name="unpack_members",
    )(packed_gate, packed_up)


def mlp_kernel(loads, groups, where_ref, normed, out_grad, down, *refs):
    sources = refs[: len(loads)]
    pre_grad, activated, normed_grad, gate_up, arrived = refs[len(loads) :]
    chip, core = where_ref[0], where_ref[1]

    @pl.when(pl.program_id(0) == 0)
    def _():
        copies = []
        for source, (flip, other, first) in zip(sources, loads):
            if flip is None:
                copies.append(pltpu.make_async_copy(source, gate_up, arrived.at[len(copies)]))
                continue
            rows = source.shape[1]
            for i in range(source.shape[0]):
                device = 2 * ((first + i) * groups + (chip % groups ^ flip)) + (core ^ other)
                target = gate_up.at[pl.ds(pl.multiple_of(device * rows, 16), rows), :]
                copies.append(pltpu.make_async_copy(source.at[i], target, arrived.at[len(copies)]))
        for copy in copies:
            copy.start()
        for copy in copies:
            copy.wait()

    ff_own = down.shape[0]
    wide = gate_up.shape[1] // 2
    gates, ups = slice(0, ff_own), slice(wide, wide + ff_own)
    n = normed[...]
    gate = dot(n, gate_up[:, gates], 1, 0)
    up = dot(n, gate_up[:, ups], 1, 0)
    act_grad = dot(out_grad[...], down[...], 1, 1)
    sig = jax.nn.sigmoid(gate)
    act = gate * sig
    activated[...] = (act * up).astype(bf16)
    if wide > ff_own:
        gap = jnp.zeros((n.shape[0], wide - ff_own), bf16)
        pre_grad[:, ff_own:wide] = gap
        pre_grad[:, wide + ff_own :] = gap
    pre_grad[:, gates] = (act_grad * up * sig * (1.0 + gate * (1.0 - sig))).astype(bf16)
    pre_grad[:, ups] = (act_grad * act).astype(bf16)
    normed_grad[...] = dot(pre_grad[...], gate_up[...], 1, 1).astype(bf16)


def mlp(where, groups, normed, out_grad, down, sources, loads, tile=256):
    rows, width = normed.shape
    ff_own, wide = down.shape[0], sources[0].shape[-1]
    count = sum(1 if flip is None else x.shape[0] for x, (flip, _, _) in zip(sources, loads))

    def by_rows(columns):
        return pl.BlockSpec((tile, columns), lambda i: (i, 0))

    return pl.pallas_call(
        functools.partial(mlp_kernel, loads, groups),
        grid=(rows // tile,),
        out_shape=[
            jax.ShapeDtypeStruct((rows, wide), bf16),
            jax.ShapeDtypeStruct((rows, ff_own), bf16),
            jax.ShapeDtypeStruct((rows, width), bf16),
        ],
        in_specs=[
            SMEM,
            by_rows(width),
            by_rows(width),
            pl.BlockSpec(down.shape, lambda i: (0, 0), pipeline_mode=pl.Buffered(1)),
        ]
        + [pl.BlockSpec(memory_space=pl.ANY)] * len(sources),
        out_specs=[by_rows(wide), by_rows(ff_own), by_rows(width)],
        scratch_shapes=[pltpu.VMEM((width, wide), bf16), pltpu.SemaphoreType.DMA((count,))],
        compiler_params=BIG,
        name="mlp",
    )(where, normed, out_grad, down, *sources)


def gate_up_grads_kernel(rows_dev, where_ref, normed, pre_grad, keep, send):
    grads = dot(normed[...], pre_grad[...], 0, 0)
    core = where_ref[1]
    for i in range(keep.shape[0]):
        low = grads[2 * i * rows_dev : (2 * i + 1) * rows_dev].astype(bf16)
        upper = grads[(2 * i + 1) * rows_dev : (2 * i + 2) * rows_dev].astype(bf16)
        keep[i] = jnp.where(core == 0, low, upper)
        send[i] = jnp.where(core == 0, upper, low)


def gate_up_grads(normed, pre_grad, side, rows_dev, where, tile=384):
    rows, width = normed.shape
    wide = pre_grad.shape[1] // 2
    chips, step = width // (2 * rows_dev), tile // (2 * rows_dev)
    result = pl.BlockSpec((step, rows_dev, wide), lambda i: (i, 0, 0))
    return pl.pallas_call(
        functools.partial(gate_up_grads_kernel, rows_dev),
        grid=(width // tile,),
        out_shape=[jax.ShapeDtypeStruct((chips, rows_dev, wide), bf16)] * 2,
        in_specs=[
            SMEM,
            pl.BlockSpec((rows, tile), lambda i: (0, i)),
            pl.BlockSpec((rows, wide), lambda i: (0, side), pipeline_mode=pl.Buffered(1)),
        ],
        out_specs=[result] * 2,
        compiler_params=BIG,
        name="gate_up_grads",
    )(where, normed, pre_grad)


def down_grads_kernel(where_ref, activated, out_grad, keep, send):
    grads = dot(activated[...], out_grad[...], 0, 0)
    core = where_ref[1]
    rows_dev = keep.shape[1]
    for i in range(keep.shape[0]):
        low = grads[2 * i * rows_dev : (2 * i + 1) * rows_dev].astype(bf16)
        upper = grads[(2 * i + 1) * rows_dev : (2 * i + 2) * rows_dev].astype(bf16)
        keep[i] = jnp.where(core == 0, low, upper)
        send[i] = jnp.where(core == 0, upper, low)


def down_grads(activated, out_grad, groups, where, tile=512):
    rows, ff_own = activated.shape
    width = out_grad.shape[1]
    rows_dev = ff_own // (2 * groups)
    result = pl.BlockSpec((groups, rows_dev, tile), lambda i: (0, 0, i))
    return pl.pallas_call(
        down_grads_kernel,
        grid=(width // tile,),
        out_shape=[jax.ShapeDtypeStruct((groups, rows_dev, width), bf16)] * 2,
        in_specs=[
            SMEM,
            pl.BlockSpec((rows, ff_own), lambda i: (0, 0), pipeline_mode=pl.Buffered(1)),
            pl.BlockSpec((rows, tile), lambda i: (0, i)),
        ],
        out_specs=[result] * 2,
        compiler_params=BIG,
        name="down_grads",
    )(where, activated, out_grad)


def project_kernel(heads, own, other, gain, weight, bias, cos, sin, normed, queries, kv):
    hq = heads * HD
    for s, tokens in enumerate((own, other)):
        x = tokens[...].astype(f32)
        scale = lax.rsqrt(jnp.mean(x * x, axis=-1, keepdims=True) + EPSILON)
        n = (x * scale * gain[...]).astype(bf16)
        normed[s] = n
        cos_s, sin_s = cos[s], sin[s]
        project = dot(n, weight[...], 1, 0) + bias[...]

        def turn(z):
            return z * cos_s + pltpu.roll(z, HD // 2, 1) * sin_s

        for h in range(heads):
            queries[s, h] = turn(project[:, h * HD : (h + 1) * HD]).astype(bf16)
        kv[s, :, :HD] = turn(project[:, hq : hq + HD]).astype(bf16)
        kv[s, :, HD:] = project[:, hq + HD :].astype(bf16)


def project(own, other, gain, weight, bias, cos, sin):
    rows, width = own.shape
    heads = H // KVH
    return pl.pallas_call(
        functools.partial(project_kernel, heads),
        out_shape=[
            jax.ShapeDtypeStruct((2, rows, width), bf16),
            jax.ShapeDtypeStruct((2, heads, rows, HD), bf16),
            jax.ShapeDtypeStruct((2, rows, 2 * HD), bf16),
        ],
        in_specs=[VMEM] * 7,
        out_specs=[VMEM] * 3,
        compiler_params=BIG,
        name="project",
    )(own, other, gain, weight, bias, cos, sin)


def pieces(cuts, half):
    found = []
    for p, (start, stop) in enumerate(cuts):
        for b in range(2):
            low, high = max(start, b * half), min(stop, (b + 1) * half)
            if low < high:
                found.append((p, low - start, low - b * half, high - low, b))
    return found


def attend_kernel(
    flips, cuts, heads, where_ref, range_ref, queries, starts, places, weight, *refs
):
    parts, (kv, attended, attended_b, logs, branch) = refs[: 2 * len(cuts)], refs[2 * len(cuts) :]
    chip = where_ref[0]
    rows = queries.shape[2]
    half = rows // 2
    count = parts[0].shape[0]
    chips = 2 * count
    for p, first, at, size, b in pieces(cuts, half):
        for k, flip in enumerate(flips[p]):
            part = parts[2 * p + k // count]
            source = chip ^ flip
            block = source if b == 0 else 2 * chips - 1 - source
            place = pl.multiple_of(block * half + at, 16)
            for s in range(2):
                kv[s, pl.ds(place, size), :] = part[k % count, s, first : first + size, :]

    for s in range(2):
        for b in range(2):
            mine = slice(b * half, (b + 1) * half)
            q = queries[s, :, mine, :].reshape(heads * half, HD)
            start = jnp.concatenate([starts[s, mine, :]] * heads, axis=0)
            place = jnp.concatenate([places[s, mine, :]] * heads, axis=0)

            def step(i, state):
                top, total, out = state
                first = pl.multiple_of(i * CHUNK, CHUNK)
                keys = kv[s, pl.ds(first, CHUNK), :HD]
                values = kv[s, pl.ds(first, CHUNK), HD:]
                scores = dot(q, keys, 1, 1) * SCALE
                key_place = first + lax.broadcasted_iota(jnp.int32, scores.shape, 1)
                seen = (key_place >= start) & (key_place <= place)
                scores = jnp.where(seen, scores, NEVER)
                new_top = jnp.maximum(top, jnp.max(scores, axis=1, keepdims=True))
                fade = jnp.exp(top - new_top)
                weights = jnp.exp(scores - new_top)
                total = total * fade + jnp.sum(weights, axis=1, keepdims=True)
                out = out * fade + dot(weights.astype(bf16), values, 1, 0)
                return new_top, total, out

            at = 4 * s + 2 * b
            top, total, out = lax.fori_loop(
                range_ref[at],
                range_ref[at + 1],
                step,
                (
                    jnp.full((heads * half, 1), NEVER, f32),
                    jnp.zeros((heads * half, 1), f32),
                    jnp.zeros((heads * half, HD), f32),
                ),
            )
            out = out / total
            logs[s, b] = top + jnp.log(total)
            attended[s, b] = out
            for h in range(heads):
                attended_b[s, mine, h * HD : (h + 1) * HD] = out[h * half : (h + 1) * half].astype(
                    bf16
                )
        branch[s] = dot(attended_b[s], weight[...], 1, 1)


def attend(where, ranges, queries, starts, places, weight, parts, flips, cuts):
    _, heads, rows, _ = queries.shape
    keys = 2 * parts[0].shape[0] * rows
    half = rows // 2
    return pl.pallas_call(
        functools.partial(attend_kernel, flips, cuts, heads),
        out_shape=[
            jax.ShapeDtypeStruct((2, keys, 2 * HD), bf16),
            jax.ShapeDtypeStruct((2, 2, heads * half, HD), f32),
            jax.ShapeDtypeStruct((2, rows, heads * HD), bf16),
            jax.ShapeDtypeStruct((2, 2, heads * half, 1), f32),
            jax.ShapeDtypeStruct((2, rows, weight.shape[0]), f32),
        ],
        in_specs=[SMEM] * 2 + [VMEM] * (4 + len(parts)),
        out_specs=[VMEM] * 5,
        compiler_params=BIG,
        name="attend",
    )(where, ranges, queries, starts, places, weight, *parts)


def attend_back_kernel(
    heads,
    range_ref,
    branch_own,
    branch_other,
    weight,
    queries,
    kv,
    attended,
    logs,
    starts,
    places,
    cos,
    sin,
    query_out,
    kv_out,
    grads,
    kv_sum,
):
    rows = queries.shape[2]
    half = rows // 2
    chips = kv.shape[1] // rows
    kv_sum[...] = jnp.zeros_like(kv_sum)
    for s, branch in enumerate((branch_own, branch_other)):
        grads[s] = dot(branch[...], weight[...], 1, 0).astype(bf16)
    for s in range(2):
        for b in range(2):
            mine = slice(b * half, (b + 1) * half)
            q = queries[s, :, mine, :].reshape(heads * half, HD)
            start = jnp.concatenate([starts[s, mine, :]] * heads, axis=0)
            place = jnp.concatenate([places[s, mine, :]] * heads, axis=0)
            grad = jnp.concatenate(
                [grads[s, mine, h * HD : (h + 1) * HD] for h in range(heads)], axis=0
            )
            delta = jnp.sum(grad.astype(f32) * attended[s, b], axis=1, keepdims=True)
            log_total = logs[s, b]

            def step(i, query_grad):
                first = pl.multiple_of(i * CHUNK, CHUNK)
                keys = kv[s, pl.ds(first, CHUNK), :HD]
                values = kv[s, pl.ds(first, CHUNK), HD:]
                scores = dot(q, keys, 1, 1) * SCALE
                key_place = first + lax.broadcasted_iota(jnp.int32, scores.shape, 1)
                seen = (key_place >= start) & (key_place <= place)
                weights = jnp.where(seen, jnp.exp(scores - log_total), 0.0)
                weight_grad = dot(grad, values, 1, 1)
                score_grad = (weights * (weight_grad - delta)).astype(bf16)
                kv_sum[s, pl.ds(first, CHUNK), :HD] += dot(score_grad, q, 0, 0)
                kv_sum[s, pl.ds(first, CHUNK), HD:] += dot(weights.astype(bf16), grad, 0, 0)
                return query_grad + dot(score_grad, keys, 1, 0)

            at = 4 * s + 2 * b
            query_grad = lax.fori_loop(
                range_ref[at], range_ref[at + 1], step, jnp.zeros((heads * half, HD), f32)
            )
            cos_b, sin_b = cos[s, mine, :] * SCALE, sin[s, mine, :] * SCALE
            for h in range(heads):
                z = query_grad[h * half : (h + 1) * half]
                z = z * cos_b - pltpu.roll(z, HD // 2, 1) * sin_b
                query_out[s, mine, h * HD : (h + 1) * HD] = z.astype(bf16)

    def give(chip, carry):
        for s in range(2):
            for b in range(2):
                block = chip if b == 0 else 2 * chips - 1 - chip
                place = pl.multiple_of(block * half, half)
                mine = slice(b * half, (b + 1) * half)
                source = kv_sum[s, pl.ds(place, half), :]
                kv_out[chip % 8, chip // 8, s, mine, :HD] = (source[:, :HD] * SCALE).astype(bf16)
                kv_out[chip % 8, chip // 8, s, mine, HD:] = source[:, HD:].astype(bf16)
        return carry

    lax.fori_loop(0, chips, give, 0)


def attend_back(
    ranges, branch_own, branch_other, weight, queries, kv, attended, logs, starts, places, cos, sin
):
    _, heads, rows, _ = queries.shape
    keys = kv.shape[1]
    chips = keys // rows
    return pl.pallas_call(
        functools.partial(attend_back_kernel, heads),
        out_shape=[
            jax.ShapeDtypeStruct((2, rows, heads * HD), bf16),
            jax.ShapeDtypeStruct((8, chips // 8, 2, rows, 2 * HD), bf16),
        ],
        in_specs=[SMEM] + [VMEM] * 11,
        out_specs=[VMEM] * 2,
        scratch_shapes=[
            pltpu.VMEM((2, rows, heads * HD), bf16),
            pltpu.VMEM((2, keys, 2 * HD), f32),
        ],
        compiler_params=BIG,
        name="attend_back",
    )(
        ranges,
        branch_own,
        branch_other,
        weight,
        queries,
        kv,
        attended,
        logs,
        starts,
        places,
        cos,
        sin,
    )


def on_device(
    tokens, cotangent, doc_lengths, norm_attn, w_qkv, b_qkv, w_out, norm_mlp, w_gate, w_up, w_down
):
    ctx_size = lax.axis_size("ctx")
    chip = lax.axis_index("ctx")
    core = lax.axis_index("wshard")
    where = jnp.stack([chip, core]).astype(jnp.int32)
    high = high_bits()
    groups = ctx_size // 8
    tok_dev, width = tokens.shape[1], tokens.shape[2]
    ff = w_gate.shape[1]
    ff_own = ff // 8
    heads = H // KVH
    hq = heads * HD
    rows_dev = w_qkv.shape[0]
    cuts = row_parts(tok_dev)
    half = tok_dev // 2
    flips = [relative_flips(high + order) for order in ORDERS]
    group_flips = relative_flips(group_bits())
    low, middle, upper = member_bits()

    n_gain, n_bias = norm_attn.shape[0], b_qkv.shape[0]
    small = jnp.concatenate([norm_attn, b_qkv, norm_mlp])[None]
    small = jnp.pad(small, ((0, 15), (hq, 2 * HD - small.shape[1])))
    qkv_send = jnp.concatenate([head_columns(w_qkv, 1 - core), small])
    qkv_own = jnp.concatenate([head_columns(w_qkv, core), small])
    token_own, out_grad_b = tokens[0], cotangent[0]
    out_t = w_out.T
    qkv_other = core_swap(qkv_send)
    token_other = core_swap(token_own)
    length_other = core_swap(doc_lengths[0])
    out_other = core_swap(half_of(out_t, 1 - core, 1))
    down_found = gather_list(w_down, group_bits())
    length_pair = jnp.stack([doc_lengths[0], length_other])
    qkv_pair = jnp.stack([qkv_own, qkv_other])[None]
    qkv_pair, w_gate, out_other = together(qkv_pair, w_gate, out_other)
    out_pair = by_core(half_of(out_t, core, 1), out_other, core)
    out_w = lax.all_gather(out_pair, "ctx", axis=0, tiled=False).reshape(width, hq)
    out_grad_all = lax.all_gather(
        after(out_grad_b, out_w), "ctx", axis=0, tiled=True, axis_index_groups=group_lists()
    )
    qkv_pair = gather_relative(qkv_pair, high)
    packed = pack_members(w_gate, w_up)
    qkv_pair, packed, down_found = together(qkv_pair, packed, down_found)
    column_cuts = ((0, hq // 2, rows_dev), (hq // 2, hq, rows_dev), (hq, hq + 2 * HD, rows_dev + 16))
    qkv_parts = [qkv_pair[:, :, :rows, start:stop] for start, stop, rows in column_cuts]
    qkv_parts = doubled(qkv_parts, [order[0] for order in ORDERS])
    down_other = [core_swap(x) for x in down_found]
    qkv_parts = doubled(qkv_parts, [order[1] for order in ORDERS])
    qkv_parts = with_arrived(qkv_parts, [order[2] for order in ORDERS])
    qkv_parts, packed = together(qkv_parts, packed)
    row_cut = rows_dev // 3
    first_rows, later_rows = packed[:, :row_cut], packed[:, row_cut:]
    first_rows = group_exchange(first_rows)

    inner = jnp.arange(tok_dev, dtype=jnp.int32)
    blocks = jnp.where(inner < half, chip, 2 * ctx_size - 1 - chip)
    places = (blocks * half + inner % half).astype(jnp.int32)
    ends = jnp.cumsum(length_pair, axis=1)
    passed = ends[:, None, :] <= places[None, :, None]
    starts = jnp.sum(jnp.where(passed, length_pair[:, None, :], 0), axis=2)
    places = jnp.broadcast_to(places[None], starts.shape)
    frequency = ROPE_BASE ** (-jnp.arange(HD // 2, dtype=f32) * 2.0 / HD)
    angles = (places - starts).astype(f32)[..., None] * frequency
    cos_half, sin_half = jnp.cos(angles), jnp.sin(angles)
    cos = jnp.concatenate([cos_half, cos_half], axis=-1)
    sin = jnp.concatenate([-sin_half, sin_half], axis=-1)
    first = jnp.min(starts.reshape(2, 2, half), axis=2) // CHUNK
    last = jnp.max(places.reshape(2, 2, half), axis=2) // CHUNK + 1
    ranges = jnp.stack([first, last], axis=-1).reshape(-1).astype(jnp.int32)
    starts, places = starts[..., None], places[..., None]

    qkv_w, small_all = order_weights(qkv_parts, flips, where)
    qkv_w = qkv_w.reshape(width, hq + 2 * HD)
    small_all = small_all.reshape(2 * ctx_size, 2 * HD)
    gain_one = small_all[:, :n_gain].reshape(1, -1)
    bias = small_all[:, n_gain : n_gain + n_bias].reshape(1, -1)
    gain_two = small_all[:, n_gain + n_bias : 2 * n_gain + n_bias].reshape(1, -1)
    bias = head_columns(bias, core)
    normed_one, queries, kv_own = project(token_own, token_other, gain_one, qkv_w, bias, cos, sin)
    kv_own = gather_relative(kv_own[None], high)
    kv_own, first_rows = together(kv_own, first_rows)

    kv_parts = [kv_own[:, :, start:stop] for start, stop in cuts]
    for step in range(2):
        kv_parts = doubled(kv_parts, [order[step] for order in ORDERS])
    down = order_rows([x[None] for x in down_found], [x[None] for x in down_other], group_flips, where)
    down = down.reshape(ff_own, width)
    kv_parts = with_arrived(kv_parts, [order[2] for order in ORDERS])
    kv_parts, down, later_rows, first_rows = together(kv_parts, down, later_rows, first_rows)
    later_rows = group_exchange(later_rows)
    kv, attended, attended_b, logs, branch = attend(
        where, ranges, queries, starts, places, out_w, kv_parts, flips, cuts
    )
    branch_other = core_swap(branch[1])
    branch_other, later_rows, first_rows = together(branch_other, later_rows, first_rows)
    packed = jnp.concatenate([first_rows, later_rows], axis=1)
    shares = ((0, 4), (4, 8))
    packed_found = [gather_list(packed[:4], group_bits())]
    packed_other = core_swap(packed)
    inputs = token_own.astype(f32)
    hidden_res = inputs + branch[0] + branch_other
    scale_two = lax.rsqrt(jnp.mean(hidden_res * hidden_res, axis=-1, keepdims=True) + EPSILON)
    normed_two = (hidden_res * scale_two * gain_two).astype(bf16)

    group_orders = ((upper, middle, low), (upper, low, middle))
    group_cuts = ((0, half), (half, tok_dev))
    token_parts = gather_relative(normed_two[None], (upper,))
    token_parts, packed, packed_found = together(token_parts, packed, packed_found)
    token_parts = [token_parts[:, start:stop] for start, stop in group_cuts]
    token_parts = doubled(token_parts, [order[1] for order in group_orders])
    packed_found.append(gather_list(packed[4:], group_bits()))
    token_parts, out_grad_all = together(token_parts, out_grad_all)
    token_parts = with_arrived(token_parts, [order[2] for order in group_orders])
    token_parts, packed_found = together(token_parts, packed_found)
    token_flips = [relative_flips(order) for order in group_orders]
    normed_all = order_tokens(token_parts, token_flips, group_cuts, groups, where)
    normed_all = normed_all.reshape(8 * tok_dev, width)

    sources, loads = [packed, packed_other], [(0, 0, 0), (0, 1, 0)]
    for found, (first, _) in zip(packed_found, shares):
        for piece, flip in list(zip(found, group_flips))[1:]:
            sources.extend([piece, core_swap(piece)])
            loads.extend([(flip, 0, first), (flip, 1, first)])
    if rows_dev % 16:
        own, other = [], []
        for flip in group_flips:
            for core_flip, side in enumerate((own, other)):
                found = [x for x, load in zip(sources, loads) if load[:2] == (flip, core_flip)]
                side.append(jnp.concatenate(found))
        sources, loads = [order_rows(own, other, group_flips, where).reshape(width, -1)], [(None, 0, 0)]
    out_grad = out_grad_b.astype(f32)
    pre_grad, activated, normed_grad_part = mlp(
        where, groups, normed_all, out_grad_all, down, sources, loads
    )

    normed_grad_part = normed_grad_part.reshape(2, 2, 2, tok_dev, width)
    scatter = Scatter(
        [normed_grad_part[:, :, :, start:stop] for start, stop in group_cuts], (upper, middle, low)
    )
    bits = [order[2] for order in group_orders]
    kept, sent = scatter.split(bits)
    gate_keep, gate_send = gate_up_grads(normed_all, after(pre_grad, *sent), 0, rows_dev, where)
    gate_arrived = core_swap(gate_send)
    branch_part = dot(after(activated, gate_send), down, 1, 0).astype(bf16)
    scatter.step(bits, kept, sent)
    scatter.parts, gate_arrived, branch_part = together(scatter.parts, gate_arrived, branch_part)

    def of_cores(keep, arrived):
        total = (keep.astype(f32) + arrived.astype(f32)).astype(bf16)
        return total.reshape(8, groups, rows_dev, -1)

    def of_group(total):
        return sum_over(total, 1, tuple(reversed(group_bits()))).astype(bf16)

    bits = [order[1] for order in group_orders]
    kept, sent = scatter.split(bits)
    gate_total = of_cores(gate_keep, gate_arrived)
    scatter.step(bits, kept, sent)
    scatter.parts, gate_total, pre_grad = together(scatter.parts, gate_total, pre_grad)

    kept, sent = scatter.split((upper, upper))
    grad_gate = of_group(gate_total)
    up_keep, up_send = gate_up_grads(normed_all, after(pre_grad, *sent), 1, rows_dev, where)
    branch_part = branch_part.reshape(2, 2, 2, tok_dev, width)
    branch_sums = Scatter(
        [branch_part[:, :, :, start:stop] for start, stop in group_cuts], (upper, middle, low)
    )
    bits = [order[2] for order in group_orders]
    branch_kept, branch_sent = branch_sums.split(bits)
    scatter.step((upper, upper), kept, sent)
    branch_arrived = [chip_swap(x, 1 << bit) for x, bit in zip(branch_sent, bits)]
    scatter.parts, grad_gate, up_send = together(scatter.parts, grad_gate, up_send)
    grad_gate = group_exchange(grad_gate)
    up_arrived = core_swap(up_send)
    normed_two_grad = jnp.concatenate(scatter.parts)
    gain_two_grad = jnp.sum(normed_two_grad * hidden_res * scale_two, axis=0)
    hidden_grad = out_grad + rms_back(normed_two_grad, hidden_res, scale_two, gain_two)

    falling = tuple(reversed(group_bits()))
    def weight_parts(x):
        return x.astype(bf16).reshape(ctx_size // 8, 8, 2, rows_dev, x.shape[1])

    branch_own = hidden_grad.astype(bf16)
    branch_other = core_swap(branch_own)
    branch_own, branch_other, up_arrived, branch_arrived = together(
        branch_own, branch_other, up_arrived, branch_arrived
    )
    grad_up = of_group(of_cores(up_keep, up_arrived))
    project_grad_q, kv_grad = attend_back(
        ranges, branch_own, branch_other, out_w, queries, kv, attended, logs, starts, places, cos, sin
    )
    (kv_grad, project_grad_q), grad_gate, grad_up, activated = together(
        (kv_grad, project_grad_q), grad_gate, grad_up, activated
    )
    kv_sum = cube_exchange(kv_grad)
    down_keep, down_send = down_grads(activated, out_grad_all, groups, where)
    branch_grad = jnp.concatenate([branch_own, branch_other])
    normed_one = normed_one.reshape(-1, width)
    project_grad_q = project_grad_q.reshape(-1, hq)
    grad_out_part = weight_parts(dot(branch_grad, attended_b.reshape(-1, hq), 0, 0))
    grad_q_part = weight_parts(dot(normed_one, project_grad_q, 0, 0))
    wide_part = jnp.concatenate([grad_q_part, grad_out_part], axis=-1)
    names = tuple(reversed(high)) + (2, 1, 0)
    wide_part = wide_part.reshape((2,) * len(names) + wide_part.shape[2:])
    third = 2 * hq // 3
    scatter = Scatter([wide_part[..., i * third : (i + 1) * third] for i in range(3)], names)
    bits = [order[0] for order in ORDERS]
    kept, sent = scatter.split(bits)
    arrived = [chip_swap(x, 1 << bit) for x, bit in zip(sent, bits)]
    kv_sum, arrived, down_send, branch_arrived = together(
        kv_sum, arrived, down_send, branch_arrived
    )

    kv_sum = jnp.sum(kv_sum.astype(f32), axis=0).astype(bf16)
    kv_sum, grad_up = together(kv_sum, grad_up)
    kv_sum = sum_over_high(kv_sum, high)
    down_arrived = core_swap(down_send)
    grad_up = group_exchange(grad_up)
    key_pre = kv_sum[..., :HD]
    key_pre = key_pre * cos - jnp.roll(key_pre, HD // 2, axis=-1) * sin
    project_grad_kv = jnp.concatenate([key_pre, kv_sum[..., HD:]], axis=-1).astype(bf16)
    project_grad_kv = project_grad_kv.reshape(-1, 2 * HD)
    grad_kv = weight_parts(dot(normed_one, project_grad_kv, 0, 0)).swapaxes(0, 1)
    project_grad = jnp.concatenate([project_grad_q, project_grad_kv], axis=1)
    normed_one_grad = dot(project_grad, qkv_w, 1, 1)
    normed_one_grad = normed_one_grad[:tok_dev] + core_swap(normed_one_grad[tok_dev:])
    scatter.add(kept, arrived)
    branch_sums.add(branch_kept, branch_arrived)
    branch_sums.step([order[1] for order in group_orders])
    down_sum = (down_keep.astype(f32) + down_arrived.astype(f32)).astype(bf16)
    grad_kv, grad_up, scatter.parts, branch_sums.parts, down_sum, normed_one_grad = together(
        grad_kv, grad_up, scatter.parts, branch_sums.parts, down_sum, normed_one_grad
    )
    grad_kv = cube_exchange(grad_kv)
    branch_sums.parts = [jnp.concatenate(branch_sums.parts, axis=-2)]
    branch_sums.step((upper,))
    scatter.step([order[1] for order in ORDERS])
    scatter.step([order[2] for order in ORDERS])
    scatter.parts = [jnp.concatenate(scatter.parts, axis=-1)]
    scale_one = lax.rsqrt(jnp.mean(inputs * inputs, axis=-1, keepdims=True) + EPSILON)
    gain_one_grad = jnp.sum(normed_one_grad * inputs * scale_one, axis=0)
    input_grad = hidden_grad + rms_back(normed_one_grad, inputs, scale_one, gain_one)

    def whole_columns(x):
        return jnp.concatenate(
            [
                x[0, :, :hq],
                x[1, :, :hq],
                x[0, :, hq : hq + HD],
                x[1, :, hq : hq + HD],
                x[0, :, hq + HD : hq + 2 * HD],
                x[1, :, hq + HD : hq + 2 * HD],
            ],
            axis=1,
        )

    bias_grad = jnp.sum(project_grad.astype(f32), axis=0, keepdims=True)
    zeros = jnp.zeros_like(bias_grad)
    bias_full = whole_columns(
        jnp.stack([jnp.where(core == 0, bias_grad, zeros), jnp.where(core == 0, zeros, bias_grad)])
    )[0]
    qk_width = (H + KVH) * HD
    sums = jnp.concatenate(
        [
            x.reshape(ctx_size, 1, -1)
            for x in (gain_one_grad, gain_two_grad, bias_full[:qk_width], bias_full[qk_width:])
        ],
        axis=2,
    )
    grad_kv, scatter.parts, branch_sums.parts, sums, down_sum = together(
        grad_kv, scatter.parts, branch_sums.parts, sums, down_sum
    )
    sums = lax.all_to_all(sums, "ctx", split_axis=0, concat_axis=0, tiled=True)
    grad_kv = jnp.sum(grad_kv.astype(f32), axis=0).astype(bf16)
    grad_kv = sum_over_high(grad_kv, high)
    grad_down = sum_over(down_sum, 0, falling)
    for bit in reversed(high):
        scatter.step((bit,))
    scattered = scatter.parts[0]
    sums = jnp.sum(sums, axis=0)
    sums = (sums + core_swap(sums))[0]
    output = (hidden_res + branch_sums.parts[0]).astype(bf16)

    grad_gate, grad_up = unpack_members(grad_gate, grad_up, ff)
    chip_grad = jnp.concatenate([scattered[..., :hq], grad_kv, scattered[..., hq:]], axis=-1)

    def pick(x, which):
        return lax.dynamic_index_in_dim(x, which, 0, keepdims=False)

    pair = by_core(pick(chip_grad, core), core_swap(pick(chip_grad, 1 - core)), core)
    grad_qkv = whole_columns(pair)
    grad_out = pair[:, :, hq + 2 * HD :].transpose(1, 0, 2).reshape(-1, 2 * hq).T

    def owned(start, size):
        return lax.dynamic_slice_in_dim(sums, start + core * (size // 2), size // 2, 0)

    own_width, own_qk, own_v = width // ctx_size, qk_width // ctx_size, KVH * HD // ctx_size
    return (
        output[None],
        input_grad[None],
        owned(0, own_width),
        grad_qkv,
        owned(2 * own_width, own_qk),
        owned(2 * own_width + own_qk, own_v),
        grad_out,
        owned(own_width, own_width),
        grad_gate,
        grad_up,
        grad_down,
    )


def solution(mesh):
    whole = ("ctx", "wshard")
    rows, columns, flat = P(whole, None), P(None, whole), P(whole)
    tokens = P("wshard", "ctx", None)
    return jax.shard_map(
        on_device,
        mesh=mesh,
        in_specs=(tokens, tokens, P("wshard", None), flat, rows, flat, columns, flat, rows, rows, rows),
        out_specs=(tokens, tokens, flat, rows, flat, flat, columns, flat, rows, rows, rows),
        check_vma=False,
    )
```

```python
import functools
import math

import jax
import jax.numpy as jnp
from jax import lax
from jax.experimental import pallas as pl
from jax.experimental.pallas import tpu as pltpu
from jax.sharding import PartitionSpec as P

H = 12
KVH = 2
HD = 128
EPSILON = 1e-06
ROPE_BASE = 1000000.0
ORDERS = ((0, 1, 2), (1, 2, 0), (2, 0, 1))
CHUNK = 256
NEVER = -1e30
SCALE = 1.0 / math.sqrt(HD)
bf16 = jnp.bfloat16
f32 = jnp.float32
VMEM = pl.BlockSpec(memory_space=pltpu.VMEM)
SMEM = pl.BlockSpec(memory_space=pltpu.SMEM)
BIG = pltpu.CompilerParams(vmem_limit_bytes=56 * 1024 * 1024)


def after(x, *others):
    return together(x, *others)[0]


def together(*groups):
    flat, tree = jax.tree.flatten(groups)
    return jax.tree.unflatten(tree, lax.optimization_barrier(flat))


def core_swap(x):
    return lax.ppermute(x, "wshard", [(0, 1), (1, 0)])


def chip_swap(x, flip):
    count = lax.axis_size("ctx")
    return lax.ppermute(x, "ctx", [(i, i ^ flip) for i in range(count)])


def cubes():
    count = lax.axis_size("ctx")
    return [list(range(i, i + 8)) for i in range(0, count, 8)]


def cube_exchange(x):
    return lax.all_to_all(
        x, "ctx", split_axis=0, concat_axis=0, tiled=True, axis_index_groups=cubes()
    )


def group_bits():
    return tuple(range(lax.axis_size("ctx").bit_length() - 4))


def member_bits():
    first = len(group_bits())
    return (first, first + 1, first + 2)


def group_lists():
    groups = lax.axis_size("ctx") // 8
    return [[g + groups * m for m in range(8)] for g in range(groups)]


def group_exchange(x):
    return lax.all_to_all(
        x, "ctx", split_axis=0, concat_axis=0, tiled=True, axis_index_groups=group_lists()
    )


def high_bits():
    return tuple(range(3, lax.axis_size("ctx").bit_length() - 1))


def my_bit(bit):
    return (lax.axis_index("ctx") >> bit) & 1


def gather_relative(x, bits):
    for bit in bits:
        x = jnp.concatenate([x, chip_swap(x, 1 << bit)], axis=0)
    return x


def gather_list(x, bits):
    found = [x]
    for bit in bits:
        found = found + [chip_swap(y, 1 << bit) for y in found]
    return found


def relative_flips(bits):
    flips = [0]
    for bit in bits:
        flips = flips + [f ^ (1 << bit) for f in flips]
    return flips


def sum_over(x, axis, bits):
    for at, bit in enumerate(bits):
        shape = x.shape
        x = x.reshape(shape[:axis] + (2, shape[axis] // 2) + shape[axis + 1 :])
        keep = lax.dynamic_index_in_dim(x, my_bit(bit), axis, keepdims=False)
        send = lax.dynamic_index_in_dim(x, 1 - my_bit(bit), axis, keepdims=False)
        x = keep.astype(f32) + chip_swap(send.astype(bf16), 1 << bit).astype(f32)
        if at < len(bits) - 1:
            x = x.astype(bf16)
    return jnp.squeeze(x, axis).astype(f32)


def sum_over_high(x, high):
    return sum_over(x, 0, tuple(reversed(high)))


def row_parts(rows):
    third = rows * 3 // 8
    return ((0, third), (third, 2 * third), (2 * third, rows))


def doubled(parts, bits):
    return [jnp.concatenate([x, chip_swap(x, 1 << bit)]) for x, bit in zip(parts, bits)]


def with_arrived(parts, bits):
    found = []
    for x, bit in zip(parts, bits):
        found.extend([x, chip_swap(x, 1 << bit)])
    return found


def both_halves(x, layout, bit):
    axis = layout.index(bit)
    keep = lax.dynamic_index_in_dim(x, my_bit(bit), axis, keepdims=False)
    send = lax.dynamic_index_in_dim(x, 1 - my_bit(bit), axis, keepdims=False)
    return keep, send


class Scatter:
    def __init__(self, parts, layout):
        self.parts = list(parts)
        self.layouts = [list(layout) for _ in self.parts]

    def split(self, bits):
        pairs = [both_halves(x, l, b) for x, l, b in zip(self.parts, self.layouts, bits)]
        for layout, bit in zip(self.layouts, bits):
            layout.remove(bit)
        return [k for k, _ in pairs], [s.astype(bf16) for _, s in pairs]

    def step(self, bits, kept=None, sent=None):
        if kept is None:
            kept, sent = self.split(bits)
        self.add(kept, [chip_swap(x, 1 << bit) for x, bit in zip(sent, bits)])

    def add(self, kept, arrived):
        self.parts = [k.astype(f32) + a.astype(f32) for k, a in zip(kept, arrived)]
        if self.layouts[0]:
            self.parts = [x.astype(bf16) for x in self.parts]


def dot(left, right, left_axis, right_axis):
    return lax.dot_general(
        left, right, (((left_axis,), (right_axis,)), ((), ())), preferred_element_type=f32
    )


def rms_back(grad_in, values, scale_rows, gain_row):
    weighted = grad_in * gain_row
    return scale_rows * weighted - values * scale_rows**3 * jnp.mean(
        weighted * values, axis=-1, keepdims=True
    )


def half_of(x, which, axis):
    size = x.shape[axis] // 2
    return lax.dynamic_slice_in_dim(x, which * size, size, axis)


def head_columns(x, core):
    q_width, kv_width = H * HD, KVH * HD
    return jnp.concatenate(
        [
            half_of(x[:, :q_width], core, 1),
            half_of(x[:, q_width : q_width + kv_width], core, 1),
            half_of(x[:, q_width + kv_width :], core, 1),
        ],
        axis=1,
    )


def by_core(mine, other, core):
    return jnp.stack([jnp.where(core == 0, mine, other), jnp.where(core == 0, other, mine)])


def order_weights_kernel(flips, extra_rows, where_ref, *refs):
    parts, out = refs[: 2 * len(flips)], refs[2 * len(flips)]
    chip, core = where_ref[0], where_ref[1]
    count, rows = parts[0].shape[0], out.shape[2]
    at = 0
    for p, part_flips in enumerate(flips):
        columns = parts[2 * p].shape[3]
        for k, flip in enumerate(part_flips):
            part = parts[2 * p + k // count]
            for h in range(2):
                out[chip ^ flip, core ^ h, :, at : at + columns] = part[k % count, h, :rows]
                if extra_rows and p == len(flips) - 1:
                    extra = part[k % count, h, rows:].astype(f32)[:1]
                    refs[-1][chip ^ flip, core ^ h] = extra
        at += columns


def order_weights(parts, flips, where):
    count, _, rows, _ = parts[0].shape
    columns = sum(p.shape[3] for p in parts[::2])
    extra = parts[-1].shape[2] > rows
    shapes = [jax.ShapeDtypeStruct((2 * count, 2, rows, columns), bf16)]
    if extra:
        shapes.append(jax.ShapeDtypeStruct((2 * count, 2, 1, parts[-1].shape[3]), f32))
    return pl.pallas_call(
        functools.partial(order_weights_kernel, flips, extra),
        out_shape=shapes,
        in_specs=[SMEM] + [VMEM] * len(parts),
        out_specs=[VMEM] * len(shapes),
        compiler_params=BIG,
        name="order_weights",
    )(where, *parts)


def order_rows_kernel(flips, where_ref, *refs):
    out = refs[-1]
    chip, core = where_ref[0], where_ref[1]
    group = chip % len(flips)
    for k, flip in enumerate(flips):
        out[:, group ^ flip, core] = refs[k][...]
        out[:, group ^ flip, 1 - core] = refs[len(flips) + k][...]


def order_rows(own, other, flips, where):
    members, rows, columns = own[0].shape
    groups = len(own)
    tile = columns // 2 if columns % 256 == 0 else columns
    source = pl.BlockSpec((1, rows, tile), lambda m, n: (m, 0, n))
    return pl.pallas_call(
        functools.partial(order_rows_kernel, flips),
        grid=(members, columns // tile),
        out_shape=jax.ShapeDtypeStruct((members, groups, 2, rows, columns), bf16),
        in_specs=[SMEM] + [source] * (2 * groups),
        out_specs=pl.BlockSpec((1, groups, 2, rows, tile), lambda m, n: (m, 0, 0, 0, n)),
        compiler_params=BIG,
        name="order_rows",
    )(where, *own, *other)


def order_tokens_kernel(flips, cuts, groups, where_ref, *refs):
    out = refs[-1]
    member = where_ref[0] // groups
    for p, (start, stop) in enumerate(cuts):
        for k, flip in enumerate(flips[p]):
            half = refs[2 * p + k // 4]
            out[member ^ (flip // groups), start:stop, :] = half[k % 4]


def order_tokens(halves, flips, cuts, groups, where):
    rows, width = cuts[-1][1], halves[0].shape[2]
    return pl.pallas_call(
        functools.partial(order_tokens_kernel, flips, cuts, groups),
        out_shape=jax.ShapeDtypeStruct((8, rows, width), bf16),
        in_specs=[SMEM] + [VMEM] * len(halves),
        out_specs=VMEM,
        compiler_params=BIG,
        name="order_tokens",
    )(where, *halves)


def padded(ff_own):
    return -(-ff_own // 128) * 128


def pack_members_kernel(gate, up, out):
    own, wide = gate.shape[1] // 8, out.shape[2] // 2
    for m in range(8):
        for at, source in ((0, gate), (wide, up)):
            out[m, :, at : at + own] = source[:, m * own : (m + 1) * own]
            out[m, :, at + own : at + wide] = jnp.zeros((out.shape[1], wide - own), bf16)


def pack_members(gate, up):
    rows, ff = gate.shape
    return pl.pallas_call(
        pack_members_kernel,
        out_shape=jax.ShapeDtypeStruct((8, rows, 2 * padded(ff // 8)), bf16),
        in_specs=[VMEM] * 2,
        out_specs=VMEM,
        compiler_params=BIG,
        name="pack_members",
    )(gate, up)


def unpack_members_kernel(packed_gate, packed_up, gate, up):
    own = gate.shape[1] // 8
    for m in range(8):
        for packed, target in ((packed_gate, gate), (packed_up, up)):
            target[:, m * own : (m + 1) * own] = packed[m, :, :own].astype(f32)


def unpack_members(packed_gate, packed_up, ff):
    rows = packed_gate.shape[1]
    return pl.pallas_call(
        unpack_members_kernel,
        out_shape=[jax.ShapeDtypeStruct((rows, ff), f32)] * 2,
        in_specs=[VMEM] * 2,
        out_specs=[VMEM] * 2,
        compiler_params=BIG,
        name="unpack_members",
    )(packed_gate, packed_up)


def mlp_kernel(loads, groups, where_ref, normed, out_grad, down, *refs):
    sources = refs[: len(loads)]
    pre_grad, activated, normed_grad, gate_up, arrived = refs[len(loads) :]
    chip, core = where_ref[0], where_ref[1]

    @pl.when(pl.program_id(0) == 0)
    def _():
        copies = []
        for source, (flip, other, first) in zip(sources, loads):
            if flip is None:
                copies.append(pltpu.make_async_copy(source, gate_up, arrived.at[len(copies)]))
                continue
            rows = source.shape[1]
            for i in range(source.shape[0]):
                device = 2 * ((first + i) * groups + (chip % groups ^ flip)) + (core ^ other)
                target = gate_up.at[pl.ds(pl.multiple_of(device * rows, 16), rows), :]
                copies.append(pltpu.make_async_copy(source.at[i], target, arrived.at[len(copies)]))
        for copy in copies:
            copy.start()
        for copy in copies:
            copy.wait()

    ff_own = down.shape[0]
    wide = gate_up.shape[1] // 2
    gates, ups = slice(0, ff_own), slice(wide, wide + ff_own)
    n = normed[...]
    gate = dot(n, gate_up[:, gates], 1, 0)
    up = dot(n, gate_up[:, ups], 1, 0)
    act_grad = dot(out_grad[...], down[...], 1, 1)
    sig = jax.nn.sigmoid(gate)
    act = gate * sig
    activated[...] = (act * up).astype(bf16)
    if wide > ff_own:
        gap = jnp.zeros((n.shape[0], wide - ff_own), bf16)
        pre_grad[:, ff_own:wide] = gap
        pre_grad[:, wide + ff_own :] = gap
    pre_grad[:, gates] = (act_grad * up * sig * (1.0 + gate * (1.0 - sig))).astype(bf16)
    pre_grad[:, ups] = (act_grad * act).astype(bf16)
    normed_grad[...] = dot(pre_grad[...], gate_up[...], 1, 1).astype(bf16)


def mlp(where, groups, normed, out_grad, down, sources, loads, tile=256):
    rows, width = normed.shape
    ff_own, wide = down.shape[0], sources[0].shape[-1]
    count = sum(1 if flip is None else x.shape[0] for x, (flip, _, _) in zip(sources, loads))

    def by_rows(columns):
        return pl.BlockSpec((tile, columns), lambda i: (i, 0))

    return pl.pallas_call(
        functools.partial(mlp_kernel, loads, groups),
        grid=(rows // tile,),
        out_shape=[
            jax.ShapeDtypeStruct((rows, wide), bf16),
            jax.ShapeDtypeStruct((rows, ff_own), bf16),
            jax.ShapeDtypeStruct((rows, width), bf16),
        ],
        in_specs=[
            SMEM,
            by_rows(width),
            by_rows(width),
            pl.BlockSpec(down.shape, lambda i: (0, 0), pipeline_mode=pl.Buffered(1)),
        ]
        + [pl.BlockSpec(memory_space=pl.ANY)] * len(sources),
        out_specs=[by_rows(wide), by_rows(ff_own), by_rows(width)],
        scratch_shapes=[pltpu.VMEM((width, wide), bf16), pltpu.SemaphoreType.DMA((count,))],
        compiler_params=BIG,
        name="mlp",
    )(where, normed, out_grad, down, *sources)


def gate_up_grads_kernel(rows_dev, where_ref, normed, pre_grad, keep, send):
    grads = dot(normed[...], pre_grad[...], 0, 0)
    core = where_ref[1]
    for i in range(keep.shape[0]):
        low = grads[2 * i * rows_dev : (2 * i + 1) * rows_dev].astype(bf16)
        upper = grads[(2 * i + 1) * rows_dev : (2 * i + 2) * rows_dev].astype(bf16)
        keep[i] = jnp.where(core == 0, low, upper)
        send[i] = jnp.where(core == 0, upper, low)


def gate_up_grads(normed, pre_grad, side, rows_dev, where, tile=384):
    rows, width = normed.shape
    wide = pre_grad.shape[1] // 2
    chips, step = width // (2 * rows_dev), tile // (2 * rows_dev)
    result = pl.BlockSpec((step, rows_dev, wide), lambda i: (i, 0, 0))
    return pl.pallas_call(
        functools.partial(gate_up_grads_kernel, rows_dev),
        grid=(width // tile,),
        out_shape=[jax.ShapeDtypeStruct((chips, rows_dev, wide), bf16)] * 2,
        in_specs=[
            SMEM,
            pl.BlockSpec((rows, tile), lambda i: (0, i)),
            pl.BlockSpec((rows, wide), lambda i: (0, side), pipeline_mode=pl.Buffered(1)),
        ],
        out_specs=[result] * 2,
        compiler_params=BIG,
        name="gate_up_grads",
    )(where, normed, pre_grad)


def down_grads_kernel(where_ref, activated, out_grad, keep, send):
    grads = dot(activated[...], out_grad[...], 0, 0)
    core = where_ref[1]
    rows_dev = keep.shape[1]
    for i in range(keep.shape[0]):
        low = grads[2 * i * rows_dev : (2 * i + 1) * rows_dev].astype(bf16)
        upper = grads[(2 * i + 1) * rows_dev : (2 * i + 2) * rows_dev].astype(bf16)
        keep[i] = jnp.where(core == 0, low, upper)
        send[i] = jnp.where(core == 0, upper, low)


def down_grads(activated, out_grad, groups, where, tile=512):
    rows, ff_own = activated.shape
    width = out_grad.shape[1]
    rows_dev = ff_own // (2 * groups)
    result = pl.BlockSpec((groups, rows_dev, tile), lambda i: (0, 0, i))
    return pl.pallas_call(
        down_grads_kernel,
        grid=(width // tile,),
        out_shape=[jax.ShapeDtypeStruct((groups, rows_dev, width), bf16)] * 2,
        in_specs=[
            SMEM,
            pl.BlockSpec((rows, ff_own), lambda i: (0, 0), pipeline_mode=pl.Buffered(1)),
            pl.BlockSpec((rows, tile), lambda i: (0, i)),
        ],
        out_specs=[result] * 2,
        compiler_params=BIG,
        name="down_grads",
    )(where, activated, out_grad)


def project_streams(heads, own, other, gain, weight, bias, cos, sin, normed, queries, kv):
    hq = heads * HD
    for s, tokens in enumerate((own, other)):
        x = tokens[...].astype(f32)
        scale = lax.rsqrt(jnp.mean(x * x, axis=-1, keepdims=True) + EPSILON)
        n = (x * scale * gain).astype(bf16)
        normed[s] = n
        cos_s, sin_s = cos[s], sin[s]
        project = dot(n, weight[...], 1, 0) + bias

        def turn(z):
            return z * cos_s + pltpu.roll(z, HD // 2, 1) * sin_s

        for h in range(heads):
            queries[s, h] = turn(project[:, h * HD : (h + 1) * HD]).astype(bf16)
        kv[s, :, :HD] = turn(project[:, hq : hq + HD]).astype(bf16)
        kv[s, :, HD:] = project[:, hq + HD :].astype(bf16)


def project_kernel(heads, own, other, gain, weight, bias, cos, sin, normed, queries, kv):
    project_streams(
        heads, own, other, gain[...], weight, bias[...], cos, sin, normed, queries, kv
    )


def project(own, other, gain, weight, bias, cos, sin):
    rows, width = own.shape
    heads = H // KVH
    return pl.pallas_call(
        functools.partial(project_kernel, heads),
        out_shape=[
            jax.ShapeDtypeStruct((2, rows, width), bf16),
            jax.ShapeDtypeStruct((2, heads, rows, HD), bf16),
            jax.ShapeDtypeStruct((2, rows, 2 * HD), bf16),
        ],
        in_specs=[VMEM] * 7,
        out_specs=[VMEM] * 3,
        compiler_params=BIG,
        name="project",
    )(own, other, gain, weight, bias, cos, sin)


def order_project_kernel(
    heads, flips, n_gain, n_bias, rows, where_ref, own, other, cos, sin, *refs
):
    parts = refs[: 2 * len(flips)]
    normed, queries, kv, weight, gains, small, line = refs[2 * len(flips) :]
    chip, core = where_ref[0], where_ref[1]
    count = parts[0].shape[0]
    at = 0
    for p, part_flips in enumerate(flips):
        columns = parts[2 * p].shape[3]
        for k, flip in enumerate(part_flips):
            part = parts[2 * p + k // count]
            for h in range(2):
                device = 2 * (chip ^ flip) + (core ^ h)
                first = pl.multiple_of(device * rows, 16)
                weight[pl.ds(first, rows), at : at + columns] = part[k % count, h, :rows]
                if p == len(flips) - 1:
                    small[pl.ds(device, 1), :] = part[k % count, h, rows:].astype(f32)[:1]
        at += columns
    devices = small.shape[0]
    total = devices * n_bias
    for d in range(devices):
        row = small[d : d + 1, :]
        gains[0:1, d * n_gain : (d + 1) * n_gain] = row[:, :n_gain]
        line[1:2, d * n_bias : (d + 1) * n_bias] = row[:, n_gain : n_gain + n_bias]
        gains[1:2, d * n_gain : (d + 1) * n_gain] = row[
            :, n_gain + n_bias : 2 * n_gain + n_bias
        ]
    hq, v = heads * HD, 2 * heads * HD + 2 * HD
    bias = jnp.where(
        core == 0,
        jnp.concatenate(
            [line[1:2, :hq], line[1:2, 2 * hq : 2 * hq + HD], line[1:2, v : v + HD]], axis=1
        ),
        jnp.concatenate(
            [line[1:2, hq : 2 * hq], line[1:2, 2 * hq + HD : v], line[1:2, v + HD : total]], axis=1
        ),
    )
    gain = gains[0:1, :]
    project_streams(heads, own, other, gain, weight, bias, cos, sin, normed, queries, kv)


def order_project(where, own, other, cos, sin, parts, flips, n_gain, n_bias, rows):
    tokens, width = own.shape
    heads = H // KVH
    columns = sum(p.shape[3] for p in parts[::2])
    devices = 4 * parts[0].shape[0]
    return pl.pallas_call(
        functools.partial(order_project_kernel, heads, flips, n_gain, n_bias, rows),
        out_shape=[
            jax.ShapeDtypeStruct((2, tokens, width), bf16),
            jax.ShapeDtypeStruct((2, heads, tokens, HD), bf16),
            jax.ShapeDtypeStruct((2, tokens, 2 * HD), bf16),
            jax.ShapeDtypeStruct((width, columns), bf16),
            jax.ShapeDtypeStruct((2, width), f32),
        ],
        in_specs=[SMEM] + [VMEM] * (4 + len(parts)),
        out_specs=[VMEM] * 5,
        scratch_shapes=[
            pltpu.VMEM((devices, parts[-1].shape[3]), f32),
            pltpu.VMEM((8, devices * n_bias), f32),
        ],
        compiler_params=BIG,
        name="order_project",
    )(where, own, other, cos, sin, *parts)


def pieces(cuts, half):
    found = []
    for p, (start, stop) in enumerate(cuts):
        for b in range(2):
            low, high = max(start, b * half), min(stop, (b + 1) * half)
            if low < high:
                found.append((p, low - start, low - b * half, high - low, b))
    return found


def attend_kernel(
    flips, cuts, heads, where_ref, range_ref, queries, starts, places, weight, *refs
):
    parts, (kv, attended, attended_b, logs, branch) = refs[: 2 * len(cuts)], refs[2 * len(cuts) :]
    chip = where_ref[0]
    rows = queries.shape[2]
    half = rows // 2
    count = parts[0].shape[0]
    chips = 2 * count
    for p, first, at, size, b in pieces(cuts, half):
        for k, flip in enumerate(flips[p]):
            part = parts[2 * p + k // count]
            source = chip ^ flip
            block = source if b == 0 else 2 * chips - 1 - source
            place = pl.multiple_of(block * half + at, 16)
            for s in range(2):
                kv[s, pl.ds(place, size), :] = part[k % count, s, first : first + size, :]

    for s in range(2):
        for b in range(2):
            mine = slice(b * half, (b + 1) * half)
            q = queries[s, :, mine, :].reshape(heads * half, HD)
            start = jnp.concatenate([starts[s, mine, :]] * heads, axis=0)
            place = jnp.concatenate([places[s, mine, :]] * heads, axis=0)

            def step(i, state):
                top, total, out = state
                first = pl.multiple_of(i * CHUNK, CHUNK)
                keys = kv[s, pl.ds(first, CHUNK), :HD]
                values = kv[s, pl.ds(first, CHUNK), HD:]
                scores = dot(q, keys, 1, 1) * SCALE
                key_place = first + lax.broadcasted_iota(jnp.int32, scores.shape, 1)
                seen = (key_place >= start) & (key_place <= place)
                scores = jnp.where(seen, scores, NEVER)
                new_top = jnp.maximum(top, jnp.max(scores, axis=1, keepdims=True))
                fade = jnp.exp(top - new_top)
                weights = jnp.exp(scores - new_top)
                total = total * fade + jnp.sum(weights, axis=1, keepdims=True)
                out = out * fade + dot(weights.astype(bf16), values, 1, 0)
                return new_top, total, out

            at = 4 * s + 2 * b
            top, total, out = lax.fori_loop(
                range_ref[at],
                range_ref[at + 1],
                step,
                (
                    jnp.full((heads * half, 1), NEVER, f32),
                    jnp.zeros((heads * half, 1), f32),
                    jnp.zeros((heads * half, HD), f32),
                ),
            )
            out = out / total
            logs[s, b] = top + jnp.log(total)
            attended[s, b] = out
            for h in range(heads):
                attended_b[s, mine, h * HD : (h + 1) * HD] = out[h * half : (h + 1) * half].astype(
                    bf16
                )
        branch[s] = dot(attended_b[s], weight[...], 1, 1)


def attend(where, ranges, queries, starts, places, weight, parts, flips, cuts):
    _, heads, rows, _ = queries.shape
    keys = 2 * parts[0].shape[0] * rows
    half = rows // 2
    return pl.pallas_call(
        functools.partial(attend_kernel, flips, cuts, heads),
        out_shape=[
            jax.ShapeDtypeStruct((2, keys, 2 * HD), bf16),
            jax.ShapeDtypeStruct((2, 2, heads * half, HD), f32),
            jax.ShapeDtypeStruct((2, rows, heads * HD), bf16),
            jax.ShapeDtypeStruct((2, 2, heads * half, 1), f32),
            jax.ShapeDtypeStruct((2, rows, weight.shape[0]), f32),
        ],
        in_specs=[SMEM] * 2 + [VMEM] * (4 + len(parts)),
        out_specs=[VMEM] * 5,
        compiler_params=BIG,
        name="attend",
    )(where, ranges, queries, starts, places, weight, *parts)


def attend_back_kernel(
    heads,
    range_ref,
    branch_own,
    branch_other,
    weight,
    queries,
    kv,
    attended,
    logs,
    starts,
    places,
    cos,
    sin,
    query_out,
    kv_out,
    grads,
    kv_sum,
):
    rows = queries.shape[2]
    half = rows // 2
    chips = kv.shape[1] // rows
    kv_sum[...] = jnp.zeros_like(kv_sum)
    for s, branch in enumerate((branch_own, branch_other)):
        grads[s] = dot(branch[...], weight[...], 1, 0).astype(bf16)
    for s in range(2):
        for b in range(2):
            mine = slice(b * half, (b + 1) * half)
            q = queries[s, :, mine, :].reshape(heads * half, HD)
            start = jnp.concatenate([starts[s, mine, :]] * heads, axis=0)
            place = jnp.concatenate([places[s, mine, :]] * heads, axis=0)
            grad = jnp.concatenate(
                [grads[s, mine, h * HD : (h + 1) * HD] for h in range(heads)], axis=0
            )
            delta = jnp.sum(grad.astype(f32) * attended[s, b], axis=1, keepdims=True)
            log_total = logs[s, b]

            def step(i, query_grad):
                first = pl.multiple_of(i * CHUNK, CHUNK)
                keys = kv[s, pl.ds(first, CHUNK), :HD]
                values = kv[s, pl.ds(first, CHUNK), HD:]
                scores = dot(q, keys, 1, 1) * SCALE
                key_place = first + lax.broadcasted_iota(jnp.int32, scores.shape, 1)
                seen = (key_place >= start) & (key_place <= place)
                weights = jnp.where(seen, jnp.exp(scores - log_total), 0.0)
                weight_grad = dot(grad, values, 1, 1)
                score_grad = (weights * (weight_grad - delta)).astype(bf16)
                kv_sum[s, pl.ds(first, CHUNK), :HD] += dot(score_grad, q, 0, 0)
                kv_sum[s, pl.ds(first, CHUNK), HD:] += dot(weights.astype(bf16), grad, 0, 0)
                return query_grad + dot(score_grad, keys, 1, 0)

            at = 4 * s + 2 * b
            query_grad = lax.fori_loop(
                range_ref[at], range_ref[at + 1], step, jnp.zeros((heads * half, HD), f32)
            )
            cos_b, sin_b = cos[s, mine, :] * SCALE, sin[s, mine, :] * SCALE
            for h in range(heads):
                z = query_grad[h * half : (h + 1) * half]
                z = z * cos_b - pltpu.roll(z, HD // 2, 1) * sin_b
                query_out[s, mine, h * HD : (h + 1) * HD] = z.astype(bf16)

    def give(chip, carry):
        for s in range(2):
            for b in range(2):
                block = chip if b == 0 else 2 * chips - 1 - chip
                place = pl.multiple_of(block * half, half)
                mine = slice(b * half, (b + 1) * half)
                source = kv_sum[s, pl.ds(place, half), :]
                kv_out[chip % 8, chip // 8, s, mine, :HD] = (source[:, :HD] * SCALE).astype(bf16)
                kv_out[chip % 8, chip // 8, s, mine, HD:] = source[:, HD:].astype(bf16)
        return carry

    lax.fori_loop(0, chips, give, 0)


def attend_back(
    ranges, branch_own, branch_other, weight, queries, kv, attended, logs, starts, places, cos, sin
):
    _, heads, rows, _ = queries.shape
    keys = kv.shape[1]
    chips = keys // rows
    return pl.pallas_call(
        functools.partial(attend_back_kernel, heads),
        out_shape=[
            jax.ShapeDtypeStruct((2, rows, heads * HD), bf16),
            jax.ShapeDtypeStruct((8, chips // 8, 2, rows, 2 * HD), bf16),
        ],
        in_specs=[SMEM] + [VMEM] * 11,
        out_specs=[VMEM] * 2,
        scratch_shapes=[
            pltpu.VMEM((2, rows, heads * HD), bf16),
            pltpu.VMEM((2, keys, 2 * HD), f32),
        ],
        compiler_params=BIG,
        name="attend_back",
    )(
        ranges,
        branch_own,
        branch_other,
        weight,
        queries,
        kv,
        attended,
        logs,
        starts,
        places,
        cos,
        sin,
    )


def on_device(
    tokens, cotangent, doc_lengths, norm_attn, w_qkv, b_qkv, w_out, norm_mlp, w_gate, w_up, w_down
):
    ctx_size = lax.axis_size("ctx")
    chip = lax.axis_index("ctx")
    core = lax.axis_index("wshard")
    where = jnp.stack([chip, core]).astype(jnp.int32)
    high = high_bits()
    groups = ctx_size // 8
    tok_dev, width = tokens.shape[1], tokens.shape[2]
    ff = w_gate.shape[1]
    ff_own = ff // 8
    heads = H // KVH
    hq = heads * HD
    rows_dev = w_qkv.shape[0]
    cuts = row_parts(tok_dev)
    half = tok_dev // 2
    flips = [relative_flips(high + order) for order in ORDERS]
    group_flips = relative_flips(group_bits())
    low, middle, upper = member_bits()

    n_gain, n_bias = norm_attn.shape[0], b_qkv.shape[0]
    small = jnp.concatenate([norm_attn, b_qkv, norm_mlp])[None]
    small = jnp.pad(small, ((0, 15), (hq, 2 * HD - small.shape[1])))
    qkv_send = jnp.concatenate([head_columns(w_qkv, 1 - core), small])
    qkv_own = jnp.concatenate([head_columns(w_qkv, core), small])
    token_own, out_grad_b = tokens[0], cotangent[0]
    out_t = w_out.T
    qkv_other = core_swap(qkv_send)
    token_other = core_swap(token_own)
    length_other = core_swap(doc_lengths[0])
    out_other = core_swap(half_of(out_t, 1 - core, 1))
    down_found = gather_list(w_down, group_bits())
    length_pair = jnp.stack([doc_lengths[0], length_other])
    qkv_pair = jnp.stack([qkv_own, qkv_other])[None]
    qkv_pair, w_gate, out_other = together(qkv_pair, w_gate, out_other)
    out_pair = by_core(half_of(out_t, core, 1), out_other, core)
    out_w = lax.all_gather(out_pair, "ctx", axis=0, tiled=False).reshape(width, hq)
    out_grad_all = lax.all_gather(
        after(out_grad_b, out_w), "ctx", axis=0, tiled=True, axis_index_groups=group_lists()
    )
    qkv_pair = gather_relative(qkv_pair, high)
    packed = pack_members(w_gate, w_up)
    qkv_pair, packed, down_found = together(qkv_pair, packed, down_found)
    column_cuts = ((0, hq // 2, rows_dev), (hq // 2, hq, rows_dev), (hq, hq + 2 * HD, rows_dev + 16))
    qkv_parts = [qkv_pair[:, :, :rows, start:stop] for start, stop, rows in column_cuts]
    qkv_parts = doubled(qkv_parts, [order[0] for order in ORDERS])
    down_other = [core_swap(x) for x in down_found]
    qkv_parts = doubled(qkv_parts, [order[1] for order in ORDERS])
    qkv_parts = with_arrived(qkv_parts, [order[2] for order in ORDERS])
    qkv_parts, packed = together(qkv_parts, packed)
    row_cut = rows_dev // 3
    first_rows, later_rows = packed[:, :row_cut], packed[:, row_cut:]
    first_rows = group_exchange(first_rows)

    inner = jnp.arange(tok_dev, dtype=jnp.int32)
    blocks = jnp.where(inner < half, chip, 2 * ctx_size - 1 - chip)
    places = (blocks * half + inner % half).astype(jnp.int32)
    ends = jnp.cumsum(length_pair, axis=1)
    passed = ends[:, None, :] <= places[None, :, None]
    starts = jnp.sum(jnp.where(passed, length_pair[:, None, :], 0), axis=2)
    places = jnp.broadcast_to(places[None], starts.shape)
    frequency = ROPE_BASE ** (-jnp.arange(HD // 2, dtype=f32) * 2.0 / HD)
    angles = (places - starts).astype(f32)[..., None] * frequency
    cos_half, sin_half = jnp.cos(angles), jnp.sin(angles)
    cos = jnp.concatenate([cos_half, cos_half], axis=-1)
    sin = jnp.concatenate([-sin_half, sin_half], axis=-1)
    first = jnp.min(starts.reshape(2, 2, half), axis=2) // CHUNK
    last = jnp.max(places.reshape(2, 2, half), axis=2) // CHUNK + 1
    ranges = jnp.stack([first, last], axis=-1).reshape(-1).astype(jnp.int32)
    starts, places = starts[..., None], places[..., None]

    if rows_dev % 16:
        qkv_w, small_all = order_weights(qkv_parts, flips, where)
        qkv_w = qkv_w.reshape(width, hq + 2 * HD)
        small_all = small_all.reshape(2 * ctx_size, 2 * HD)
        gain_one = small_all[:, :n_gain].reshape(1, -1)
        bias = small_all[:, n_gain : n_gain + n_bias].reshape(1, -1)
        gain_two = small_all[:, n_gain + n_bias : 2 * n_gain + n_bias].reshape(1, -1)
        bias = head_columns(bias, core)
        normed_one, queries, kv_own = project(token_own, token_other, gain_one, qkv_w, bias, cos, sin)
    else:
        normed_one, queries, kv_own, qkv_w, gains = order_project(
            where, token_own, token_other, cos, sin, qkv_parts, flips, n_gain, n_bias, rows_dev
        )
        gain_one, gain_two = gains[:1], gains[1:]
    kv_own = gather_relative(kv_own[None], high)
    kv_own, first_rows = together(kv_own, first_rows)

    kv_parts = [kv_own[:, :, start:stop] for start, stop in cuts]
    for step in range(2):
        kv_parts = doubled(kv_parts, [order[step] for order in ORDERS])
    down = order_rows([x[None] for x in down_found], [x[None] for x in down_other], group_flips, where)
    down = down.reshape(ff_own, width)
    kv_parts = with_arrived(kv_parts, [order[2] for order in ORDERS])
    kv_parts, down, later_rows, first_rows = together(kv_parts, down, later_rows, first_rows)
    later_rows = group_exchange(later_rows)
    kv, attended, attended_b, logs, branch = attend(
        where, ranges, queries, starts, places, out_w, kv_parts, flips, cuts
    )
    branch_other = core_swap(branch[1])
    branch_other, later_rows, first_rows = together(branch_other, later_rows, first_rows)
    packed = jnp.concatenate([first_rows, later_rows], axis=1)
    shares = ((0, 4), (4, 8))
    packed_found = [gather_list(packed[:4], group_bits())]
    packed_other = core_swap(packed)
    inputs = token_own.astype(f32)
    hidden_res = inputs + branch[0] + branch_other
    scale_two = lax.rsqrt(jnp.mean(hidden_res * hidden_res, axis=-1, keepdims=True) + EPSILON)
    normed_two = (hidden_res * scale_two * gain_two).astype(bf16)

    group_orders = ((upper, middle, low), (upper, low, middle))
    group_cuts = ((0, half), (half, tok_dev))
    token_parts = gather_relative(normed_two[None], (upper,))
    token_parts, packed, packed_found = together(token_parts, packed, packed_found)
    token_parts = [token_parts[:, start:stop] for start, stop in group_cuts]
    token_parts = doubled(token_parts, [order[1] for order in group_orders])
    packed_found.append(gather_list(packed[4:], group_bits()))
    token_parts, out_grad_all = together(token_parts, out_grad_all)
    token_parts = with_arrived(token_parts, [order[2] for order in group_orders])
    token_parts, packed_found = together(token_parts, packed_found)
    token_flips = [relative_flips(order) for order in group_orders]
    normed_all = order_tokens(token_parts, token_flips, group_cuts, groups, where)
    normed_all = normed_all.reshape(8 * tok_dev, width)

    sources, loads = [packed, packed_other], [(0, 0, 0), (0, 1, 0)]
    for found, (first, _) in zip(packed_found, shares):
        for piece, flip in list(zip(found, group_flips))[1:]:
            sources.extend([piece, core_swap(piece)])
            loads.extend([(flip, 0, first), (flip, 1, first)])
    if rows_dev % 16:
        own, other = [], []
        for flip in group_flips:
            for core_flip, side in enumerate((own, other)):
                found = [x for x, load in zip(sources, loads) if load[:2] == (flip, core_flip)]
                side.append(jnp.concatenate(found))
        sources, loads = [order_rows(own, other, group_flips, where).reshape(width, -1)], [(None, 0, 0)]
    out_grad = out_grad_b.astype(f32)
    pre_grad, activated, normed_grad_part = mlp(
        where, groups, normed_all, out_grad_all, down, sources, loads
    )

    normed_grad_part = normed_grad_part.reshape(2, 2, 2, tok_dev, width)
    scatter = Scatter(
        [normed_grad_part[:, :, :, start:stop] for start, stop in group_cuts], (upper, middle, low)
    )
    bits = [order[2] for order in group_orders]
    kept, sent = scatter.split(bits)
    gate_keep, gate_send = gate_up_grads(normed_all, after(pre_grad, *sent), 0, rows_dev, where)
    gate_arrived = core_swap(gate_send)
    branch_part = dot(after(activated, gate_send), down, 1, 0).astype(bf16)
    scatter.step(bits, kept, sent)
    scatter.parts, gate_arrived, branch_part = together(scatter.parts, gate_arrived, branch_part)

    def of_cores(keep, arrived):
        total = (keep.astype(f32) + arrived.astype(f32)).astype(bf16)
        return total.reshape(8, groups, rows_dev, -1)

    def of_group(total):
        return sum_over(total, 1, tuple(reversed(group_bits()))).astype(bf16)

    bits = [order[1] for order in group_orders]
    kept, sent = scatter.split(bits)
    gate_total = of_cores(gate_keep, gate_arrived)
    scatter.step(bits, kept, sent)
    scatter.parts, gate_total, pre_grad = together(scatter.parts, gate_total, pre_grad)

    kept, sent = scatter.split((upper, upper))
    grad_gate = of_group(gate_total)
    up_keep, up_send = gate_up_grads(normed_all, after(pre_grad, *sent), 1, rows_dev, where)
    branch_part = branch_part.reshape(2, 2, 2, tok_dev, width)
    branch_sums = Scatter(
        [branch_part[:, :, :, start:stop] for start, stop in group_cuts], (upper, middle, low)
    )
    bits = [order[2] for order in group_orders]
    branch_kept, branch_sent = branch_sums.split(bits)
    scatter.step((upper, upper), kept, sent)
    branch_arrived = [chip_swap(x, 1 << bit) for x, bit in zip(branch_sent, bits)]
    scatter.parts, grad_gate, up_send = together(scatter.parts, grad_gate, up_send)
    grad_gate = group_exchange(grad_gate)
    up_arrived = core_swap(up_send)
    normed_two_grad = jnp.concatenate(scatter.parts)
    gain_two_grad = jnp.sum(normed_two_grad * hidden_res * scale_two, axis=0)
    hidden_grad = out_grad + rms_back(normed_two_grad, hidden_res, scale_two, gain_two)

    falling = tuple(reversed(group_bits()))
    def weight_parts(x):
        return x.astype(bf16).reshape(ctx_size // 8, 8, 2, rows_dev, x.shape[1])

    branch_own = hidden_grad.astype(bf16)
    branch_other = core_swap(branch_own)
    branch_own, branch_other, up_arrived, branch_arrived = together(
        branch_own, branch_other, up_arrived, branch_arrived
    )
    grad_up = of_group(of_cores(up_keep, up_arrived))
    project_grad_q, kv_grad = attend_back(
        ranges, branch_own, branch_other, out_w, queries, kv, attended, logs, starts, places, cos, sin
    )
    (kv_grad, project_grad_q), grad_gate, grad_up, activated = together(
        (kv_grad, project_grad_q), grad_gate, grad_up, activated
    )
    kv_sum = cube_exchange(kv_grad)
    down_keep, down_send = down_grads(activated, out_grad_all, groups, where)
    branch_grad = jnp.concatenate([branch_own, branch_other])
    normed_one = normed_one.reshape(-1, width)
    project_grad_q = project_grad_q.reshape(-1, hq)
    grad_out_part = weight_parts(dot(branch_grad, attended_b.reshape(-1, hq), 0, 0))
    grad_q_part = weight_parts(dot(normed_one, project_grad_q, 0, 0))
    wide_part = jnp.concatenate([grad_q_part, grad_out_part], axis=-1)
    names = tuple(reversed(high)) + (2, 1, 0)
    wide_part = wide_part.reshape((2,) * len(names) + wide_part.shape[2:])
    third = 2 * hq // 3
    scatter = Scatter([wide_part[..., i * third : (i + 1) * third] for i in range(3)], names)
    bits = [order[0] for order in ORDERS]
    kept, sent = scatter.split(bits)
    arrived = [chip_swap(x, 1 << bit) for x, bit in zip(sent, bits)]
    kv_sum, arrived, down_send, branch_arrived = together(
        kv_sum, arrived, down_send, branch_arrived
    )

    kv_sum = jnp.sum(kv_sum.astype(f32), axis=0).astype(bf16)
    kv_sum, grad_up = together(kv_sum, grad_up)
    kv_sum = sum_over_high(kv_sum, high)
    down_arrived = core_swap(down_send)
    grad_up = group_exchange(grad_up)
    key_pre = kv_sum[..., :HD]
    key_pre = key_pre * cos - jnp.roll(key_pre, HD // 2, axis=-1) * sin
    project_grad_kv = jnp.concatenate([key_pre, kv_sum[..., HD:]], axis=-1).astype(bf16)
    project_grad_kv = project_grad_kv.reshape(-1, 2 * HD)
    grad_kv = weight_parts(dot(normed_one, project_grad_kv, 0, 0)).swapaxes(0, 1)
    project_grad = jnp.concatenate([project_grad_q, project_grad_kv], axis=1)
    normed_one_grad = dot(project_grad, qkv_w, 1, 1)
    normed_one_grad = normed_one_grad[:tok_dev] + core_swap(normed_one_grad[tok_dev:])
    scatter.add(kept, arrived)
    branch_sums.add(branch_kept, branch_arrived)
    branch_sums.step([order[1] for order in group_orders])
    down_sum = (down_keep.astype(f32) + down_arrived.astype(f32)).astype(bf16)
    grad_kv, grad_up, scatter.parts, branch_sums.parts, down_sum, normed_one_grad = together(
        grad_kv, grad_up, scatter.parts, branch_sums.parts, down_sum, normed_one_grad
    )
    grad_kv = cube_exchange(grad_kv)
    branch_sums.parts = [jnp.concatenate(branch_sums.parts, axis=-2)]
    branch_sums.step((upper,))
    scatter.step([order[1] for order in ORDERS])
    scatter.step([order[2] for order in ORDERS])
    scatter.parts = [jnp.concatenate(scatter.parts, axis=-1)]
    scale_one = lax.rsqrt(jnp.mean(inputs * inputs, axis=-1, keepdims=True) + EPSILON)
    gain_one_grad = jnp.sum(normed_one_grad * inputs * scale_one, axis=0)
    input_grad = hidden_grad + rms_back(normed_one_grad, inputs, scale_one, gain_one)

    def whole_columns(x):
        return jnp.concatenate(
            [
                x[0, :, :hq],
                x[1, :, :hq],
                x[0, :, hq : hq + HD],
                x[1, :, hq : hq + HD],
                x[0, :, hq + HD : hq + 2 * HD],
                x[1, :, hq + HD : hq + 2 * HD],
            ],
            axis=1,
        )

    bias_grad = jnp.sum(project_grad.astype(f32), axis=0, keepdims=True)
    zeros = jnp.zeros_like(bias_grad)
    bias_full = whole_columns(
        jnp.stack([jnp.where(core == 0, bias_grad, zeros), jnp.where(core == 0, zeros, bias_grad)])
    )[0]
    qk_width = (H + KVH) * HD
    sums = jnp.concatenate(
        [
            x.reshape(ctx_size, 1, -1)
            for x in (gain_one_grad, gain_two_grad, bias_full[:qk_width], bias_full[qk_width:])
        ],
        axis=2,
    )
    grad_kv, scatter.parts, branch_sums.parts, sums, down_sum = together(
        grad_kv, scatter.parts, branch_sums.parts, sums, down_sum
    )
    sums = lax.all_to_all(sums, "ctx", split_axis=0, concat_axis=0, tiled=True)
    grad_kv = jnp.sum(grad_kv.astype(f32), axis=0).astype(bf16)
    grad_kv = sum_over_high(grad_kv, high)
    grad_down = sum_over(down_sum, 0, falling)
    for bit in reversed(high):
        scatter.step((bit,))
    scattered = scatter.parts[0]
    sums = jnp.sum(sums, axis=0)
    sums = (sums + core_swap(sums))[0]
    output = (hidden_res + branch_sums.parts[0]).astype(bf16)

    grad_gate, grad_up = unpack_members(grad_gate, grad_up, ff)
    chip_grad = jnp.concatenate([scattered[..., :hq], grad_kv, scattered[..., hq:]], axis=-1)

    def pick(x, which):
        return lax.dynamic_index_in_dim(x, which, 0, keepdims=False)

    pair = by_core(pick(chip_grad, core), core_swap(pick(chip_grad, 1 - core)), core)
    grad_qkv = whole_columns(pair)
    grad_out = pair[:, :, hq + 2 * HD :].transpose(1, 0, 2).reshape(-1, 2 * hq).T

    def owned(start, size):
        return lax.dynamic_slice_in_dim(sums, start + core * (size // 2), size // 2, 0)

    own_width, own_qk, own_v = width // ctx_size, qk_width // ctx_size, KVH * HD // ctx_size
    return (
        output[None],
        input_grad[None],
        owned(0, own_width),
        grad_qkv,
        owned(2 * own_width, own_qk),
        owned(2 * own_width + own_qk, own_v),
        grad_out,
        owned(own_width, own_width),
        grad_gate,
        grad_up,
        grad_down,
    )


def solution(mesh):
    whole = ("ctx", "wshard")
    rows, columns, flat = P(whole, None), P(None, whole), P(whole)
    tokens = P("wshard", "ctx", None)
    return jax.shard_map(
        on_device,
        mesh=mesh,
        in_specs=(tokens, tokens, P("wshard", None), flat, rows, flat, columns, flat, rows, rows, rows),
        out_specs=(tokens, tokens, flat, rows, flat, flat, columns, flat, rows, rows, rows),
        check_vma=False,
    )
```

```python
import functools
import math

import jax
import jax.numpy as jnp
from jax import lax
from jax.experimental import pallas as pl
from jax.experimental.pallas import tpu as pltpu
from jax.sharding import PartitionSpec as P

H = 12
KVH = 2
HD = 128
EPSILON = 1e-06
ROPE_BASE = 1000000.0
ORDERS = ((0, 1, 2), (1, 2, 0), (2, 0, 1))
CHUNK = 256
NEVER = -1e30
SCALE = 1.0 / math.sqrt(HD)
bf16 = jnp.bfloat16
f32 = jnp.float32
VMEM = pl.BlockSpec(memory_space=pltpu.VMEM)
SMEM = pl.BlockSpec(memory_space=pltpu.SMEM)
BIG = pltpu.CompilerParams(vmem_limit_bytes=56 * 1024 * 1024)


def after(x, *others):
    return together(x, *others)[0]


def together(*groups):
    flat, tree = jax.tree.flatten(groups)
    return jax.tree.unflatten(tree, lax.optimization_barrier(flat))


def core_swap(x):
    return lax.ppermute(x, "wshard", [(0, 1), (1, 0)])


def chip_swap(x, flip):
    count = lax.axis_size("ctx")
    return lax.ppermute(x, "ctx", [(i, i ^ flip) for i in range(count)])


def cubes():
    count = lax.axis_size("ctx")
    return [list(range(i, i + 8)) for i in range(0, count, 8)]


def cube_exchange(x):
    return lax.all_to_all(
        x, "ctx", split_axis=0, concat_axis=0, tiled=True, axis_index_groups=cubes()
    )


def group_bits():
    return tuple(range(lax.axis_size("ctx").bit_length() - 4))


def member_bits():
    first = len(group_bits())
    return (first, first + 1, first + 2)


def group_lists():
    groups = lax.axis_size("ctx") // 8
    return [[g + groups * m for m in range(8)] for g in range(groups)]


def group_exchange(x):
    return lax.all_to_all(
        x, "ctx", split_axis=0, concat_axis=0, tiled=True, axis_index_groups=group_lists()
    )


def high_bits():
    return tuple(range(3, lax.axis_size("ctx").bit_length() - 1))


def my_bit(bit):
    return (lax.axis_index("ctx") >> bit) & 1


def gather_relative(x, bits):
    for bit in bits:
        x = jnp.concatenate([x, chip_swap(x, 1 << bit)], axis=0)
    return x


def gather_list(x, bits):
    found = [x]
    for bit in bits:
        found = found + [chip_swap(y, 1 << bit) for y in found]
    return found


def relative_flips(bits):
    flips = [0]
    for bit in bits:
        flips = flips + [f ^ (1 << bit) for f in flips]
    return flips


def sum_over(x, axis, bits):
    for at, bit in enumerate(bits):
        shape = x.shape
        x = x.reshape(shape[:axis] + (2, shape[axis] // 2) + shape[axis + 1 :])
        keep = lax.dynamic_index_in_dim(x, my_bit(bit), axis, keepdims=False)
        send = lax.dynamic_index_in_dim(x, 1 - my_bit(bit), axis, keepdims=False)
        x = keep.astype(f32) + chip_swap(send.astype(bf16), 1 << bit).astype(f32)
        if at < len(bits) - 1:
            x = x.astype(bf16)
    return jnp.squeeze(x, axis).astype(f32)


def sum_over_high(x, high):
    return sum_over(x, 0, tuple(reversed(high)))


def row_parts(rows):
    third = rows * 3 // 8
    return ((0, third), (third, 2 * third), (2 * third, rows))


def doubled(parts, bits):
    return [jnp.concatenate([x, chip_swap(x, 1 << bit)]) for x, bit in zip(parts, bits)]


def with_arrived(parts, bits):
    found = []
    for x, bit in zip(parts, bits):
        found.extend([x, chip_swap(x, 1 << bit)])
    return found


def both_halves(x, layout, bit):
    axis = layout.index(bit)
    keep = lax.dynamic_index_in_dim(x, my_bit(bit), axis, keepdims=False)
    send = lax.dynamic_index_in_dim(x, 1 - my_bit(bit), axis, keepdims=False)
    return keep, send


class Scatter:
    def __init__(self, parts, layout):
        self.parts = list(parts)
        self.layouts = [list(layout) for _ in self.parts]

    def split(self, bits):
        pairs = [both_halves(x, l, b) for x, l, b in zip(self.parts, self.layouts, bits)]
        for layout, bit in zip(self.layouts, bits):
            layout.remove(bit)
        return [k for k, _ in pairs], [s.astype(bf16) for _, s in pairs]

    def step(self, bits, kept=None, sent=None):
        if kept is None:
            kept, sent = self.split(bits)
        self.add(kept, [chip_swap(x, 1 << bit) for x, bit in zip(sent, bits)])

    def add(self, kept, arrived):
        self.parts = [k.astype(f32) + a.astype(f32) for k, a in zip(kept, arrived)]
        if self.layouts[0]:
            self.parts = [x.astype(bf16) for x in self.parts]


def dot(left, right, left_axis, right_axis):
    return lax.dot_general(
        left, right, (((left_axis,), (right_axis,)), ((), ())), preferred_element_type=f32
    )


def rms_back(grad_in, values, scale_rows, gain_row):
    weighted = grad_in * gain_row
    return scale_rows * weighted - values * scale_rows**3 * jnp.mean(
        weighted * values, axis=-1, keepdims=True
    )


def half_of(x, which, axis):
    size = x.shape[axis] // 2
    return lax.dynamic_slice_in_dim(x, which * size, size, axis)


def head_columns(x, core):
    q_width, kv_width = H * HD, KVH * HD
    return jnp.concatenate(
        [
            half_of(x[:, :q_width], core, 1),
            half_of(x[:, q_width : q_width + kv_width], core, 1),
            half_of(x[:, q_width + kv_width :], core, 1),
        ],
        axis=1,
    )


def by_core(mine, other, core):
    return jnp.stack([jnp.where(core == 0, mine, other), jnp.where(core == 0, other, mine)])


def order_weights_kernel(flips, extra_rows, where_ref, *refs):
    parts, out = refs[: 2 * len(flips)], refs[2 * len(flips)]
    chip, core = where_ref[0], where_ref[1]
    count, rows = parts[0].shape[0], out.shape[2]
    at = 0
    for p, part_flips in enumerate(flips):
        columns = parts[2 * p].shape[3]
        for k, flip in enumerate(part_flips):
            part = parts[2 * p + k // count]
            for h in range(2):
                out[chip ^ flip, core ^ h, :, at : at + columns] = part[k % count, h, :rows]
                if extra_rows and p == len(flips) - 1:
                    extra = part[k % count, h, rows:].astype(f32)[:1]
                    refs[-1][chip ^ flip, core ^ h] = extra
        at += columns


def order_weights(parts, flips, where):
    count, _, rows, _ = parts[0].shape
    columns = sum(p.shape[3] for p in parts[::2])
    extra = parts[-1].shape[2] > rows
    shapes = [jax.ShapeDtypeStruct((2 * count, 2, rows, columns), bf16)]
    if extra:
        shapes.append(jax.ShapeDtypeStruct((2 * count, 2, 1, parts[-1].shape[3]), f32))
    return pl.pallas_call(
        functools.partial(order_weights_kernel, flips, extra),
        out_shape=shapes,
        in_specs=[SMEM] + [VMEM] * len(parts),
        out_specs=[VMEM] * len(shapes),
        compiler_params=BIG,
        name="order_weights",
    )(where, *parts)


def order_rows_kernel(flips, where_ref, *refs):
    out = refs[-1]
    chip, core = where_ref[0], where_ref[1]
    group = chip % len(flips)
    for k, flip in enumerate(flips):
        out[:, group ^ flip, core] = refs[k][...]
        out[:, group ^ flip, 1 - core] = refs[len(flips) + k][...]


def order_rows(own, other, flips, where):
    members, rows, columns = own[0].shape
    groups = len(own)
    tile = columns // 2 if columns % 256 == 0 else columns
    source = pl.BlockSpec((1, rows, tile), lambda m, n: (m, 0, n))
    return pl.pallas_call(
        functools.partial(order_rows_kernel, flips),
        grid=(members, columns // tile),
        out_shape=jax.ShapeDtypeStruct((members, groups, 2, rows, columns), bf16),
        in_specs=[SMEM] + [source] * (2 * groups),
        out_specs=pl.BlockSpec((1, groups, 2, rows, tile), lambda m, n: (m, 0, 0, 0, n)),
        compiler_params=BIG,
        name="order_rows",
    )(where, *own, *other)


def order_tokens_kernel(flips, cuts, groups, where_ref, *refs):
    out = refs[-1]
    member = where_ref[0] // groups
    for p, (start, stop) in enumerate(cuts):
        for k, flip in enumerate(flips[p]):
            half = refs[2 * p + k // 4]
            out[member ^ (flip // groups), start:stop, :] = half[k % 4]


def order_tokens(halves, flips, cuts, groups, where):
    rows, width = cuts[-1][1], halves[0].shape[2]
    return pl.pallas_call(
        functools.partial(order_tokens_kernel, flips, cuts, groups),
        out_shape=jax.ShapeDtypeStruct((8, rows, width), bf16),
        in_specs=[SMEM] + [VMEM] * len(halves),
        out_specs=VMEM,
        compiler_params=BIG,
        name="order_tokens",
    )(where, *halves)


def padded(ff_own):
    return -(-ff_own // 128) * 128


def pack_members_kernel(gate, up, out):
    own, wide = gate.shape[1] // 8, out.shape[2] // 2
    for m in range(8):
        for at, source in ((0, gate), (wide, up)):
            out[m, :, at : at + own] = source[:, m * own : (m + 1) * own]
            out[m, :, at + own : at + wide] = jnp.zeros((out.shape[1], wide - own), bf16)


def pack_members(gate, up):
    rows, ff = gate.shape
    return pl.pallas_call(
        pack_members_kernel,
        out_shape=jax.ShapeDtypeStruct((8, rows, 2 * padded(ff // 8)), bf16),
        in_specs=[VMEM] * 2,
        out_specs=VMEM,
        compiler_params=BIG,
        name="pack_members",
    )(gate, up)


def unpack_members_kernel(packed_gate, packed_up, gate, up):
    own = gate.shape[1] // 8
    for m in range(8):
        for packed, target in ((packed_gate, gate), (packed_up, up)):
            target[:, m * own : (m + 1) * own] = packed[m, :, :own].astype(f32)


def unpack_members(packed_gate, packed_up, ff):
    rows = packed_gate.shape[1]
    return pl.pallas_call(
        unpack_members_kernel,
        out_shape=[jax.ShapeDtypeStruct((rows, ff), f32)] * 2,
        in_specs=[VMEM] * 2,
        out_specs=[VMEM] * 2,
        compiler_params=BIG,
        name="unpack_members",
    )(packed_gate, packed_up)


def mlp_kernel(loads, groups, where_ref, normed, out_grad, down, *refs):
    sources = refs[: len(loads)]
    pre_grad, activated, normed_grad, gate_up, arrived = refs[len(loads) :]
    chip, core = where_ref[0], where_ref[1]

    @pl.when(pl.program_id(0) == 0)
    def _():
        copies = []
        for source, (flip, other, first) in zip(sources, loads):
            if flip is None:
                copies.append(pltpu.make_async_copy(source, gate_up, arrived.at[len(copies)]))
                continue
            rows = source.shape[1]
            for i in range(source.shape[0]):
                device = 2 * ((first + i) * groups + (chip % groups ^ flip)) + (core ^ other)
                target = gate_up.at[pl.ds(pl.multiple_of(device * rows, 16), rows), :]
                copies.append(pltpu.make_async_copy(source.at[i], target, arrived.at[len(copies)]))
        for copy in copies:
            copy.start()
        for copy in copies:
            copy.wait()

    ff_own = down.shape[0]
    wide = gate_up.shape[1] // 2
    gates, ups = slice(0, ff_own), slice(wide, wide + ff_own)
    n = normed[...]
    gate = dot(n, gate_up[:, gates], 1, 0)
    up = dot(n, gate_up[:, ups], 1, 0)
    act_grad = dot(out_grad[...], down[...], 1, 1)
    sig = jax.nn.sigmoid(gate)
    act = gate * sig
    activated[...] = (act * up).astype(bf16)
    if wide > ff_own:
        gap = jnp.zeros((n.shape[0], wide - ff_own), bf16)
        pre_grad[:, ff_own:wide] = gap
        pre_grad[:, wide + ff_own :] = gap
    pre_grad[:, gates] = (act_grad * up * sig * (1.0 + gate * (1.0 - sig))).astype(bf16)
    pre_grad[:, ups] = (act_grad * act).astype(bf16)
    normed_grad[...] = dot(pre_grad[...], gate_up[...], 1, 1).astype(bf16)


def mlp(where, groups, normed, out_grad, down, sources, loads, tile=256):
    rows, width = normed.shape
    ff_own, wide = down.shape[0], sources[0].shape[-1]
    count = sum(1 if flip is None else x.shape[0] for x, (flip, _, _) in zip(sources, loads))

    def by_rows(columns):
        return pl.BlockSpec((tile, columns), lambda i: (i, 0))

    return pl.pallas_call(
        functools.partial(mlp_kernel, loads, groups),
        grid=(rows // tile,),
        out_shape=[
            jax.ShapeDtypeStruct((rows, wide), bf16),
            jax.ShapeDtypeStruct((rows, ff_own), bf16),
            jax.ShapeDtypeStruct((rows, width), bf16),
        ],
        in_specs=[
            SMEM,
            by_rows(width),
            by_rows(width),
            pl.BlockSpec(down.shape, lambda i: (0, 0), pipeline_mode=pl.Buffered(1)),
        ]
        + [pl.BlockSpec(memory_space=pl.ANY)] * len(sources),
        out_specs=[by_rows(wide), by_rows(ff_own), by_rows(width)],
        scratch_shapes=[pltpu.VMEM((width, wide), bf16), pltpu.SemaphoreType.DMA((count,))],
        compiler_params=BIG,
        name="mlp",
    )(where, normed, out_grad, down, *sources)


def gate_up_grads_kernel(rows_dev, where_ref, normed, pre_grad, keep, send):
    grads = dot(normed[...], pre_grad[...], 0, 0)
    core = where_ref[1]
    for i in range(keep.shape[0]):
        low = grads[2 * i * rows_dev : (2 * i + 1) * rows_dev].astype(bf16)
        upper = grads[(2 * i + 1) * rows_dev : (2 * i + 2) * rows_dev].astype(bf16)
        keep[i] = jnp.where(core == 0, low, upper)
        send[i] = jnp.where(core == 0, upper, low)


def gate_up_grads(normed, pre_grad, side, rows_dev, where, tile=384):
    rows, width = normed.shape
    wide = pre_grad.shape[1] // 2
    chips, step = width // (2 * rows_dev), tile // (2 * rows_dev)
    result = pl.BlockSpec((step, rows_dev, wide), lambda i: (i, 0, 0))
    return pl.pallas_call(
        functools.partial(gate_up_grads_kernel, rows_dev),
        grid=(width // tile,),
        out_shape=[jax.ShapeDtypeStruct((chips, rows_dev, wide), bf16)] * 2,
        in_specs=[
            SMEM,
            pl.BlockSpec((rows, tile), lambda i: (0, i)),
            pl.BlockSpec((rows, wide), lambda i: (0, side), pipeline_mode=pl.Buffered(1)),
        ],
        out_specs=[result] * 2,
        compiler_params=BIG,
        name="gate_up_grads",
    )(where, normed, pre_grad)


def down_grads_kernel(where_ref, activated, out_grad, keep, send):
    grads = dot(activated[...], out_grad[...], 0, 0)
    core = where_ref[1]
    rows_dev = keep.shape[1]
    for i in range(keep.shape[0]):
        low = grads[2 * i * rows_dev : (2 * i + 1) * rows_dev].astype(bf16)
        upper = grads[(2 * i + 1) * rows_dev : (2 * i + 2) * rows_dev].astype(bf16)
        keep[i] = jnp.where(core == 0, low, upper)
        send[i] = jnp.where(core == 0, upper, low)


def down_grads(activated, out_grad, groups, where, tile=512):
    rows, ff_own = activated.shape
    width = out_grad.shape[1]
    rows_dev = ff_own // (2 * groups)
    result = pl.BlockSpec((groups, rows_dev, tile), lambda i: (0, 0, i))
    return pl.pallas_call(
        down_grads_kernel,
        grid=(width // tile,),
        out_shape=[jax.ShapeDtypeStruct((groups, rows_dev, width), bf16)] * 2,
        in_specs=[
            SMEM,
            pl.BlockSpec((rows, ff_own), lambda i: (0, 0), pipeline_mode=pl.Buffered(1)),
            pl.BlockSpec((rows, tile), lambda i: (0, i)),
        ],
        out_specs=[result] * 2,
        compiler_params=BIG,
        name="down_grads",
    )(where, activated, out_grad)


def project_streams(heads, own, other, gain, weight, bias, cos, sin, normed, queries, kv):
    hq = heads * HD
    for s, tokens in enumerate((own, other)):
        x = tokens[...].astype(f32)
        scale = lax.rsqrt(jnp.mean(x * x, axis=-1, keepdims=True) + EPSILON)
        n = (x * scale * gain).astype(bf16)
        normed[s] = n
        cos_s, sin_s = cos[s], sin[s]
        project = dot(n, weight[...], 1, 0) + bias

        def turn(z):
            return z * cos_s + pltpu.roll(z, HD // 2, 1) * sin_s

        for h in range(heads):
            queries[s, h] = turn(project[:, h * HD : (h + 1) * HD]).astype(bf16)
        kv[s, :, :HD] = turn(project[:, hq : hq + HD]).astype(bf16)
        kv[s, :, HD:] = project[:, hq + HD :].astype(bf16)


def project_kernel(heads, own, other, gain, weight, bias, cos, sin, normed, queries, kv):
    project_streams(
        heads, own, other, gain[...], weight, bias[...], cos, sin, normed, queries, kv
    )


def project(own, other, gain, weight, bias, cos, sin):
    rows, width = own.shape
    heads = H // KVH
    return pl.pallas_call(
        functools.partial(project_kernel, heads),
        out_shape=[
            jax.ShapeDtypeStruct((2, rows, width), bf16),
            jax.ShapeDtypeStruct((2, heads, rows, HD), bf16),
            jax.ShapeDtypeStruct((2, rows, 2 * HD), bf16),
        ],
        in_specs=[VMEM] * 7,
        out_specs=[VMEM] * 3,
        compiler_params=BIG,
        name="project",
    )(own, other, gain, weight, bias, cos, sin)


def order_project_kernel(
    heads, flips, n_gain, n_bias, rows, where_ref, own, other, cos, sin, *refs
):
    parts = refs[: 2 * len(flips)]
    normed, queries, kv, weight, gains, small, line = refs[2 * len(flips) :]
    chip, core = where_ref[0], where_ref[1]
    count = parts[0].shape[0]
    at = 0
    for p, part_flips in enumerate(flips):
        columns = parts[2 * p].shape[3]
        for k, flip in enumerate(part_flips):
            part = parts[2 * p + k // count]
            for h in range(2):
                device = 2 * (chip ^ flip) + (core ^ h)
                first = pl.multiple_of(device * rows, 16)
                weight[pl.ds(first, rows), at : at + columns] = part[k % count, h, :rows]
                if p == len(flips) - 1:
                    small[pl.ds(device, 1), :] = part[k % count, h, rows:].astype(f32)[:1]
        at += columns
    devices = small.shape[0]
    total = devices * n_bias
    for d in range(devices):
        row = small[d : d + 1, :]
        gains[0:1, d * n_gain : (d + 1) * n_gain] = row[:, :n_gain]
        line[1:2, d * n_bias : (d + 1) * n_bias] = row[:, n_gain : n_gain + n_bias]
        gains[1:2, d * n_gain : (d + 1) * n_gain] = row[
            :, n_gain + n_bias : 2 * n_gain + n_bias
        ]
    hq, v = heads * HD, 2 * heads * HD + 2 * HD
    bias = jnp.where(
        core == 0,
        jnp.concatenate(
            [line[1:2, :hq], line[1:2, 2 * hq : 2 * hq + HD], line[1:2, v : v + HD]], axis=1
        ),
        jnp.concatenate(
            [line[1:2, hq : 2 * hq], line[1:2, 2 * hq + HD : v], line[1:2, v + HD : total]], axis=1
        ),
    )
    gain = gains[0:1, :]
    project_streams(heads, own, other, gain, weight, bias, cos, sin, normed, queries, kv)


def order_project(where, own, other, cos, sin, parts, flips, n_gain, n_bias, rows):
    tokens, width = own.shape
    heads = H // KVH
    columns = sum(p.shape[3] for p in parts[::2])
    devices = 4 * parts[0].shape[0]
    return pl.pallas_call(
        functools.partial(order_project_kernel, heads, flips, n_gain, n_bias, rows),
        out_shape=[
            jax.ShapeDtypeStruct((2, tokens, width), bf16),
            jax.ShapeDtypeStruct((2, heads, tokens, HD), bf16),
            jax.ShapeDtypeStruct((2, tokens, 2 * HD), bf16),
            jax.ShapeDtypeStruct((width, columns), bf16),
            jax.ShapeDtypeStruct((2, width), f32),
        ],
        in_specs=[SMEM] + [VMEM] * (4 + len(parts)),
        out_specs=[VMEM] * 5,
        scratch_shapes=[
            pltpu.VMEM((devices, parts[-1].shape[3]), f32),
            pltpu.VMEM((8, devices * n_bias), f32),
        ],
        compiler_params=BIG,
        name="order_project",
    )(where, own, other, cos, sin, *parts)


def pieces(cuts, half):
    found = []
    for p, (start, stop) in enumerate(cuts):
        for b in range(2):
            low, high = max(start, b * half), min(stop, (b + 1) * half)
            if low < high:
                found.append((p, low - start, low - b * half, high - low, b))
    return found


def attend_kernel(
    flips, cuts, heads, where_ref, range_ref, queries, starts, places, weight, *refs
):
    parts, (kv, attended, attended_b, logs, branch) = refs[: 2 * len(cuts)], refs[2 * len(cuts) :]
    chip = where_ref[0]
    rows = queries.shape[2]
    half = rows // 2
    count = parts[0].shape[0]
    chips = 2 * count
    for p, first, at, size, b in pieces(cuts, half):
        for k, flip in enumerate(flips[p]):
            part = parts[2 * p + k // count]
            source = chip ^ flip
            block = source if b == 0 else 2 * chips - 1 - source
            place = pl.multiple_of(block * half + at, 16)
            for s in range(2):
                kv[s, pl.ds(place, size), :] = part[k % count, s, first : first + size, :]

    for s in range(2):
        for b in range(2):
            mine = slice(b * half, (b + 1) * half)
            q = queries[s, :, mine, :].reshape(heads * half, HD)
            start = jnp.concatenate([starts[s, mine, :]] * heads, axis=0)
            place = jnp.concatenate([places[s, mine, :]] * heads, axis=0)

            def step(i, state):
                top, total, out = state
                first = pl.multiple_of(i * CHUNK, CHUNK)
                keys = kv[s, pl.ds(first, CHUNK), :HD]
                values = kv[s, pl.ds(first, CHUNK), HD:]
                scores = dot(q, keys, 1, 1) * SCALE
                key_place = first + lax.broadcasted_iota(jnp.int32, scores.shape, 1)
                seen = (key_place >= start) & (key_place <= place)
                scores = jnp.where(seen, scores, NEVER)
                new_top = jnp.maximum(top, jnp.max(scores, axis=1, keepdims=True))
                fade = jnp.exp(top - new_top)
                weights = jnp.exp(scores - new_top)
                total = total * fade + jnp.sum(weights, axis=1, keepdims=True)
                out = out * fade + dot(weights.astype(bf16), values, 1, 0)
                return new_top, total, out

            at = 4 * s + 2 * b
            top, total, out = lax.fori_loop(
                range_ref[at],
                range_ref[at + 1],
                step,
                (
                    jnp.full((heads * half, 1), NEVER, f32),
                    jnp.zeros((heads * half, 1), f32),
                    jnp.zeros((heads * half, HD), f32),
                ),
            )
            out = out / total
            logs[s, b] = top + jnp.log(total)
            attended[s, b] = out
            for h in range(heads):
                attended_b[s, mine, h * HD : (h + 1) * HD] = out[h * half : (h + 1) * half].astype(
                    bf16
                )
        branch[s] = dot(attended_b[s], weight[...], 1, 1)


def attend(where, ranges, queries, starts, places, weight, parts, flips, cuts):
    _, heads, rows, _ = queries.shape
    keys = 2 * parts[0].shape[0] * rows
    half = rows // 2
    return pl.pallas_call(
        functools.partial(attend_kernel, flips, cuts, heads),
        out_shape=[
            jax.ShapeDtypeStruct((2, keys, 2 * HD), bf16),
            jax.ShapeDtypeStruct((2, 2, heads * half, HD), f32),
            jax.ShapeDtypeStruct((2, rows, heads * HD), bf16),
            jax.ShapeDtypeStruct((2, 2, heads * half, 1), f32),
            jax.ShapeDtypeStruct((2, rows, weight.shape[0]), f32),
        ],
        in_specs=[SMEM] * 2 + [VMEM] * (4 + len(parts)),
        out_specs=[VMEM] * 5,
        compiler_params=BIG,
        name="attend",
    )(where, ranges, queries, starts, places, weight, *parts)


def attend_back_kernel(
    heads,
    range_ref,
    branch_own,
    branch_other,
    weight,
    queries,
    kv,
    attended,
    logs,
    starts,
    places,
    cos,
    sin,
    query_out,
    kv_out,
    grads,
    kv_sum,
):
    rows = queries.shape[2]
    half = rows // 2
    chips = kv.shape[1] // rows
    kv_sum[...] = jnp.zeros_like(kv_sum)
    for s, branch in enumerate((branch_own, branch_other)):
        grads[s] = dot(branch[...], weight[...], 1, 0).astype(bf16)
    for s in range(2):
        for b in range(2):
            mine = slice(b * half, (b + 1) * half)
            q = queries[s, :, mine, :].reshape(heads * half, HD)
            start = jnp.concatenate([starts[s, mine, :]] * heads, axis=0)
            place = jnp.concatenate([places[s, mine, :]] * heads, axis=0)
            grad = jnp.concatenate(
                [grads[s, mine, h * HD : (h + 1) * HD] for h in range(heads)], axis=0
            )
            delta = jnp.sum(grad.astype(f32) * attended[s, b], axis=1, keepdims=True)
            log_total = logs[s, b]

            def step(i, query_grad):
                first = pl.multiple_of(i * CHUNK, CHUNK)
                keys = kv[s, pl.ds(first, CHUNK), :HD]
                values = kv[s, pl.ds(first, CHUNK), HD:]
                scores = dot(q, keys, 1, 1) * SCALE
                key_place = first + lax.broadcasted_iota(jnp.int32, scores.shape, 1)
                seen = (key_place >= start) & (key_place <= place)
                weights = jnp.where(seen, jnp.exp(scores - log_total), 0.0)
                weight_grad = dot(grad, values, 1, 1)
                score_grad = (weights * (weight_grad - delta)).astype(bf16)
                kv_sum[s, pl.ds(first, CHUNK), :HD] += dot(score_grad, q, 0, 0)
                kv_sum[s, pl.ds(first, CHUNK), HD:] += dot(weights.astype(bf16), grad, 0, 0)
                return query_grad + dot(score_grad, keys, 1, 0)

            at = 4 * s + 2 * b
            query_grad = lax.fori_loop(
                range_ref[at], range_ref[at + 1], step, jnp.zeros((heads * half, HD), f32)
            )
            cos_b, sin_b = cos[s, mine, :] * SCALE, sin[s, mine, :] * SCALE
            for h in range(heads):
                z = query_grad[h * half : (h + 1) * half]
                z = z * cos_b - pltpu.roll(z, HD // 2, 1) * sin_b
                query_out[s, mine, h * HD : (h + 1) * HD] = z.astype(bf16)

    def give(chip, carry):
        for s in range(2):
            for b in range(2):
                block = chip if b == 0 else 2 * chips - 1 - chip
                place = pl.multiple_of(block * half, half)
                mine = slice(b * half, (b + 1) * half)
                source = kv_sum[s, pl.ds(place, half), :]
                kv_out[chip % 8, chip // 8, s, mine, :HD] = (source[:, :HD] * SCALE).astype(bf16)
                kv_out[chip % 8, chip // 8, s, mine, HD:] = source[:, HD:].astype(bf16)
        return carry

    lax.fori_loop(0, chips, give, 0)


def attend_back(
    ranges, branch_own, branch_other, weight, queries, kv, attended, logs, starts, places, cos, sin
):
    _, heads, rows, _ = queries.shape
    keys = kv.shape[1]
    chips = keys // rows
    return pl.pallas_call(
        functools.partial(attend_back_kernel, heads),
        out_shape=[
            jax.ShapeDtypeStruct((2, rows, heads * HD), bf16),
            jax.ShapeDtypeStruct((8, chips // 8, 2, rows, 2 * HD), bf16),
        ],
        in_specs=[SMEM] + [VMEM] * 11,
        out_specs=[VMEM] * 2,
        scratch_shapes=[
            pltpu.VMEM((2, rows, heads * HD), bf16),
            pltpu.VMEM((2, keys, 2 * HD), f32),
        ],
        compiler_params=BIG,
        name="attend_back",
    )(
        ranges,
        branch_own,
        branch_other,
        weight,
        queries,
        kv,
        attended,
        logs,
        starts,
        places,
        cos,
        sin,
    )


def on_device(
    tokens, cotangent, doc_lengths, norm_attn, w_qkv, b_qkv, w_out, norm_mlp, w_gate, w_up, w_down
):
    ctx_size = lax.axis_size("ctx")
    chip = lax.axis_index("ctx")
    core = lax.axis_index("wshard")
    where = jnp.stack([chip, core]).astype(jnp.int32)
    high = high_bits()
    groups = ctx_size // 8
    tok_dev, width = tokens.shape[1], tokens.shape[2]
    ff = w_gate.shape[1]
    ff_own = ff // 8
    heads = H // KVH
    hq = heads * HD
    rows_dev = w_qkv.shape[0]
    cuts = row_parts(tok_dev)
    half = tok_dev // 2
    flips = [relative_flips(high + order) for order in ORDERS]
    group_flips = relative_flips(group_bits())
    low, middle, upper = member_bits()

    n_gain, n_bias = norm_attn.shape[0], b_qkv.shape[0]
    small = jnp.concatenate([norm_attn, b_qkv, norm_mlp])[None]
    small = jnp.pad(small, ((0, 15), (hq, 2 * HD - small.shape[1])))
    qkv_send = jnp.concatenate([head_columns(w_qkv, 1 - core), small])
    qkv_own = jnp.concatenate([head_columns(w_qkv, core), small])
    token_own, out_grad_b = tokens[0], cotangent[0]
    out_t = w_out.T
    qkv_other = core_swap(qkv_send)
    token_other = core_swap(token_own)
    length_other = core_swap(doc_lengths[0])
    out_other = core_swap(half_of(out_t, 1 - core, 1))
    down_found = gather_list(w_down, group_bits())
    length_pair = jnp.stack([doc_lengths[0], length_other])
    qkv_pair = jnp.stack([qkv_own, qkv_other])[None]
    qkv_pair, w_gate, out_other = together(qkv_pair, w_gate, out_other)
    out_pair = by_core(half_of(out_t, core, 1), out_other, core)
    out_w = lax.all_gather(out_pair, "ctx", axis=0, tiled=False).reshape(width, hq)
    out_grad_all = lax.all_gather(
        after(out_grad_b, out_w), "ctx", axis=0, tiled=True, axis_index_groups=group_lists()
    )
    qkv_pair = gather_relative(qkv_pair, high)
    packed = pack_members(w_gate, w_up)
    qkv_pair, packed, down_found = together(qkv_pair, packed, down_found)
    column_cuts = ((0, hq // 2, rows_dev), (hq // 2, hq, rows_dev), (hq, hq + 2 * HD, rows_dev + 16))
    qkv_parts = [qkv_pair[:, :, :rows, start:stop] for start, stop, rows in column_cuts]
    qkv_parts = doubled(qkv_parts, [order[0] for order in ORDERS])
    down_other = [core_swap(x) for x in down_found]
    qkv_parts = doubled(qkv_parts, [order[1] for order in ORDERS])
    qkv_parts = with_arrived(qkv_parts, [order[2] for order in ORDERS])
    qkv_parts, packed = together(qkv_parts, packed)
    row_cut = rows_dev // 3
    first_rows, later_rows = packed[:, :row_cut], packed[:, row_cut:]
    first_rows = group_exchange(first_rows)

    inner = jnp.arange(tok_dev, dtype=jnp.int32)
    blocks = jnp.where(inner < half, chip, 2 * ctx_size - 1 - chip)
    places = (blocks * half + inner % half).astype(jnp.int32)
    ends = jnp.cumsum(length_pair, axis=1)
    passed = ends[:, None, :] <= places[None, :, None]
    starts = jnp.sum(jnp.where(passed, length_pair[:, None, :], 0), axis=2)
    places = jnp.broadcast_to(places[None], starts.shape)
    frequency = ROPE_BASE ** (-jnp.arange(HD // 2, dtype=f32) * 2.0 / HD)
    angles = (places - starts).astype(f32)[..., None] * frequency
    cos_half, sin_half = jnp.cos(angles), jnp.sin(angles)
    cos = jnp.concatenate([cos_half, cos_half], axis=-1)
    sin = jnp.concatenate([-sin_half, sin_half], axis=-1)
    first = jnp.min(starts.reshape(2, 2, half), axis=2) // CHUNK
    last = jnp.max(places.reshape(2, 2, half), axis=2) // CHUNK + 1
    ranges = jnp.stack([first, last], axis=-1).reshape(-1).astype(jnp.int32)
    starts, places = starts[..., None], places[..., None]

    if rows_dev % 16:
        qkv_w, small_all = order_weights(qkv_parts, flips, where)
        qkv_w = qkv_w.reshape(width, hq + 2 * HD)
        small_all = small_all.reshape(2 * ctx_size, 2 * HD)
        gain_one = small_all[:, :n_gain].reshape(1, -1)
        bias = small_all[:, n_gain : n_gain + n_bias].reshape(1, -1)
        gain_two = small_all[:, n_gain + n_bias : 2 * n_gain + n_bias].reshape(1, -1)
        bias = head_columns(bias, core)
        normed_one, queries, kv_own = project(token_own, token_other, gain_one, qkv_w, bias, cos, sin)
    else:
        normed_one, queries, kv_own, qkv_w, gains = order_project(
            where, token_own, token_other, cos, sin, qkv_parts, flips, n_gain, n_bias, rows_dev
        )
        gain_one, gain_two = gains[:1], gains[1:]
    kv_own = gather_relative(kv_own[None], high)
    kv_own, first_rows = together(kv_own, first_rows)

    kv_parts = [kv_own[:, :, start:stop] for start, stop in cuts]
    for step in range(2):
        kv_parts = doubled(kv_parts, [order[step] for order in ORDERS])
    down = order_rows([x[None] for x in down_found], [x[None] for x in down_other], group_flips, where)
    down = down.reshape(ff_own, width)
    kv_parts = with_arrived(kv_parts, [order[2] for order in ORDERS])
    kv_parts, down, later_rows, first_rows = together(kv_parts, down, later_rows, first_rows)
    later_rows = group_exchange(later_rows)
    kv, attended, attended_b, logs, branch = attend(
        where, ranges, queries, starts, places, out_w, kv_parts, flips, cuts
    )
    branch_other = core_swap(branch[1])
    branch_other, later_rows, first_rows = together(branch_other, later_rows, first_rows)
    packed = jnp.concatenate([first_rows, later_rows], axis=1)
    shares = ((0, 4), (4, 8))
    packed_found = [gather_list(packed[:4], group_bits())]
    packed_other = core_swap(packed)
    inputs = token_own.astype(f32)
    hidden_res = inputs + branch[0] + branch_other
    scale_two = lax.rsqrt(jnp.mean(hidden_res * hidden_res, axis=-1, keepdims=True) + EPSILON)
    normed_two = (hidden_res * scale_two * gain_two).astype(bf16)

    group_orders = ((upper, middle, low), (upper, low, middle))
    group_cuts = ((0, half), (half, tok_dev))
    token_parts = gather_relative(normed_two[None], (upper,))
    token_parts, packed, packed_found = together(token_parts, packed, packed_found)
    token_parts = [token_parts[:, start:stop] for start, stop in group_cuts]
    token_parts = doubled(token_parts, [order[1] for order in group_orders])
    packed_found.append(gather_list(packed[4:], group_bits()))
    token_parts, out_grad_all = together(token_parts, out_grad_all)
    token_parts = with_arrived(token_parts, [order[2] for order in group_orders])
    token_parts, packed_found = together(token_parts, packed_found)
    token_flips = [relative_flips(order) for order in group_orders]
    normed_all = order_tokens(token_parts, token_flips, group_cuts, groups, where)
    normed_all = normed_all.reshape(8 * tok_dev, width)

    sources, loads = [packed, packed_other], [(0, 0, 0), (0, 1, 0)]
    for found, (first, _) in zip(packed_found, shares):
        for piece, flip in list(zip(found, group_flips))[1:]:
            sources.extend([piece, core_swap(piece)])
            loads.extend([(flip, 0, first), (flip, 1, first)])
    if rows_dev % 16:
        own, other = [], []
        for flip in group_flips:
            for core_flip, side in enumerate((own, other)):
                found = [x for x, load in zip(sources, loads) if load[:2] == (flip, core_flip)]
                side.append(jnp.concatenate(found))
        sources, loads = [order_rows(own, other, group_flips, where).reshape(width, -1)], [(None, 0, 0)]
    out_grad = out_grad_b.astype(f32)
    pre_grad, activated, normed_grad_part = mlp(
        where, groups, normed_all, out_grad_all, down, sources, loads
    )

    normed_grad_part = normed_grad_part.reshape(2, 2, 2, tok_dev, width)
    scatter = Scatter(
        [normed_grad_part[:, :, :, start:stop] for start, stop in group_cuts], (upper, middle, low)
    )
    bits = [order[2] for order in group_orders]
    kept, sent = scatter.split(bits)
    gate_keep, gate_send = gate_up_grads(normed_all, after(pre_grad, *sent), 0, rows_dev, where)
    gate_arrived = core_swap(gate_send)
    branch_part = dot(after(activated, gate_send), down, 1, 0).astype(bf16)
    scatter.step(bits, kept, sent)
    scatter.parts, gate_arrived, branch_part = together(scatter.parts, gate_arrived, branch_part)

    def of_cores(keep, arrived):
        total = (keep.astype(f32) + arrived.astype(f32)).astype(bf16)
        return total.reshape(8, groups, rows_dev, -1)

    def of_group(total):
        return sum_over(total, 1, tuple(reversed(group_bits()))).astype(bf16)

    bits = [order[1] for order in group_orders]
    kept, sent = scatter.split(bits)
    gate_total = of_cores(gate_keep, gate_arrived)
    scatter.step(bits, kept, sent)
    scatter.parts, gate_total, pre_grad = together(scatter.parts, gate_total, pre_grad)

    kept, sent = scatter.split((upper, upper))
    grad_gate = of_group(gate_total)
    up_keep, up_send = gate_up_grads(normed_all, after(pre_grad, *sent), 1, rows_dev, where)
    branch_part = branch_part.reshape(2, 2, 2, tok_dev, width)
    branch_sums = Scatter(
        [branch_part[:, :, :, start:stop] for start, stop in group_cuts], (upper, middle, low)
    )
    bits = [order[2] for order in group_orders]
    branch_kept, branch_sent = branch_sums.split(bits)
    scatter.step((upper, upper), kept, sent)
    branch_arrived = [chip_swap(x, 1 << bit) for x, bit in zip(branch_sent, bits)]
    scatter.parts, grad_gate, up_send = together(scatter.parts, grad_gate, up_send)
    grad_gate = group_exchange(grad_gate)
    up_arrived = core_swap(up_send)
    normed_two_grad = jnp.concatenate(scatter.parts)
    gain_two_grad = jnp.sum(normed_two_grad * hidden_res * scale_two, axis=0)
    hidden_grad = out_grad + rms_back(normed_two_grad, hidden_res, scale_two, gain_two)

    falling = tuple(reversed(group_bits()))
    def weight_parts(x):
        return x.astype(bf16).reshape(ctx_size // 8, 8, 2, rows_dev, x.shape[1])

    branch_own = hidden_grad.astype(bf16)
    branch_other = core_swap(branch_own)
    branch_own, branch_other, up_arrived, branch_arrived = together(
        branch_own, branch_other, up_arrived, branch_arrived
    )
    grad_up = of_group(of_cores(up_keep, up_arrived))
    project_grad_q, kv_grad = attend_back(
        ranges, branch_own, branch_other, out_w, queries, kv, attended, logs, starts, places, cos, sin
    )
    (kv_grad, project_grad_q), grad_gate, grad_up, activated = together(
        (kv_grad, project_grad_q), grad_gate, grad_up, activated
    )
    kv_sum = cube_exchange(kv_grad)
    down_keep, down_send = down_grads(activated, out_grad_all, groups, where)
    branch_grad = jnp.concatenate([branch_own, branch_other])
    normed_one = normed_one.reshape(-1, width)
    project_grad_q = project_grad_q.reshape(-1, hq)
    grad_out_part = weight_parts(dot(branch_grad, attended_b.reshape(-1, hq), 0, 0))
    grad_q_part = weight_parts(dot(normed_one, project_grad_q, 0, 0))
    names = tuple(reversed(high)) + (2, 1, 0)
    wide_parts = [
        x.reshape((2,) * len(names) + x.shape[2:]) for x in (grad_q_part, grad_out_part)
    ]
    scatter = Scatter(wide_parts, names)
    bits = (0, 1)
    kept, sent = scatter.split(bits)
    arrived = [chip_swap(x, 1 << bit) for x, bit in zip(sent, bits)]
    kv_sum, down_send, branch_arrived = together(kv_sum, down_send, branch_arrived)

    kv_sum = jnp.sum(kv_sum.astype(f32), axis=0).astype(bf16)
    kv_sum = sum_over_high(kv_sum, high)
    down_arrived = core_swap(down_send)
    kv_sum, arrived, grad_up = together(kv_sum, arrived, grad_up)
    grad_up = group_exchange(grad_up)
    key_pre = kv_sum[..., :HD]
    key_pre = key_pre * cos - jnp.roll(key_pre, HD // 2, axis=-1) * sin
    project_grad_kv = jnp.concatenate([key_pre, kv_sum[..., HD:]], axis=-1).astype(bf16)
    project_grad_kv = project_grad_kv.reshape(-1, 2 * HD)
    grad_kv = weight_parts(dot(normed_one, project_grad_kv, 0, 0)).swapaxes(0, 1)
    project_grad = jnp.concatenate([project_grad_q, project_grad_kv], axis=1)
    normed_one_grad = dot(project_grad, qkv_w, 1, 1)
    normed_one_grad = normed_one_grad[:tok_dev] + core_swap(normed_one_grad[tok_dev:])
    scatter.add(kept, arrived)
    branch_sums.add(branch_kept, branch_arrived)
    branch_sums.step([order[1] for order in group_orders])
    down_sum = (down_keep.astype(f32) + down_arrived.astype(f32)).astype(bf16)
    grad_kv, grad_up, scatter.parts, branch_sums.parts, down_sum, normed_one_grad = together(
        grad_kv, grad_up, scatter.parts, branch_sums.parts, down_sum, normed_one_grad
    )
    grad_kv = cube_exchange(grad_kv)
    branch_sums.parts = [jnp.concatenate(branch_sums.parts, axis=-2)]
    branch_sums.step((upper,))
    scatter.step((2, 0))
    scatter.step((1, 2))
    scatter.parts = [jnp.concatenate(scatter.parts, axis=-1)]
    scale_one = lax.rsqrt(jnp.mean(inputs * inputs, axis=-1, keepdims=True) + EPSILON)
    gain_one_grad = jnp.sum(normed_one_grad * inputs * scale_one, axis=0)
    input_grad = hidden_grad + rms_back(normed_one_grad, inputs, scale_one, gain_one)

    def whole_columns(x):
        return jnp.concatenate(
            [
                x[0, :, :hq],
                x[1, :, :hq],
                x[0, :, hq : hq + HD],
                x[1, :, hq : hq + HD],
                x[0, :, hq + HD : hq + 2 * HD],
                x[1, :, hq + HD : hq + 2 * HD],
            ],
            axis=1,
        )

    bias_grad = jnp.sum(project_grad.astype(f32), axis=0, keepdims=True)
    zeros = jnp.zeros_like(bias_grad)
    bias_full = whole_columns(
        jnp.stack([jnp.where(core == 0, bias_grad, zeros), jnp.where(core == 0, zeros, bias_grad)])
    )[0]
    qk_width = (H + KVH) * HD
    sums = jnp.concatenate(
        [
            x.reshape(ctx_size, 1, -1)
            for x in (gain_one_grad, gain_two_grad, bias_full[:qk_width], bias_full[qk_width:])
        ],
        axis=2,
    )
    grad_kv, scatter.parts, branch_sums.parts, sums, down_sum = together(
        grad_kv, scatter.parts, branch_sums.parts, sums, down_sum
    )
    sums = lax.all_to_all(sums, "ctx", split_axis=0, concat_axis=0, tiled=True)
    grad_kv = jnp.sum(grad_kv.astype(f32), axis=0).astype(bf16)
    grad_kv = sum_over_high(grad_kv, high)
    grad_down = sum_over(down_sum, 0, falling)
    for bit in reversed(high):
        scatter.step((bit,))
    scattered = scatter.parts[0]
    sums = jnp.sum(sums, axis=0)
    sums = (sums + core_swap(sums))[0]
    output = (hidden_res + branch_sums.parts[0]).astype(bf16)

    grad_gate, grad_up = unpack_members(grad_gate, grad_up, ff)
    chip_grad = jnp.concatenate([scattered[..., :hq], grad_kv, scattered[..., hq:]], axis=-1)

    def pick(x, which):
        return lax.dynamic_index_in_dim(x, which, 0, keepdims=False)

    pair = by_core(pick(chip_grad, core), core_swap(pick(chip_grad, 1 - core)), core)
    grad_qkv = whole_columns(pair)
    grad_out = pair[:, :, hq + 2 * HD :].transpose(1, 0, 2).reshape(-1, 2 * hq).T

    def owned(start, size):
        return lax.dynamic_slice_in_dim(sums, start + core * (size // 2), size // 2, 0)

    own_width, own_qk, own_v = width // ctx_size, qk_width // ctx_size, KVH * HD // ctx_size
    return (
        output[None],
        input_grad[None],
        owned(0, own_width),
        grad_qkv,
        owned(2 * own_width, own_qk),
        owned(2 * own_width + own_qk, own_v),
        grad_out,
        owned(own_width, own_width),
        grad_gate,
        grad_up,
        grad_down,
    )


def solution(mesh):
    whole = ("ctx", "wshard")
    rows, columns, flat = P(whole, None), P(None, whole), P(whole)
    tokens = P("wshard", "ctx", None)
    return jax.shard_map(
        on_device,
        mesh=mesh,
        in_specs=(tokens, tokens, P("wshard", None), flat, rows, flat, columns, flat, rows, rows, rows),
        out_specs=(tokens, tokens, flat, rows, flat, flat, columns, flat, rows, rows, rows),
        check_vma=False,
    )
```

```python
import functools
import math

import jax
import jax.numpy as jnp
from jax import lax
from jax.experimental import pallas as pl
from jax.experimental.pallas import tpu as pltpu
from jax.sharding import PartitionSpec as P

H = 12
KVH = 2
HD = 128
EPSILON = 1e-06
ROPE_BASE = 1000000.0
ORDERS = ((0, 1, 2), (1, 2, 0), (2, 0, 1))
CHUNK = 512
NEVER = -1e30
SCALE = 1.0 / math.sqrt(HD)
bf16 = jnp.bfloat16
f32 = jnp.float32
VMEM = pl.BlockSpec(memory_space=pltpu.VMEM)
SMEM = pl.BlockSpec(memory_space=pltpu.SMEM)
BIG = pltpu.CompilerParams(vmem_limit_bytes=56 * 1024 * 1024)


def after(x, *others):
    return together(x, *others)[0]


def together(*groups):
    flat, tree = jax.tree.flatten(groups)
    return jax.tree.unflatten(tree, lax.optimization_barrier(flat))


def core_swap(x):
    return lax.ppermute(x, "wshard", [(0, 1), (1, 0)])


def chip_swap(x, flip):
    count = lax.axis_size("ctx")
    return lax.ppermute(x, "ctx", [(i, i ^ flip) for i in range(count)])


def cubes():
    count = lax.axis_size("ctx")
    return [list(range(i, i + 8)) for i in range(0, count, 8)]


def cube_exchange(x):
    return lax.all_to_all(
        x, "ctx", split_axis=0, concat_axis=0, tiled=True, axis_index_groups=cubes()
    )


def group_bits():
    return tuple(range(lax.axis_size("ctx").bit_length() - 4))


def member_bits():
    first = len(group_bits())
    return (first, first + 1, first + 2)


def group_lists():
    groups = lax.axis_size("ctx") // 8
    return [[g + groups * m for m in range(8)] for g in range(groups)]


def group_exchange(x):
    return lax.all_to_all(
        x, "ctx", split_axis=0, concat_axis=0, tiled=True, axis_index_groups=group_lists()
    )


def high_bits():
    return tuple(range(3, lax.axis_size("ctx").bit_length() - 1))


def my_bit(bit):
    return (lax.axis_index("ctx") >> bit) & 1


def gather_relative(x, bits):
    for bit in bits:
        x = jnp.concatenate([x, chip_swap(x, 1 << bit)], axis=0)
    return x


def gather_list(x, bits):
    found = [x]
    for bit in bits:
        found = found + [chip_swap(y, 1 << bit) for y in found]
    return found


def relative_flips(bits):
    flips = [0]
    for bit in bits:
        flips = flips + [f ^ (1 << bit) for f in flips]
    return flips


def sum_over(x, axis, bits):
    for at, bit in enumerate(bits):
        shape = x.shape
        x = x.reshape(shape[:axis] + (2, shape[axis] // 2) + shape[axis + 1 :])
        keep = lax.dynamic_index_in_dim(x, my_bit(bit), axis, keepdims=False)
        send = lax.dynamic_index_in_dim(x, 1 - my_bit(bit), axis, keepdims=False)
        x = keep.astype(f32) + chip_swap(send.astype(bf16), 1 << bit).astype(f32)
        if at < len(bits) - 1:
            x = x.astype(bf16)
    return jnp.squeeze(x, axis).astype(f32)


def sum_over_high(x, high):
    return sum_over(x, 0, tuple(reversed(high)))


def row_parts(rows):
    third = rows * 3 // 8
    return ((0, third), (third, 2 * third), (2 * third, rows))


def doubled(parts, bits):
    return [jnp.concatenate([x, chip_swap(x, 1 << bit)]) for x, bit in zip(parts, bits)]


def with_arrived(parts, bits):
    found = []
    for x, bit in zip(parts, bits):
        found.extend([x, chip_swap(x, 1 << bit)])
    return found


def both_halves(x, layout, bit):
    axis = layout.index(bit)
    keep = lax.dynamic_index_in_dim(x, my_bit(bit), axis, keepdims=False)
    send = lax.dynamic_index_in_dim(x, 1 - my_bit(bit), axis, keepdims=False)
    return keep, send


class Scatter:
    def __init__(self, parts, layout):
        self.parts = list(parts)
        self.layouts = [list(layout) for _ in self.parts]

    def split(self, bits):
        pairs = [both_halves(x, l, b) for x, l, b in zip(self.parts, self.layouts, bits)]
        for layout, bit in zip(self.layouts, bits):
            layout.remove(bit)
        return [k for k, _ in pairs], [s.astype(bf16) for _, s in pairs]

    def step(self, bits, kept=None, sent=None):
        if kept is None:
            kept, sent = self.split(bits)
        self.add(kept, [chip_swap(x, 1 << bit) for x, bit in zip(sent, bits)])

    def add(self, kept, arrived):
        self.parts = [k.astype(f32) + a.astype(f32) for k, a in zip(kept, arrived)]
        if self.layouts[0]:
            self.parts = [x.astype(bf16) for x in self.parts]


def dot(left, right, left_axis, right_axis):
    return lax.dot_general(
        left, right, (((left_axis,), (right_axis,)), ((), ())), preferred_element_type=f32
    )


def rms_back(grad_in, values, scale_rows, gain_row):
    weighted = grad_in * gain_row
    return scale_rows * weighted - values * scale_rows**3 * jnp.mean(
        weighted * values, axis=-1, keepdims=True
    )


def half_of(x, which, axis):
    size = x.shape[axis] // 2
    return lax.dynamic_slice_in_dim(x, which * size, size, axis)


def head_columns(x, core):
    q_width, kv_width = H * HD, KVH * HD
    return jnp.concatenate(
        [
            half_of(x[:, :q_width], core, 1),
            half_of(x[:, q_width : q_width + kv_width], core, 1),
            half_of(x[:, q_width + kv_width :], core, 1),
        ],
        axis=1,
    )


def by_core(mine, other, core):
    return jnp.stack([jnp.where(core == 0, mine, other), jnp.where(core == 0, other, mine)])


def order_weights_kernel(flips, extra_rows, where_ref, *refs):
    parts, out = refs[: 2 * len(flips)], refs[2 * len(flips)]
    chip, core = where_ref[0], where_ref[1]
    count, rows = parts[0].shape[0], out.shape[2]
    at = 0
    for p, part_flips in enumerate(flips):
        columns = parts[2 * p].shape[3]
        for k, flip in enumerate(part_flips):
            part = parts[2 * p + k // count]
            for h in range(2):
                out[chip ^ flip, core ^ h, :, at : at + columns] = part[k % count, h, :rows]
                if extra_rows and p == len(flips) - 1:
                    extra = part[k % count, h, rows:].astype(f32)[:1]
                    refs[-1][chip ^ flip, core ^ h] = extra
        at += columns


def order_weights(parts, flips, where):
    count, _, rows, _ = parts[0].shape
    columns = sum(p.shape[3] for p in parts[::2])
    extra = parts[-1].shape[2] > rows
    shapes = [jax.ShapeDtypeStruct((2 * count, 2, rows, columns), bf16)]
    if extra:
        shapes.append(jax.ShapeDtypeStruct((2 * count, 2, 1, parts[-1].shape[3]), f32))
    return pl.pallas_call(
        functools.partial(order_weights_kernel, flips, extra),
        out_shape=shapes,
        in_specs=[SMEM] + [VMEM] * len(parts),
        out_specs=[VMEM] * len(shapes),
        compiler_params=BIG,
        name="order_weights",
    )(where, *parts)


def order_rows_kernel(flips, where_ref, *refs):
    out = refs[-1]
    chip, core = where_ref[0], where_ref[1]
    group = chip % len(flips)
    for k, flip in enumerate(flips):
        out[:, group ^ flip, core] = refs[k][...]
        out[:, group ^ flip, 1 - core] = refs[len(flips) + k][...]


def order_rows(own, other, flips, where):
    members, rows, columns = own[0].shape
    groups = len(own)
    tile = columns // 2 if columns % 256 == 0 else columns
    source = pl.BlockSpec((1, rows, tile), lambda m, n: (m, 0, n))
    return pl.pallas_call(
        functools.partial(order_rows_kernel, flips),
        grid=(members, columns // tile),
        out_shape=jax.ShapeDtypeStruct((members, groups, 2, rows, columns), bf16),
        in_specs=[SMEM] + [source] * (2 * groups),
        out_specs=pl.BlockSpec((1, groups, 2, rows, tile), lambda m, n: (m, 0, 0, 0, n)),
        compiler_params=BIG,
        name="order_rows",
    )(where, *own, *other)


def order_tokens_kernel(flips, cuts, groups, where_ref, *refs):
    out = refs[-1]
    member = where_ref[0] // groups
    for p, (start, stop) in enumerate(cuts):
        for k, flip in enumerate(flips[p]):
            half = refs[2 * p + k // 4]
            out[member ^ (flip // groups), start:stop, :] = half[k % 4]


def order_tokens(halves, flips, cuts, groups, where):
    rows, width = cuts[-1][1], halves[0].shape[2]
    return pl.pallas_call(
        functools.partial(order_tokens_kernel, flips, cuts, groups),
        out_shape=jax.ShapeDtypeStruct((8, rows, width), bf16),
        in_specs=[SMEM] + [VMEM] * len(halves),
        out_specs=VMEM,
        compiler_params=BIG,
        name="order_tokens",
    )(where, *halves)


def padded(ff_own):
    return -(-ff_own // 128) * 128


def pack_members_kernel(gate, up, out):
    own, wide = gate.shape[1] // 8, out.shape[2] // 2
    for m in range(8):
        for at, source in ((0, gate), (wide, up)):
            out[m, :, at : at + own] = source[:, m * own : (m + 1) * own]
            out[m, :, at + own : at + wide] = jnp.zeros((out.shape[1], wide - own), bf16)


def pack_members(gate, up):
    rows, ff = gate.shape
    return pl.pallas_call(
        pack_members_kernel,
        out_shape=jax.ShapeDtypeStruct((8, rows, 2 * padded(ff // 8)), bf16),
        in_specs=[VMEM] * 2,
        out_specs=VMEM,
        compiler_params=BIG,
        name="pack_members",
    )(gate, up)


def unpack_members_kernel(packed_gate, packed_up, gate, up):
    own = gate.shape[1] // 8
    for m in range(8):
        for packed, target in ((packed_gate, gate), (packed_up, up)):
            target[:, m * own : (m + 1) * own] = packed[m, :, :own].astype(f32)


def unpack_members(packed_gate, packed_up, ff):
    rows = packed_gate.shape[1]
    return pl.pallas_call(
        unpack_members_kernel,
        out_shape=[jax.ShapeDtypeStruct((rows, ff), f32)] * 2,
        in_specs=[VMEM] * 2,
        out_specs=[VMEM] * 2,
        compiler_params=BIG,
        name="unpack_members",
    )(packed_gate, packed_up)


def mlp_kernel(loads, groups, where_ref, normed, out_grad, down, *refs):
    sources = refs[: len(loads)]
    pre_grad, activated, normed_grad, gate_up, arrived = refs[len(loads) :]
    chip, core = where_ref[0], where_ref[1]

    @pl.when(pl.program_id(0) == 0)
    def _():
        copies = []
        for source, (flip, other, first) in zip(sources, loads):
            if flip is None:
                copies.append(pltpu.make_async_copy(source, gate_up, arrived.at[len(copies)]))
                continue
            rows = source.shape[1]
            for i in range(source.shape[0]):
                device = 2 * ((first + i) * groups + (chip % groups ^ flip)) + (core ^ other)
                target = gate_up.at[pl.ds(pl.multiple_of(device * rows, 16), rows), :]
                copies.append(pltpu.make_async_copy(source.at[i], target, arrived.at[len(copies)]))
        for copy in copies:
            copy.start()
        for copy in copies:
            copy.wait()

    ff_own = down.shape[0]
    wide = gate_up.shape[1] // 2
    gates, ups = slice(0, ff_own), slice(wide, wide + ff_own)
    n = normed[...]
    gate = dot(n, gate_up[:, gates], 1, 0)
    up = dot(n, gate_up[:, ups], 1, 0)
    act_grad = dot(out_grad[...], down[...], 1, 1)
    sig = jax.nn.sigmoid(gate)
    act = gate * sig
    activated[...] = (act * up).astype(bf16)
    if wide > ff_own:
        gap = jnp.zeros((n.shape[0], wide - ff_own), bf16)
        pre_grad[:, ff_own:wide] = gap
        pre_grad[:, wide + ff_own :] = gap
    pre_grad[:, gates] = (act_grad * up * sig * (1.0 + gate * (1.0 - sig))).astype(bf16)
    pre_grad[:, ups] = (act_grad * act).astype(bf16)
    normed_grad[...] = dot(pre_grad[...], gate_up[...], 1, 1).astype(bf16)


def mlp(where, groups, normed, out_grad, down, sources, loads, tile=256):
    rows, width = normed.shape
    ff_own, wide = down.shape[0], sources[0].shape[-1]
    count = sum(1 if flip is None else x.shape[0] for x, (flip, _, _) in zip(sources, loads))

    def by_rows(columns):
        return pl.BlockSpec((tile, columns), lambda i: (i, 0))

    return pl.pallas_call(
        functools.partial(mlp_kernel, loads, groups),
        grid=(rows // tile,),
        out_shape=[
            jax.ShapeDtypeStruct((rows, wide), bf16),
            jax.ShapeDtypeStruct((rows, ff_own), bf16),
            jax.ShapeDtypeStruct((rows, width), bf16),
        ],
        in_specs=[
            SMEM,
            by_rows(width),
            by_rows(width),
            pl.BlockSpec(down.shape, lambda i: (0, 0), pipeline_mode=pl.Buffered(1)),
        ]
        + [pl.BlockSpec(memory_space=pl.ANY)] * len(sources),
        out_specs=[by_rows(wide), by_rows(ff_own), by_rows(width)],
        scratch_shapes=[pltpu.VMEM((width, wide), bf16), pltpu.SemaphoreType.DMA((count,))],
        compiler_params=BIG,
        name="mlp",
    )(where, normed, out_grad, down, *sources)


def gate_up_grads_kernel(rows_dev, where_ref, normed, pre_grad, keep, send):
    grads = dot(normed[...], pre_grad[...], 0, 0)
    core = where_ref[1]
    for i in range(keep.shape[0]):
        low = grads[2 * i * rows_dev : (2 * i + 1) * rows_dev].astype(bf16)
        upper = grads[(2 * i + 1) * rows_dev : (2 * i + 2) * rows_dev].astype(bf16)
        keep[i] = jnp.where(core == 0, low, upper)
        send[i] = jnp.where(core == 0, upper, low)


def gate_up_grads(normed, pre_grad, side, rows_dev, where, tile=384):
    rows, width = normed.shape
    wide = pre_grad.shape[1] // 2
    chips, step = width // (2 * rows_dev), tile // (2 * rows_dev)
    result = pl.BlockSpec((step, rows_dev, wide), lambda i: (i, 0, 0))
    return pl.pallas_call(
        functools.partial(gate_up_grads_kernel, rows_dev),
        grid=(width // tile,),
        out_shape=[jax.ShapeDtypeStruct((chips, rows_dev, wide), bf16)] * 2,
        in_specs=[
            SMEM,
            pl.BlockSpec((rows, tile), lambda i: (0, i)),
            pl.BlockSpec((rows, wide), lambda i: (0, side), pipeline_mode=pl.Buffered(1)),
        ],
        out_specs=[result] * 2,
        compiler_params=BIG,
        name="gate_up_grads",
    )(where, normed, pre_grad)


def down_grads_kernel(where_ref, activated, out_grad, keep, send):
    grads = dot(activated[...], out_grad[...], 0, 0)
    core = where_ref[1]
    rows_dev = keep.shape[1]
    for i in range(keep.shape[0]):
        low = grads[2 * i * rows_dev : (2 * i + 1) * rows_dev].astype(bf16)
        upper = grads[(2 * i + 1) * rows_dev : (2 * i + 2) * rows_dev].astype(bf16)
        keep[i] = jnp.where(core == 0, low, upper)
        send[i] = jnp.where(core == 0, upper, low)


def down_grads(activated, out_grad, groups, where, tile=512):
    rows, ff_own = activated.shape
    width = out_grad.shape[1]
    rows_dev = ff_own // (2 * groups)
    result = pl.BlockSpec((groups, rows_dev, tile), lambda i: (0, 0, i))
    return pl.pallas_call(
        down_grads_kernel,
        grid=(width // tile,),
        out_shape=[jax.ShapeDtypeStruct((groups, rows_dev, width), bf16)] * 2,
        in_specs=[
            SMEM,
            pl.BlockSpec((rows, ff_own), lambda i: (0, 0), pipeline_mode=pl.Buffered(1)),
            pl.BlockSpec((rows, tile), lambda i: (0, i)),
        ],
        out_specs=[result] * 2,
        compiler_params=BIG,
        name="down_grads",
    )(where, activated, out_grad)


def project_streams(heads, own, other, gain, weight, bias, cos, sin, normed, queries, kv):
    hq = heads * HD
    for s, tokens in enumerate((own, other)):
        x = tokens[...].astype(f32)
        scale = lax.rsqrt(jnp.mean(x * x, axis=-1, keepdims=True) + EPSILON)
        n = (x * scale * gain).astype(bf16)
        normed[s] = n
        cos_s, sin_s = cos[s], sin[s]
        project = dot(n, weight[...], 1, 0) + bias

        def turn(z):
            return z * cos_s + pltpu.roll(z, HD // 2, 1) * sin_s

        for h in range(heads):
            queries[s, h] = turn(project[:, h * HD : (h + 1) * HD]).astype(bf16)
        kv[s, :, :HD] = turn(project[:, hq : hq + HD]).astype(bf16)
        kv[s, :, HD:] = project[:, hq + HD :].astype(bf16)


def project_kernel(heads, own, other, gain, weight, bias, cos, sin, normed, queries, kv):
    project_streams(
        heads, own, other, gain[...], weight, bias[...], cos, sin, normed, queries, kv
    )


def project(own, other, gain, weight, bias, cos, sin):
    rows, width = own.shape
    heads = H // KVH
    return pl.pallas_call(
        functools.partial(project_kernel, heads),
        out_shape=[
            jax.ShapeDtypeStruct((2, rows, width), bf16),
            jax.ShapeDtypeStruct((2, heads, rows, HD), bf16),
            jax.ShapeDtypeStruct((2, rows, 2 * HD), bf16),
        ],
        in_specs=[VMEM] * 7,
        out_specs=[VMEM] * 3,
        compiler_params=BIG,
        name="project",
    )(own, other, gain, weight, bias, cos, sin)


def order_project_kernel(
    heads, flips, n_gain, n_bias, rows, where_ref, own, other, cos, sin, *refs
):
    parts = refs[: 2 * len(flips)]
    normed, queries, kv, weight, gains, small, line = refs[2 * len(flips) :]
    chip, core = where_ref[0], where_ref[1]
    count = parts[0].shape[0]
    at = 0
    for p, part_flips in enumerate(flips):
        columns = parts[2 * p].shape[3]
        for k, flip in enumerate(part_flips):
            part = parts[2 * p + k // count]
            for h in range(2):
                device = 2 * (chip ^ flip) + (core ^ h)
                first = pl.multiple_of(device * rows, 16)
                weight[pl.ds(first, rows), at : at + columns] = part[k % count, h, :rows]
                if p == len(flips) - 1:
                    small[pl.ds(device, 1), :] = part[k % count, h, rows:].astype(f32)[:1]
        at += columns
    devices = small.shape[0]
    total = devices * n_bias
    for d in range(devices):
        row = small[d : d + 1, :]
        gains[0:1, d * n_gain : (d + 1) * n_gain] = row[:, :n_gain]
        line[1:2, d * n_bias : (d + 1) * n_bias] = row[:, n_gain : n_gain + n_bias]
        gains[1:2, d * n_gain : (d + 1) * n_gain] = row[
            :, n_gain + n_bias : 2 * n_gain + n_bias
        ]
    hq, v = heads * HD, 2 * heads * HD + 2 * HD
    bias = jnp.where(
        core == 0,
        jnp.concatenate(
            [line[1:2, :hq], line[1:2, 2 * hq : 2 * hq + HD], line[1:2, v : v + HD]], axis=1
        ),
        jnp.concatenate(
            [line[1:2, hq : 2 * hq], line[1:2, 2 * hq + HD : v], line[1:2, v + HD : total]], axis=1
        ),
    )
    gain = gains[0:1, :]
    project_streams(heads, own, other, gain, weight, bias, cos, sin, normed, queries, kv)


def order_project(where, own, other, cos, sin, parts, flips, n_gain, n_bias, rows):
    tokens, width = own.shape
    heads = H // KVH
    columns = sum(p.shape[3] for p in parts[::2])
    devices = 4 * parts[0].shape[0]
    return pl.pallas_call(
        functools.partial(order_project_kernel, heads, flips, n_gain, n_bias, rows),
        out_shape=[
            jax.ShapeDtypeStruct((2, tokens, width), bf16),
            jax.ShapeDtypeStruct((2, heads, tokens, HD), bf16),
            jax.ShapeDtypeStruct((2, tokens, 2 * HD), bf16),
            jax.ShapeDtypeStruct((width, columns), bf16),
            jax.ShapeDtypeStruct((2, width), f32),
        ],
        in_specs=[SMEM] + [VMEM] * (4 + len(parts)),
        out_specs=[VMEM] * 5,
        scratch_shapes=[
            pltpu.VMEM((devices, parts[-1].shape[3]), f32),
            pltpu.VMEM((8, devices * n_bias), f32),
        ],
        compiler_params=BIG,
        name="order_project",
    )(where, own, other, cos, sin, *parts)


def pieces(cuts, half):
    found = []
    for p, (start, stop) in enumerate(cuts):
        for b in range(2):
            low, high = max(start, b * half), min(stop, (b + 1) * half)
            if low < high:
                found.append((p, low - start, low - b * half, high - low, b))
    return found


def attend_kernel(
    flips, cuts, heads, where_ref, range_ref, queries, starts, places, weight, *refs
):
    parts, (kv, attended, attended_b, logs, branch) = refs[: 2 * len(cuts)], refs[2 * len(cuts) :]
    chip = where_ref[0]
    rows = queries.shape[2]
    half = rows // 2
    count = parts[0].shape[0]
    chips = 2 * count
    for p, first, at, size, b in pieces(cuts, half):
        for k, flip in enumerate(flips[p]):
            part = parts[2 * p + k // count]
            source = chip ^ flip
            block = source if b == 0 else 2 * chips - 1 - source
            place = pl.multiple_of(block * half + at, 16)
            for s in range(2):
                kv[s, pl.ds(place, size), :] = part[k % count, s, first : first + size, :]

    for s in range(2):
        for b in range(2):
            mine = slice(b * half, (b + 1) * half)
            q = queries[s, :, mine, :].reshape(heads * half, HD)
            start = jnp.concatenate([starts[s, mine, :]] * heads, axis=0)
            place = jnp.concatenate([places[s, mine, :]] * heads, axis=0)

            def step(i, state):
                top, total, out = state
                first = pl.multiple_of(i * CHUNK, CHUNK)
                keys = kv[s, pl.ds(first, CHUNK), :HD]
                values = kv[s, pl.ds(first, CHUNK), HD:]
                scores = dot(q, keys, 1, 1) * SCALE
                key_place = first + lax.broadcasted_iota(jnp.int32, scores.shape, 1)
                seen = (key_place >= start) & (key_place <= place)
                scores = jnp.where(seen, scores, NEVER)
                new_top = jnp.maximum(top, jnp.max(scores, axis=1, keepdims=True))
                fade = jnp.exp(top - new_top)
                weights = jnp.exp(scores - new_top)
                total = total * fade + jnp.sum(weights, axis=1, keepdims=True)
                out = out * fade + dot(weights.astype(bf16), values, 1, 0)
                return new_top, total, out

            at = 4 * s + 2 * b
            top, total, out = lax.fori_loop(
                range_ref[at],
                range_ref[at + 1],
                step,
                (
                    jnp.full((heads * half, 1), NEVER, f32),
                    jnp.zeros((heads * half, 1), f32),
                    jnp.zeros((heads * half, HD), f32),
                ),
            )
            out = out / total
            logs[s, b] = top + jnp.log(total)
            attended[s, b] = out
            for h in range(heads):
                attended_b[s, mine, h * HD : (h + 1) * HD] = out[h * half : (h + 1) * half].astype(
                    bf16
                )
        branch[s] = dot(attended_b[s], weight[...], 1, 1)


def attend(where, ranges, queries, starts, places, weight, parts, flips, cuts):
    _, heads, rows, _ = queries.shape
    keys = 2 * parts[0].shape[0] * rows
    half = rows // 2
    return pl.pallas_call(
        functools.partial(attend_kernel, flips, cuts, heads),
        out_shape=[
            jax.ShapeDtypeStruct((2, keys, 2 * HD), bf16),
            jax.ShapeDtypeStruct((2, 2, heads * half, HD), f32),
            jax.ShapeDtypeStruct((2, rows, heads * HD), bf16),
            jax.ShapeDtypeStruct((2, 2, heads * half, 1), f32),
            jax.ShapeDtypeStruct((2, rows, weight.shape[0]), f32),
        ],
        in_specs=[SMEM] * 2 + [VMEM] * (4 + len(parts)),
        out_specs=[VMEM] * 5,
        compiler_params=BIG,
        name="attend",
    )(where, ranges, queries, starts, places, weight, *parts)


def attend_back_kernel(
    heads,
    range_ref,
    branch_own,
    branch_other,
    weight,
    queries,
    kv,
    attended,
    logs,
    starts,
    places,
    cos,
    sin,
    query_out,
    kv_out,
    grads,
    kv_sum,
):
    rows = queries.shape[2]
    half = rows // 2
    chips = kv.shape[1] // rows
    kv_sum[...] = jnp.zeros_like(kv_sum)
    for s, branch in enumerate((branch_own, branch_other)):
        grads[s] = dot(branch[...], weight[...], 1, 0).astype(bf16)
    for s in range(2):
        for b in range(2):
            mine = slice(b * half, (b + 1) * half)
            q = queries[s, :, mine, :].reshape(heads * half, HD)
            start = jnp.concatenate([starts[s, mine, :]] * heads, axis=0)
            place = jnp.concatenate([places[s, mine, :]] * heads, axis=0)
            grad = jnp.concatenate(
                [grads[s, mine, h * HD : (h + 1) * HD] for h in range(heads)], axis=0
            )
            delta = jnp.sum(grad.astype(f32) * attended[s, b], axis=1, keepdims=True)
            log_total = logs[s, b]

            def step(i, query_grad):
                first = pl.multiple_of(i * CHUNK, CHUNK)
                keys = kv[s, pl.ds(first, CHUNK), :HD]
                values = kv[s, pl.ds(first, CHUNK), HD:]
                scores = dot(q, keys, 1, 1) * SCALE
                key_place = first + lax.broadcasted_iota(jnp.int32, scores.shape, 1)
                seen = (key_place >= start) & (key_place <= place)
                weights = jnp.where(seen, jnp.exp(scores - log_total), 0.0)
                weight_grad = dot(grad, values, 1, 1)
                score_grad = (weights * (weight_grad - delta)).astype(bf16)
                kv_sum[s, pl.ds(first, CHUNK), :HD] += dot(score_grad, q, 0, 0)
                kv_sum[s, pl.ds(first, CHUNK), HD:] += dot(weights.astype(bf16), grad, 0, 0)
                return query_grad + dot(score_grad, keys, 1, 0)

            at = 4 * s + 2 * b
            query_grad = lax.fori_loop(
                range_ref[at], range_ref[at + 1], step, jnp.zeros((heads * half, HD), f32)
            )
            cos_b, sin_b = cos[s, mine, :] * SCALE, sin[s, mine, :] * SCALE
            for h in range(heads):
                z = query_grad[h * half : (h + 1) * half]
                z = z * cos_b - pltpu.roll(z, HD // 2, 1) * sin_b
                query_out[s, mine, h * HD : (h + 1) * HD] = z.astype(bf16)

    def give(chip, carry):
        for s in range(2):
            for b in range(2):
                block = chip if b == 0 else 2 * chips - 1 - chip
                place = pl.multiple_of(block * half, half)
                mine = slice(b * half, (b + 1) * half)
                source = kv_sum[s, pl.ds(place, half), :]
                kv_out[chip % 8, chip // 8, s, mine, :HD] = (source[:, :HD] * SCALE).astype(bf16)
                kv_out[chip % 8, chip // 8, s, mine, HD:] = source[:, HD:].astype(bf16)
        return carry

    lax.fori_loop(0, chips, give, 0)


def attend_back(
    ranges, branch_own, branch_other, weight, queries, kv, attended, logs, starts, places, cos, sin
):
    _, heads, rows, _ = queries.shape
    keys = kv.shape[1]
    chips = keys // rows
    return pl.pallas_call(
        functools.partial(attend_back_kernel, heads),
        out_shape=[
            jax.ShapeDtypeStruct((2, rows, heads * HD), bf16),
            jax.ShapeDtypeStruct((8, chips // 8, 2, rows, 2 * HD), bf16),
        ],
        in_specs=[SMEM] + [VMEM] * 11,
        out_specs=[VMEM] * 2,
        scratch_shapes=[
            pltpu.VMEM((2, rows, heads * HD), bf16),
            pltpu.VMEM((2, keys, 2 * HD), f32),
        ],
        compiler_params=BIG,
        name="attend_back",
    )(
        ranges,
        branch_own,
        branch_other,
        weight,
        queries,
        kv,
        attended,
        logs,
        starts,
        places,
        cos,
        sin,
    )


def on_device(
    tokens, cotangent, doc_lengths, norm_attn, w_qkv, b_qkv, w_out, norm_mlp, w_gate, w_up, w_down
):
    ctx_size = lax.axis_size("ctx")
    chip = lax.axis_index("ctx")
    core = lax.axis_index("wshard")
    where = jnp.stack([chip, core]).astype(jnp.int32)
    high = high_bits()
    groups = ctx_size // 8
    tok_dev, width = tokens.shape[1], tokens.shape[2]
    ff = w_gate.shape[1]
    ff_own = ff // 8
    heads = H // KVH
    hq = heads * HD
    rows_dev = w_qkv.shape[0]
    cuts = row_parts(tok_dev)
    half = tok_dev // 2
    flips = [relative_flips(high + order) for order in ORDERS]
    group_flips = relative_flips(group_bits())
    low, middle, upper = member_bits()

    n_gain, n_bias = norm_attn.shape[0], b_qkv.shape[0]
    small = jnp.concatenate([norm_attn, b_qkv, norm_mlp])[None]
    small = jnp.pad(small, ((0, 15), (hq, 2 * HD - small.shape[1])))
    qkv_send = jnp.concatenate([head_columns(w_qkv, 1 - core), small])
    qkv_own = jnp.concatenate([head_columns(w_qkv, core), small])
    token_own, out_grad_b = tokens[0], cotangent[0]
    out_t = w_out.T
    qkv_other = core_swap(qkv_send)
    token_other = core_swap(token_own)
    length_other = core_swap(doc_lengths[0])
    out_other = core_swap(half_of(out_t, 1 - core, 1))
    down_found = gather_list(w_down, group_bits())
    length_pair = jnp.stack([doc_lengths[0], length_other])
    qkv_pair = jnp.stack([qkv_own, qkv_other])[None]
    qkv_pair, w_gate, out_other = together(qkv_pair, w_gate, out_other)
    out_pair = by_core(half_of(out_t, core, 1), out_other, core)
    out_w = lax.all_gather(out_pair, "ctx", axis=0, tiled=False).reshape(width, hq)
    out_grad_all = lax.all_gather(
        after(out_grad_b, out_w), "ctx", axis=0, tiled=True, axis_index_groups=group_lists()
    )
    qkv_pair = gather_relative(qkv_pair, high)
    packed = pack_members(w_gate, w_up)
    qkv_pair, packed, down_found = together(qkv_pair, packed, down_found)
    column_cuts = ((0, hq // 2, rows_dev), (hq // 2, hq, rows_dev), (hq, hq + 2 * HD, rows_dev + 16))
    qkv_parts = [qkv_pair[:, :, :rows, start:stop] for start, stop, rows in column_cuts]
    qkv_parts = doubled(qkv_parts, [order[0] for order in ORDERS])
    down_other = [core_swap(x) for x in down_found]
    qkv_parts = doubled(qkv_parts, [order[1] for order in ORDERS])
    qkv_parts = with_arrived(qkv_parts, [order[2] for order in ORDERS])
    qkv_parts, packed = together(qkv_parts, packed)
    row_cut = rows_dev // 3
    first_rows, later_rows = packed[:, :row_cut], packed[:, row_cut:]
    first_rows = group_exchange(first_rows)

    inner = jnp.arange(tok_dev, dtype=jnp.int32)
    blocks = jnp.where(inner < half, chip, 2 * ctx_size - 1 - chip)
    places = (blocks * half + inner % half).astype(jnp.int32)
    ends = jnp.cumsum(length_pair, axis=1)
    passed = ends[:, None, :] <= places[None, :, None]
    starts = jnp.sum(jnp.where(passed, length_pair[:, None, :], 0), axis=2)
    places = jnp.broadcast_to(places[None], starts.shape)
    frequency = ROPE_BASE ** (-jnp.arange(HD // 2, dtype=f32) * 2.0 / HD)
    angles = (places - starts).astype(f32)[..., None] * frequency
    cos_half, sin_half = jnp.cos(angles), jnp.sin(angles)
    cos = jnp.concatenate([cos_half, cos_half], axis=-1)
    sin = jnp.concatenate([-sin_half, sin_half], axis=-1)
    first = jnp.min(starts.reshape(2, 2, half), axis=2) // CHUNK
    last = jnp.max(places.reshape(2, 2, half), axis=2) // CHUNK + 1
    ranges = jnp.stack([first, last], axis=-1).reshape(-1).astype(jnp.int32)
    starts, places = starts[..., None], places[..., None]

    if rows_dev % 16:
        qkv_w, small_all = order_weights(qkv_parts, flips, where)
        qkv_w = qkv_w.reshape(width, hq + 2 * HD)
        small_all = small_all.reshape(2 * ctx_size, 2 * HD)
        gain_one = small_all[:, :n_gain].reshape(1, -1)
        bias = small_all[:, n_gain : n_gain + n_bias].reshape(1, -1)
        gain_two = small_all[:, n_gain + n_bias : 2 * n_gain + n_bias].reshape(1, -1)
        bias = head_columns(bias, core)
        normed_one, queries, kv_own = project(token_own, token_other, gain_one, qkv_w, bias, cos, sin)
    else:
        normed_one, queries, kv_own, qkv_w, gains = order_project(
            where, token_own, token_other, cos, sin, qkv_parts, flips, n_gain, n_bias, rows_dev
        )
        gain_one, gain_two = gains[:1], gains[1:]
    kv_own = gather_relative(kv_own[None], high)
    kv_own, first_rows = together(kv_own, first_rows)

    kv_parts = [kv_own[:, :, start:stop] for start, stop in cuts]
    for step in range(2):
        kv_parts = doubled(kv_parts, [order[step] for order in ORDERS])
    down = order_rows([x[None] for x in down_found], [x[None] for x in down_other], group_flips, where)
    down = down.reshape(ff_own, width)
    kv_parts = with_arrived(kv_parts, [order[2] for order in ORDERS])
    kv_parts, down, later_rows, first_rows = together(kv_parts, down, later_rows, first_rows)
    later_rows = group_exchange(later_rows)
    kv, attended, attended_b, logs, branch = attend(
        where, ranges, queries, starts, places, out_w, kv_parts, flips, cuts
    )
    branch_other = core_swap(branch[1])
    branch_other, later_rows, first_rows = together(branch_other, later_rows, first_rows)
    packed = jnp.concatenate([first_rows, later_rows], axis=1)
    shares = ((0, 4), (4, 8))
    packed_found = [gather_list(packed[:4], group_bits())]
    packed_other = core_swap(packed)
    inputs = token_own.astype(f32)
    hidden_res = inputs + branch[0] + branch_other
    scale_two = lax.rsqrt(jnp.mean(hidden_res * hidden_res, axis=-1, keepdims=True) + EPSILON)
    normed_two = (hidden_res * scale_two * gain_two).astype(bf16)

    group_orders = ((upper, middle, low), (upper, low, middle))
    group_cuts = ((0, half), (half, tok_dev))
    token_parts = gather_relative(normed_two[None], (upper,))
    token_parts, packed, packed_found = together(token_parts, packed, packed_found)
    token_parts = [token_parts[:, start:stop] for start, stop in group_cuts]
    token_parts = doubled(token_parts, [order[1] for order in group_orders])
    packed_found.append(gather_list(packed[4:], group_bits()))
    token_parts, out_grad_all = together(token_parts, out_grad_all)
    token_parts = with_arrived(token_parts, [order[2] for order in group_orders])
    token_parts, packed_found = together(token_parts, packed_found)
    token_flips = [relative_flips(order) for order in group_orders]
    normed_all = order_tokens(token_parts, token_flips, group_cuts, groups, where)
    normed_all = normed_all.reshape(8 * tok_dev, width)

    sources, loads = [packed, packed_other], [(0, 0, 0), (0, 1, 0)]
    for found, (first, _) in zip(packed_found, shares):
        for piece, flip in list(zip(found, group_flips))[1:]:
            sources.extend([piece, core_swap(piece)])
            loads.extend([(flip, 0, first), (flip, 1, first)])
    if rows_dev % 16:
        own, other = [], []
        for flip in group_flips:
            for core_flip, side in enumerate((own, other)):
                found = [x for x, load in zip(sources, loads) if load[:2] == (flip, core_flip)]
                side.append(jnp.concatenate(found))
        sources, loads = [order_rows(own, other, group_flips, where).reshape(width, -1)], [(None, 0, 0)]
    out_grad = out_grad_b.astype(f32)
    pre_grad, activated, normed_grad_part = mlp(
        where, groups, normed_all, out_grad_all, down, sources, loads
    )

    normed_grad_part = normed_grad_part.reshape(2, 2, 2, tok_dev, width)
    scatter = Scatter(
        [normed_grad_part[:, :, :, start:stop] for start, stop in group_cuts], (upper, middle, low)
    )
    bits = [order[2] for order in group_orders]
    kept, sent = scatter.split(bits)
    gate_keep, gate_send = gate_up_grads(normed_all, after(pre_grad, *sent), 0, rows_dev, where)
    gate_arrived = core_swap(gate_send)
    branch_part = dot(after(activated, gate_send), down, 1, 0).astype(bf16)
    scatter.step(bits, kept, sent)
    scatter.parts, gate_arrived, branch_part = together(scatter.parts, gate_arrived, branch_part)

    def of_cores(keep, arrived):
        total = (keep.astype(f32) + arrived.astype(f32)).astype(bf16)
        return total.reshape(8, groups, rows_dev, -1)

    def of_group(total):
        return sum_over(total, 1, tuple(reversed(group_bits()))).astype(bf16)

    bits = [order[1] for order in group_orders]
    kept, sent = scatter.split(bits)
    gate_total = of_cores(gate_keep, gate_arrived)
    scatter.step(bits, kept, sent)
    scatter.parts, gate_total, pre_grad = together(scatter.parts, gate_total, pre_grad)

    kept, sent = scatter.split((upper, upper))
    grad_gate = of_group(gate_total)
    up_keep, up_send = gate_up_grads(normed_all, after(pre_grad, *sent), 1, rows_dev, where)
    branch_part = branch_part.reshape(2, 2, 2, tok_dev, width)
    branch_sums = Scatter(
        [branch_part[:, :, :, start:stop] for start, stop in group_cuts], (upper, middle, low)
    )
    bits = [order[2] for order in group_orders]
    branch_kept, branch_sent = branch_sums.split(bits)
    scatter.step((upper, upper), kept, sent)
    branch_arrived = [chip_swap(x, 1 << bit) for x, bit in zip(branch_sent, bits)]
    scatter.parts, grad_gate, up_send = together(scatter.parts, grad_gate, up_send)
    grad_gate = group_exchange(grad_gate)
    up_arrived = core_swap(up_send)
    normed_two_grad = jnp.concatenate(scatter.parts)
    gain_two_grad = jnp.sum(normed_two_grad * hidden_res * scale_two, axis=0)
    hidden_grad = out_grad + rms_back(normed_two_grad, hidden_res, scale_two, gain_two)

    falling = tuple(reversed(group_bits()))
    def weight_parts(x):
        return x.astype(bf16).reshape(ctx_size // 8, 8, 2, rows_dev, x.shape[1])

    branch_own = hidden_grad.astype(bf16)
    branch_other = core_swap(branch_own)
    branch_own, branch_other, up_arrived, branch_arrived = together(
        branch_own, branch_other, up_arrived, branch_arrived
    )
    grad_up = of_group(of_cores(up_keep, up_arrived))
    project_grad_q, kv_grad = attend_back(
        ranges, branch_own, branch_other, out_w, queries, kv, attended, logs, starts, places, cos, sin
    )
    (kv_grad, project_grad_q), grad_gate, grad_up, activated = together(
        (kv_grad, project_grad_q), grad_gate, grad_up, activated
    )
    kv_sum = cube_exchange(kv_grad)
    down_keep, down_send = down_grads(activated, out_grad_all, groups, where)
    branch_grad = jnp.concatenate([branch_own, branch_other])
    normed_one = normed_one.reshape(-1, width)
    project_grad_q = project_grad_q.reshape(-1, hq)
    grad_out_part = weight_parts(dot(branch_grad, attended_b.reshape(-1, hq), 0, 0))
    grad_q_part = weight_parts(dot(normed_one, project_grad_q, 0, 0))
    wide_part = jnp.concatenate([grad_q_part, grad_out_part], axis=-1)
    names = tuple(reversed(high)) + (2, 1, 0)
    wide_part = wide_part.reshape((2,) * len(names) + wide_part.shape[2:])
    third = 2 * hq // 3
    scatter = Scatter([wide_part[..., i * third : (i + 1) * third] for i in range(3)], names)
    bits = [order[0] for order in ORDERS]
    kept, sent = scatter.split(bits)
    arrived = [chip_swap(x, 1 << bit) for x, bit in zip(sent, bits)]
    kv_sum, arrived, down_send, branch_arrived = together(
        kv_sum, arrived, down_send, branch_arrived
    )

    kv_sum = jnp.sum(kv_sum.astype(f32), axis=0).astype(bf16)
    kv_sum, grad_up = together(kv_sum, grad_up)
    kv_sum = sum_over_high(kv_sum, high)
    down_arrived = core_swap(down_send)
    grad_up = group_exchange(grad_up)
    key_pre = kv_sum[..., :HD]
    key_pre = key_pre * cos - jnp.roll(key_pre, HD // 2, axis=-1) * sin
    project_grad_kv = jnp.concatenate([key_pre, kv_sum[..., HD:]], axis=-1).astype(bf16)
    project_grad_kv = project_grad_kv.reshape(-1, 2 * HD)
    grad_kv = weight_parts(dot(normed_one, project_grad_kv, 0, 0)).swapaxes(0, 1)
    project_grad = jnp.concatenate([project_grad_q, project_grad_kv], axis=1)
    normed_one_grad = dot(project_grad, qkv_w, 1, 1)
    normed_one_grad = normed_one_grad[:tok_dev] + core_swap(normed_one_grad[tok_dev:])
    scatter.add(kept, arrived)
    branch_sums.add(branch_kept, branch_arrived)
    branch_sums.step([order[1] for order in group_orders])
    down_sum = (down_keep.astype(f32) + down_arrived.astype(f32)).astype(bf16)
    grad_kv, grad_up, scatter.parts, branch_sums.parts, down_sum, normed_one_grad = together(
        grad_kv, grad_up, scatter.parts, branch_sums.parts, down_sum, normed_one_grad
    )
    grad_kv = cube_exchange(grad_kv)
    branch_sums.parts = [jnp.concatenate(branch_sums.parts, axis=-2)]
    branch_sums.step((upper,))
    scatter.step([order[1] for order in ORDERS])
    scatter.step([order[2] for order in ORDERS])
    scatter.parts = [jnp.concatenate(scatter.parts, axis=-1)]
    scale_one = lax.rsqrt(jnp.mean(inputs * inputs, axis=-1, keepdims=True) + EPSILON)
    gain_one_grad = jnp.sum(normed_one_grad * inputs * scale_one, axis=0)
    input_grad = hidden_grad + rms_back(normed_one_grad, inputs, scale_one, gain_one)

    def whole_columns(x):
        return jnp.concatenate(
            [
                x[0, :, :hq],
                x[1, :, :hq],
                x[0, :, hq : hq + HD],
                x[1, :, hq : hq + HD],
                x[0, :, hq + HD : hq + 2 * HD],
                x[1, :, hq + HD : hq + 2 * HD],
            ],
            axis=1,
        )

    bias_grad = jnp.sum(project_grad.astype(f32), axis=0, keepdims=True)
    zeros = jnp.zeros_like(bias_grad)
    bias_full = whole_columns(
        jnp.stack([jnp.where(core == 0, bias_grad, zeros), jnp.where(core == 0, zeros, bias_grad)])
    )[0]
    qk_width = (H + KVH) * HD
    sums = jnp.concatenate(
        [
            x.reshape(ctx_size, 1, -1)
            for x in (gain_one_grad, gain_two_grad, bias_full[:qk_width], bias_full[qk_width:])
        ],
        axis=2,
    )
    grad_kv, scatter.parts, branch_sums.parts, sums, down_sum = together(
        grad_kv, scatter.parts, branch_sums.parts, sums, down_sum
    )
    sums = lax.all_to_all(sums, "ctx", split_axis=0, concat_axis=0, tiled=True)
    grad_kv = jnp.sum(grad_kv.astype(f32), axis=0).astype(bf16)
    grad_kv = sum_over_high(grad_kv, high)
    grad_down = sum_over(down_sum, 0, falling)
    for bit in reversed(high):
        scatter.step((bit,))
    scattered = scatter.parts[0]
    sums = jnp.sum(sums, axis=0)
    sums = (sums + core_swap(sums))[0]
    output = (hidden_res + branch_sums.parts[0]).astype(bf16)

    grad_gate, grad_up = unpack_members(grad_gate, grad_up, ff)
    chip_grad = jnp.concatenate([scattered[..., :hq], grad_kv, scattered[..., hq:]], axis=-1)

    def pick(x, which):
        return lax.dynamic_index_in_dim(x, which, 0, keepdims=False)

    pair = by_core(pick(chip_grad, core), core_swap(pick(chip_grad, 1 - core)), core)
    grad_qkv = whole_columns(pair)
    grad_out = pair[:, :, hq + 2 * HD :].transpose(1, 0, 2).reshape(-1, 2 * hq).T

    def owned(start, size):
        return lax.dynamic_slice_in_dim(sums, start + core * (size // 2), size // 2, 0)

    own_width, own_qk, own_v = width // ctx_size, qk_width // ctx_size, KVH * HD // ctx_size
    return (
        output[None],
        input_grad[None],
        owned(0, own_width),
        grad_qkv,
        owned(2 * own_width, own_qk),
        owned(2 * own_width + own_qk, own_v),
        grad_out,
        owned(own_width, own_width),
        grad_gate,
        grad_up,
        grad_down,
    )


def solution(mesh):
    whole = ("ctx", "wshard")
    rows, columns, flat = P(whole, None), P(None, whole), P(whole)
    tokens = P("wshard", "ctx", None)
    return jax.shard_map(
        on_device,
        mesh=mesh,
        in_specs=(tokens, tokens, P("wshard", None), flat, rows, flat, columns, flat, rows, rows, rows),
        out_specs=(tokens, tokens, flat, rows, flat, flat, columns, flat, rows, rows, rows),
        check_vma=False,
    )
```
